128 devices in a mesh: branch: 16 (over z_lo, y, core), head: 8 (over z_hi, x).
Axes of the slice: x: 4, y: 4, z: 4 (z_hi: 2, z_lo: 2; z = z_hi * 2 + z_lo), core: 2. Of those that a mesh axis runs over, the one named last changes fastest.
Arguments:
- queries: bfloat16 [16, 64, 3, 8192], P('branch', None, None, 'head'), may hold values from -16 to 16
- new_keys: bfloat16 [16, 64, 3, 1024], P('branch', None, None, 'head'), may hold values from -8 to 8
- new_values: bfloat16 [16, 64, 3, 1024], P('branch', None, None, 'head'), may hold values from -6 to 6
- prompt_keys: bfloat16 [8192, 1024], P('branch', 'head'), may hold values from -16 to 16
- prompt_values: bfloat16 [8192, 1024], P('branch', 'head'), may hold values from -6 to 6
- span_keys: bfloat16 [16, 64, 64, 1024], P('branch', None, None, 'head'), may hold values from -8 to 8
- span_values: bfloat16 [16, 64, 64, 1024], P('branch', None, None, 'head'), may hold values from -6 to 6
- span_lengths: int32 [64, 16], replicated, may hold values from 1 to 64, as said below
- join_offsets: int32 [64, 16], replicated, may hold values from 8192 to 9152, as said below
- pattern: int32 [16, 4, 16], P('branch'), may hold values 0 or 1
- out_weight: bfloat16 [8192, 8192], P('head'), may hold values from -0.0625 to 0.0625
Outputs:
- mixed: bfloat16 [16, 64, 3, 8192], P('branch')
- joined_keys: bfloat16 [64, 1024, 1024], P('branch', None, 'head')
- joined_values: bfloat16 [64, 1024, 1024], P('branch', None, 'head')
The draws below stay inside these ranges and needn't reach their ends.
Inputs may be any that keep to these rules, and one draw needn't show every extreme that they name: `span_lengths`: each problem has at least one branch whose cache is full, 64 live slots; all branches of problem 0 are full. `join_offsets`: for each problem the branches are taken in some order and their live slots laid end to end after the 8192 prompt positions: a branch's offset is 8192 plus the live slots of the branches before it in that order.
All inputs are finite; a program needn't handle non-finite values. No bound on the sum of `pattern` on one device may be relied on, other than what follows from the above.
Results may differ from the reference program's by a relative error of at most 0.02.
Values may be sent and summed in bfloat16 or wider, within the bound.
No kernel may reach another device: no remote copies, remote signals or barrier semaphores. Data moves between devices by JAX's collectives and lax.ppermute only.
A program may use at most 128 MiB of HBM per device.

```python
import math
import jax
import jax.numpy as jnp
from jax import lax

D = 8192
HEADS = 64
KVH = 8
HD = 128
PROBS = 64
STEPS = 3
SPAN = 64
P_DEV = 512
QPROBS = 16
BRANCHES = 16
PROMPT = 8192
QBLOCKS = 4


def join_pair(key):
    length_key, order_key = jax.random.split(jax.random.fold_in(key, 41))
    lengths = jax.random.randint(length_key, (PROBS, BRANCHES), 1, SPAN + 1, dtype=jnp.int32)
    full_branch = jnp.arange(PROBS, dtype=jnp.int32)[:, None] % BRANCHES == jnp.arange(BRANCHES, dtype=jnp.int32)[None, :]
    full_problem = (jnp.arange(PROBS, dtype=jnp.int32) == 0)[:, None]
    lengths = jnp.where(full_branch | full_problem, SPAN, lengths).astype(jnp.int32)
    order_keys = jax.random.split(order_key, PROBS)
    orders = jax.vmap(lambda single: jax.random.permutation(single, BRANCHES))(order_keys).astype(jnp.int32)
    ordered = jnp.take_along_axis(lengths, orders, axis=1)
    before = jnp.cumsum(ordered, axis=1) - ordered
    inverse = jnp.argsort(orders, axis=1).astype(jnp.int32)
    offsets = jnp.take_along_axis(before, inverse, axis=1) + PROMPT
    return (lengths, offsets.astype(jnp.int32))


def draw_span_lengths(key, part):
    shared = join_pair(key)
    return shared[0]


def draw_join_offsets(key, part):
    shared = join_pair(key)
    return shared[1]


def draw_queries(key, part):
    key = jax.random.fold_in(key, 5)
    base = jnp.clip(2.5 * jax.random.normal(key, (BRANCHES, PROBS, STEPS, HEADS, HD), jnp.float32), -10.0, 10.0)
    return base.reshape(BRANCHES, PROBS, STEPS, HEADS * HD).astype(jnp.bfloat16)


def draw_prompt_keys(key, part):
    key = jax.random.fold_in(key, 7)
    base = jnp.clip(jax.random.normal(key, (PROMPT, KVH, HD), jnp.float32), -6.0, 6.0)
    return base.reshape(PROMPT, KVH * HD).astype(jnp.bfloat16)


def with_ends(array, own_key, low, top_value):
    longest = array.shape.index(max(array.shape))
    spots = []
    for shift in (0, 1):
        where = [jax.random.randint(jax.random.fold_in(own_key, axis), (), 0, length) for axis, length in enumerate(array.shape)]
        where[longest] = (where[longest] + shift) % array.shape[longest]
        spots.append(tuple(where))
    return array.at[spots[0]].set(low).at[spots[1]].set(top_value)


def block_levels(own_key, extent, shards, least, high):
    gain = 1.0
    for dim, blocks in shards:
        steps = jax.random.uniform(jax.random.fold_in(jax.random.fold_in(own_key, 6), dim), (blocks,), jnp.float32, least / len(shards), high / len(shards))
        gain = gain * jnp.repeat(jnp.exp(steps), extent[dim] // blocks).reshape((-1,) + (1,) * (len(extent) - 1 - dim))
    return gain


def scatter_about(rng, extent, width, bound, cuts=(), kind=jnp.bfloat16):
    drawn = jax.random.normal(rng, extent, jnp.float32) * width
    if len(cuts) > 0:
        drawn = block_levels(rng, extent, cuts, -0.22, 0.18) * drawn
    return jnp.clip(drawn, min=-bound, max=bound).astype(kind)


def setup_inputs(seed: int = 0) -> dict:
    splits = jax.random.split(jax.random.key(seed), 12)
    queries = draw_queries(jax.random.fold_in(splits[11], 71), 0)
    new_keys = scatter_about(splits[1], (BRANCHES, PROBS, STEPS, KVH * HD), 2.0, 8.0, ((0, 16), (3, 8)))
    new_values = scatter_about(splits[2], (BRANCHES, PROBS, STEPS, KVH * HD), 1.0, 6.0, ((0, 16), (3, 8)))
    prompt_keys = draw_prompt_keys(jax.random.fold_in(splits[11], 71), 0)
    prompt_values = scatter_about(splits[4], (PROMPT, KVH * HD), 1.0, 6.0, ((0, 16), (1, 8)))
    span_keys = scatter_about(splits[5], (BRANCHES, PROBS, SPAN, KVH * HD), 1.5, 8.0, ((0, 16), (3, 8)))
    span_values = scatter_about(splits[6], (BRANCHES, PROBS, SPAN, KVH * HD), 1.0, 6.0, ((0, 16), (3, 8)))
    span_lengths = draw_span_lengths(jax.random.fold_in(splits[11], 71), 0)
    join_offsets = draw_join_offsets(jax.random.fold_in(splits[11], 71), 0)
    pattern = with_ends((jax.random.randint(splits[9], (BRANCHES, QBLOCKS, BRANCHES), 0, 2) < 1).astype(jnp.int32), jax.random.fold_in(splits[9], 1), 0, 1)
    out_weight = scatter_about(splits[10], (HEADS * HD, D), (HEADS * HD) ** -0.5, 0.0625, ((0, 8),))
    return {"queries": queries, "new_keys": new_keys, "new_values": new_values, "prompt_keys": prompt_keys, "prompt_values": prompt_values, "span_keys": span_keys, "span_values": span_values, "span_lengths": span_lengths, "join_offsets": join_offsets, "pattern": pattern, "out_weight": out_weight}


rope_base = 500000.0
masked_score = -1e+30

def rotate(values, position):
    half = values.shape[-1] // 2
    exponent = jnp.arange(half, dtype=jnp.float32) * (2.0 / values.shape[-1])
    frequency = jnp.exp(-math.log(rope_base) * exponent)
    angle = position.astype(jnp.float32)[..., None] * frequency
    cosine = jnp.cos(angle)
    sine = jnp.sin(angle)
    first = values[..., :half]
    second = values[..., half:]
    return jnp.concatenate([first * cosine - second * sine, second * cosine + first * sine], -1)

def pack_slots(source, lengths, starts):
    branch_count = source.shape[0]
    problems = source.shape[1]
    slots = source.shape[2]
    flat = jnp.transpose(source, (1, 0, 2, 3)).reshape(problems, branch_count * slots, source.shape[3])
    target = jnp.arange(branch_count * slots, dtype=jnp.int32)
    begin = starts[:, :, None]
    inside = (target[None, None, :] >= begin) & (target[None, None, :] < begin + lengths[:, :, None])
    anchor = jnp.arange(branch_count, dtype=jnp.int32)[None, :, None] * slots + target[None, None, :] - begin
    index = lax.optimization_barrier(jnp.sum(jnp.where(inside, anchor, 0), axis=1)).astype(jnp.int32)
    valid = jnp.any(inside, axis=1)
    picked = jnp.take_along_axis(flat, index[:, :, None], axis=1)
    return jnp.where(valid[:, :, None], picked, jnp.zeros_like(picked))

def widen(rounded):
    return lax.optimization_barrier(rounded).astype(jnp.float32)

def reference(queries, new_keys, new_values, prompt_keys, prompt_values, span_keys, span_values, span_lengths, join_offsets, pattern, out_weight):
    group = HEADS // KVH
    scale = 1.0 / math.sqrt(HD)
    step_index = jnp.arange(STEPS, dtype=jnp.int32)
    key_block = jnp.arange(PROMPT, dtype=jnp.int32) // P_DEV
    slot_index = jnp.arange(SPAN, dtype=jnp.int32)
    fresh_allowed = step_index[None, :] <= step_index[:, None]

    def one_branch(branch):
        lengths = span_lengths[:, branch]
        position = PROMPT + lengths[:, None] + step_index[None, :]
        query_rot = rotate(queries[branch].astype(jnp.float32).reshape(PROBS, STEPS, KVH, group, HD), position[:, :, None, None]).astype(jnp.bfloat16)
        key_rot = rotate(new_keys[branch].astype(jnp.float32).reshape(PROBS, STEPS, KVH, HD), position[:, :, None]).astype(jnp.bfloat16)
        fresh_vals = new_values[branch].reshape(PROBS, STEPS, KVH, HD)
        cached_keys = span_keys[branch].reshape(PROBS, SPAN, KVH, HD)
        cached_vals = span_values[branch].reshape(PROBS, SPAN, KVH, HD)
        allowed_blocks = pattern[branch]
        block_ok = jnp.take(allowed_blocks, key_block, axis=1) > 0
        prompt_ok = jnp.repeat(block_ok, QPROBS, axis=0)[:, None, None, :]
        span_ok = (slot_index[None, :] < lengths[:, None])[:, None, None, :]
        fresh_ok = fresh_allowed[None, :, None, :]

        def one_group(head_group):
            query_group = query_rot[:, :, head_group]
            group_keys = lax.dynamic_slice_in_dim(prompt_keys, head_group * HD, HD, 1)
            group_vals = lax.dynamic_slice_in_dim(prompt_values, head_group * HD, HD, 1)
            prompt_scores = jnp.dot(query_group.reshape(-1, HD), group_keys.T, preferred_element_type=jnp.float32).reshape(PROBS, STEPS, group, PROMPT) * scale
            span_scores = jnp.einsum('psgd,pkd->psgk', query_group.astype(jnp.float32), cached_keys[:, :, head_group].astype(jnp.float32)) * scale
            fresh_scores = jnp.einsum('psgd,ptd->psgt', query_group.astype(jnp.float32), key_rot[:, :, head_group].astype(jnp.float32)) * scale
            prompt_scores = jnp.where(prompt_ok, prompt_scores, masked_score)
            span_scores = jnp.where(span_ok, span_scores, masked_score)
            fresh_scores = jnp.where(fresh_ok, fresh_scores, masked_score)
            top = jnp.maximum(jnp.maximum(prompt_scores.max(-1), span_scores.max(-1)), fresh_scores.max(-1))[..., None]
            prompt_weights = jnp.where(prompt_ok, jnp.exp(prompt_scores - top), 0.0)
            span_weights = jnp.where(span_ok, jnp.exp(span_scores - top), 0.0)
            fresh_weights = jnp.where(fresh_ok, jnp.exp(fresh_scores - top), 0.0)
            total = prompt_weights.sum(-1) + span_weights.sum(-1) + fresh_weights.sum(-1)
            numer = jnp.dot(prompt_weights.astype(jnp.bfloat16).reshape(-1, PROMPT), group_vals, preferred_element_type=jnp.float32).reshape(PROBS, STEPS, group, HD)
            numer = numer + jnp.einsum('psgk,pkd->psgd', widen(span_weights.astype(jnp.bfloat16)), cached_vals[:, :, head_group].astype(jnp.float32))
            numer = numer + jnp.einsum('psgt,ptd->psgd', widen(fresh_weights.astype(jnp.bfloat16)), fresh_vals[:, :, head_group].astype(jnp.float32))
            attended = (numer / total[..., None]).astype(jnp.bfloat16)
            weight_rows = lax.dynamic_slice_in_dim(out_weight, head_group * group * HD, group * HD, 0)
            return jnp.dot(attended.reshape(PROBS * STEPS, group * HD), weight_rows, preferred_element_type=jnp.float32).astype(jnp.bfloat16)
        partials = lax.map(one_group, jnp.arange(KVH, dtype=jnp.int32))
        summed = lax.optimization_barrier(jnp.sum(partials.astype(jnp.float32), axis=0)).astype(jnp.bfloat16)
        return summed.reshape(PROBS, STEPS, D)
    mixed = lax.map(one_branch, jnp.arange(BRANCHES, dtype=jnp.int32))
    shift_by = (join_offsets.T - PROMPT).astype(jnp.int32)
    rekeyed = rotate(span_keys.astype(jnp.float32).reshape(BRANCHES, PROBS, SPAN, KVH, HD), shift_by[:, :, None, None]).astype(jnp.bfloat16).reshape(BRANCHES, PROBS, SPAN, KVH * HD)
    starts = (join_offsets - PROMPT).astype(jnp.int32)
    joined_keys = pack_slots(rekeyed, span_lengths, starts)
    joined_values = pack_slots(span_values, span_lengths, starts)
    return (mixed, joined_keys, joined_values)
```

```python
import functools
import math

import jax
import jax.numpy as jnp
from jax import lax
from jax.experimental import pallas as pl
from jax.experimental.pallas import tpu as pltpu
from jax.sharding import PartitionSpec as P

HEADS = 64
KVH = 8
HD = 128
GROUP = HEADS // KVH
STEPS = 3
SPAN = 64
BRANCHES = 16
QBLOCKS = 4
PROBS = 64
QP = PROBS // QBLOCKS
PIECES = STEPS * GROUP
TILE = PIECES * QP
P_DEV = 512
CHUNK = 512

rope_base = 500000.0
masked_score = -1e30
SCALE2 = math.log2(math.e) / math.sqrt(HD)
VMEM = 40 * 1024 * 1024


def params(grid_rank=1):
    return pltpu.CompilerParams(
        dimension_semantics=("arbitrary",) * grid_rank, vmem_limit_bytes=VMEM
    )


def tables(position):
    half = HD // 2
    exponent = jnp.arange(half, dtype=jnp.float32) * (2.0 / HD)
    frequency = jnp.exp(-math.log(rope_base) * exponent)
    angle = position.astype(jnp.float32)[..., None] * frequency
    cosine = jnp.cos(angle)
    sine = jnp.sin(angle)
    return jnp.concatenate([cosine, cosine], -1), jnp.concatenate([-sine, sine], -1)


def turn(values, cosine, sine):
    return values * cosine + pltpu.roll(values, HD // 2, values.ndim - 1) * sine


def with_ones(values):
    return jnp.concatenate([values, jnp.ones_like(values)], 1)


def dot_nt(a, b):
    return lax.dot_general(a, b, (((1,), (1,)), ((), ())), preferred_element_type=jnp.float32)


def span_kernel(
    q_ref, qcos_ref, qsin_ref, nk_ref, nv_ref, sk_ref, sv_ref, code_ref, kcos_ref, ksin_ref,
    q_out, m_out, acc_out, sent_out,
):
    pieces = []
    for g in range(GROUP):
        for s in range(STEPS):
            lanes = slice(g * HD, (g + 1) * HD)
            raw = q_ref[s, :, lanes].astype(jnp.float32)
            rotated = turn(raw, qcos_ref[s], qsin_ref[s]).astype(jnp.bfloat16)
            q_out[s, :, lanes] = rotated
            pieces.append(rotated)
    query = jnp.concatenate(pieces, 0)
    fresh = [
        turn(nk_ref[s].astype(jnp.float32), qcos_ref[s], qsin_ref[s]).astype(jnp.bfloat16)
        for s in range(STEPS)
    ]
    pad = jnp.zeros((HD - STEPS * QP, HD), jnp.bfloat16)
    fresh_keys = jnp.concatenate(fresh + [pad], 0)
    fresh_vals = jnp.concatenate([nv_ref[s] for s in range(STEPS)] + [pad], 0)
    span_keys = sk_ref[...].reshape(QP * SPAN, HD)
    span_vals = sv_ref[...].reshape(QP * SPAN, HD)
    span_aug = with_ones(span_vals)
    fresh_aug = with_ones(fresh_vals)
    code = code_ref[0]
    rows = 128
    for r0 in range(0, TILE, rows):
        q = query[r0 : r0 + rows]
        row = lax.broadcasted_iota(jnp.int32, (rows, 1), 0) + r0
        prob = row & (QP - 1)
        piece = row >> 4
        step = piece - 3 * ((piece * 22) >> 6)
        s1 = jnp.where(code == prob, dot_nt(q, span_keys), masked_score)
        lane = lax.broadcasted_iota(jnp.int32, (1, HD), 1)
        ok = ((lane & (QP - 1)) == prob) & ((lane >> 4) <= step)
        s2 = jnp.where(ok, dot_nt(q, fresh_keys), masked_score)
        top = jnp.maximum(s1.max(1, keepdims=True), s2.max(1, keepdims=True)) * SCALE2
        p1 = jnp.exp2(s1 * SCALE2 - top).astype(jnp.bfloat16)
        p2 = jnp.exp2(s2 * SCALE2 - top).astype(jnp.bfloat16)
        m_out[0, r0 : r0 + rows, :] = jnp.broadcast_to(top, (rows, HD))
        acc_out[0, r0 : r0 + rows, :] = jnp.dot(
            p1, span_aug, preferred_element_type=jnp.float32
        ) + jnp.dot(p2, fresh_aug, preferred_element_type=jnp.float32)
    keys = sk_ref[...].astype(jnp.float32)
    kcos = kcos_ref[...][:, None, :]
    ksin = ksin_ref[...][:, None, :]
    sent_out[:, :, :HD] = turn(keys, kcos, ksin).astype(jnp.bfloat16)
    sent_out[:, :, HD:] = sv_ref[...]


def span_part(queries, qcos, qsin, new_keys, new_values, span_keys, span_values, code, kcos, ksin):
    three = lambda width: pl.BlockSpec((STEPS, QP, width), lambda i: (0, i, 0))
    span = lambda width: pl.BlockSpec((QP, SPAN, width), lambda i: (i, 0, 0))
    state = lambda width: pl.BlockSpec((1, TILE, width), lambda i: (i, 0, 0))
    wide = GROUP * HD
    return pl.pallas_call(
        span_kernel,
        grid=(QBLOCKS,),
        in_specs=[
            three(wide), three(HD), three(HD), three(HD), three(HD), span(HD), span(HD),
            pl.BlockSpec((1, 1, QP * SPAN), lambda i: (i, 0, 0)),
            pl.BlockSpec((QP, HD), lambda i: (i, 0)),
            pl.BlockSpec((QP, HD), lambda i: (i, 0)),
        ],
        out_specs=[three(wide), state(HD), state(2 * HD), span(2 * HD)],
        out_shape=[
            jax.ShapeDtypeStruct((STEPS, PROBS, wide), jnp.bfloat16),
            jax.ShapeDtypeStruct((QBLOCKS, TILE, HD), jnp.float32),
            jax.ShapeDtypeStruct((QBLOCKS, TILE, 2 * HD), jnp.float32),
            jax.ShapeDtypeStruct((PROBS, SPAN, 2 * HD), jnp.bfloat16),
        ],
        compiler_params=params(),
        cost_estimate=pl.CostEstimate(
            flops=4 * QBLOCKS * TILE * 1152 * 256, bytes_accessed=10 << 20, transcendentals=0
        ),
    )(queries, qcos, qsin, new_keys, new_values, span_keys, span_values, code, kcos, ksin)


def prompt_kernel(final, parts, pat_ref, q_ref, m_in, acc_in, *refs):
    kv_refs = refs[:parts]
    if final:
        att_out, qs, m_ref, acc_ref = refs[parts:]
    else:
        m_out, acc_out, qs = refs[parts:]
        m_ref, acc_ref = m_out.at[0], acc_out.at[0]
    i = pl.program_id(0)
    for g in range(GROUP):
        for s in range(STEPS):
            at = (g * STEPS + s) * QP
            qs[at : at + QP, :] = q_ref[s, :, g * HD : (g + 1) * HD]
    m_ref[...] = m_in[0]
    acc_ref[...] = acc_in[0]
    rows = 128
    for part in range(parts):
        kv_ref = kv_refs[part]
        count = kv_ref.shape[0]

        def body(j, carry, kv_ref=kv_ref, base=part * count):
            @pl.when(pat_ref[i, base + j] > 0)
            def _():
                keys = kv_ref[j, :P_DEV, :]
                vals = with_ones(kv_ref[j, P_DEV:, :])
                for r0 in range(0, TILE, rows):
                    at = slice(r0, r0 + rows)
                    scores = dot_nt(qs[at, :], keys)
                    old = m_ref[at, :]
                    top = jnp.maximum(old, scores.max(1, keepdims=True) * SCALE2)
                    factor = jnp.exp2(old - top)
                    weights = jnp.concatenate(
                        [
                            jnp.exp2(scores[:, c : c + HD] * SCALE2 - top).astype(jnp.bfloat16)
                            for c in range(0, P_DEV, HD)
                        ],
                        1,
                    )
                    m_ref[at, :] = top
                    acc_ref[at, :] = acc_ref[at, :] * jnp.concatenate(
                        [factor, factor], 1
                    ) + jnp.dot(weights, vals, preferred_element_type=jnp.float32)

            return carry

        lax.fori_loop(0, count, body, 0)
    if final:
        done = (acc_ref[:, :HD] / acc_ref[:, HD:]).astype(jnp.bfloat16)
        for g in range(GROUP):
            for s in range(STEPS):
                at = (g * STEPS + s) * QP
                att_out[s, :, g * HD : (g + 1) * HD] = done[at : at + QP]


def prompt_part(pattern, query, top, accum, stacks, final):
    wide = GROUP * HD
    parts = len(stacks)
    count = stacks[0].shape[0]
    three = pl.BlockSpec((STEPS, QP, wide), lambda i, pat: (0, i, 0))
    state = lambda width: pl.BlockSpec((1, TILE, width), lambda i, pat: (i, 0, 0))
    whole = pl.BlockSpec((count, 2 * P_DEV, HD), lambda i, pat: (0, 0, 0))
    if final:
        out_specs = three
        out_shape = jax.ShapeDtypeStruct((STEPS, PROBS, wide), jnp.bfloat16)
        scratch = [
            pltpu.VMEM((TILE, HD), jnp.bfloat16),
            pltpu.VMEM((TILE, HD), jnp.float32),
            pltpu.VMEM((TILE, 2 * HD), jnp.float32),
        ]
    else:
        out_specs = [state(HD), state(2 * HD)]
        out_shape = [
            jax.ShapeDtypeStruct((QBLOCKS, TILE, HD), jnp.float32),
            jax.ShapeDtypeStruct((QBLOCKS, TILE, 2 * HD), jnp.float32),
        ]
        scratch = [pltpu.VMEM((TILE, HD), jnp.bfloat16)]
    return pl.pallas_call(
        functools.partial(prompt_kernel, final, parts),
        grid_spec=pltpu.PrefetchScalarGridSpec(
            num_scalar_prefetch=1,
            grid=(QBLOCKS,),
            in_specs=[three, state(HD), state(2 * HD)] + [whole] * parts,
            out_specs=out_specs,
            scratch_shapes=scratch,
        ),
        out_shape=out_shape,
        compiler_params=params(),
        cost_estimate=pl.CostEstimate(
            flops=QBLOCKS * TILE * P_DEV * HD * 6 * parts * count,
            bytes_accessed=(5 << 20) + parts * count * (1 << 18),
            transcendentals=0,
        ),
    )(pattern, query, top, accum, *stacks)


def project_kernel(cols, a_ref, w_ref, o_ref):
    o_ref[0] = jnp.dot(
        a_ref[...], w_ref[...], preferred_element_type=jnp.float32
    ).astype(jnp.bfloat16)


def project(attended, weight, columns):
    rows, depth = attended.shape
    count = columns.shape[0]
    return pl.pallas_call(
        project_kernel,
        grid_spec=pltpu.PrefetchScalarGridSpec(
            num_scalar_prefetch=1,
            grid=(count,),
            in_specs=[
                pl.BlockSpec((rows, depth), lambda i, cols: (0, 0)),
                pl.BlockSpec((depth, CHUNK), lambda i, cols: (0, cols[i])),
            ],
            out_specs=pl.BlockSpec((1, rows, CHUNK), lambda i, cols: (i, 0, 0)),
        ),
        out_shape=jax.ShapeDtypeStruct((count, rows, CHUNK), jnp.bfloat16),
        compiler_params=params(),
        cost_estimate=pl.CostEstimate(
            flops=2 * count * rows * depth * CHUNK,
            bytes_accessed=2 * count * CHUNK * (depth + rows) + 2 * rows * depth,
            transcendentals=0,
        ),
    )(columns, attended, weight)


def join_kernel(parts, tgt_ref, *refs):
    sources = refs[:parts]
    keys_out, vals_out = refs[parts:]
    flat = jnp.concatenate([ref[r, 0] for ref in sources for r in range(2)], 0)
    total = flat.shape[0]
    target = tgt_ref[0]
    rows = 256
    for r0 in range(0, total, rows):
        slot = lax.broadcasted_iota(jnp.int32, (rows, 1), 0) + r0
        pick = jnp.where(target == slot, 1.0, 0.0).astype(jnp.bfloat16)
        got = jnp.dot(pick, flat, preferred_element_type=jnp.float32).astype(jnp.bfloat16)
        keys_out[0, r0 : r0 + rows, :] = got[:, :HD]
        vals_out[0, r0 : r0 + rows, :] = got[:, HD:]


def join(target, sources):
    share = target.shape[0]
    total = target.shape[2]
    out = pl.BlockSpec((1, total, HD), lambda i: (i, 0, 0))
    shape = jax.ShapeDtypeStruct((share, total, HD), jnp.bfloat16)
    return pl.pallas_call(
        functools.partial(join_kernel, len(sources)),
        grid=(share,),
        in_specs=[pl.BlockSpec((1, 1, total), lambda i: (i, 0, 0))]
        + [pl.BlockSpec((2, 1, SPAN, 2 * HD), lambda i: (0, i, 0, 0))] * len(sources),
        out_specs=[out, out],
        out_shape=[shape, shape],
        compiler_params=params(),
        cost_estimate=pl.CostEstimate(
            flops=2 * share * total * total * 2 * HD, bytes_accessed=4 << 20, transcendentals=0
        ),
    )(target, *sources)


NEAR = [(0, 1), (0, 3), (1, 0)]
FAR = [(0, 2), (1, 1), (1, 3), (1, 2)]


def chip_of(branch, dz, dy):
    return ((branch // 8) ^ dz) * 8 + ((branch // 2 + dy) % 4) * 2


def move_chip(value, dz, dy):
    perm = [(b, chip_of(b, dz, dy) + b % 2) for b in range(BRANCHES)]
    return lax.ppermute(value, "branch", perm)


def swap_core(value):
    return lax.ppermute(value, "branch", [(b, b ^ 1) for b in range(BRANCHES)])


def move_p(value):
    return lax.ppermute(value, "head", [(h, h ^ 1) for h in range(KVH)])


def move_q(value):
    return lax.ppermute(value, "head", [(h, (h // 4) * 4 + 3 - h % 4) for h in range(KVH)])


def move_z(value):
    return lax.ppermute(value, "head", [(h, h ^ 4) for h in range(KVH)])


def plus(a, b):
    return (a.astype(jnp.float32) + b.astype(jnp.float32)).astype(jnp.bfloat16)


def reduce_x(part):
    half = part.shape[-2] // 2
    a, b = part[..., :half, :], part[..., half:, :]
    got_a = move_p(a[..., 0:2, :, :])
    got_b = move_q(jnp.concatenate([b[..., 0:1, :, :], b[..., 2:3, :, :]], -3))
    a = plus(a[..., 2:4, :, :], got_a)
    b = plus(jnp.concatenate([b[..., 1:2, :, :], b[..., 3:4, :, :]], -3), got_b)
    got_a = move_q(a[..., 0, :, :])
    got_b = move_p(b[..., 0, :, :])
    return jnp.concatenate([plus(a[..., 1, :, :], got_a), plus(b[..., 1, :, :], got_b)], -2)


def gather_x(own):
    half = own.shape[-2] // 2
    from_p = move_p(own)
    from_q = move_q(own)
    o_a = move_p(from_q[..., :half, :])
    o_b = move_q(from_p[..., half:, :])
    return [jnp.concatenate([o_a, o_b], -2), from_p, from_q, own]


def shards(
    queries, new_keys, new_values, prompt_keys, prompt_values, span_keys, span_values,
    span_lengths, join_offsets, pattern, out_weight,
):
    me = lax.axis_index("branch")
    core = me % 2
    head = lax.axis_index("head")
    zh, x = head // 4, head % 4
    prompt_len = P_DEV * BRANCHES

    own = jnp.concatenate([prompt_keys, prompt_values], 0)
    near = [own] + [move_chip(own, dz, dy) for dz, dy in NEAR]
    far = [move_chip(own, dz, dy) for dz, dy in FAR]
    near_stack = jnp.stack(near)
    far_stack = jnp.stack(far)
    near_other = swap_core(near_stack)
    far_other = swap_core(far_stack)
    near_owner = jnp.stack([chip_of(me, dz, -dy) for dz, dy in [(0, 0)] + NEAR])
    far_owner = jnp.stack([chip_of(me, dz, -dy) for dz, dy in FAR])

    def allowed(owner):
        return jnp.take(pattern[0], owner, axis=1)

    lengths = lax.dynamic_slice_in_dim(span_lengths, me, 1, 1)[:, 0]
    starts = join_offsets - prompt_len
    shift = lax.dynamic_slice_in_dim(starts, me, 1, 1)[:, 0]
    position = prompt_len + lengths[None, :] + jnp.arange(STEPS, dtype=jnp.int32)[:, None]
    qcos, qsin = tables(position)
    kcos, ksin = tables(shift)
    slot = jnp.arange(SPAN, dtype=jnp.int32)
    problem = jnp.arange(PROBS, dtype=jnp.int32) % QP
    code = jnp.where(slot[None, :] < lengths[:, None], problem[:, None], -1)
    query, top, accum, sent = span_part(
        jnp.transpose(queries[0], (1, 0, 2)),
        qcos,
        qsin,
        jnp.transpose(new_keys[0], (1, 0, 2)),
        jnp.transpose(new_values[0], (1, 0, 2)),
        span_keys[0],
        span_values[0],
        code.reshape(QBLOCKS, 1, QP * SPAN),
        kcos,
        ksin,
    )

    top, accum = prompt_part(allowed(near_owner + core), query, top, accum, [near_stack], False)
    top, accum = prompt_part(
        allowed(near_owner + 1 - core), query, top, accum, [near_other], False
    )
    top, accum = prompt_part(allowed(far_owner + core), query, top, accum, [far_stack], False)
    attended = prompt_part(
        allowed(far_owner + 1 - core), query, top, accum, [far_other], True
    ).reshape(STEPS * PROBS, GROUP * HD)

    roles = jnp.stack([x ^ 2, x ^ 1, 3 - x, x])
    half = 8
    zfirst_send = project(attended, out_weight, half + (1 - zh) * 4 + roles)
    got_z = move_z(zfirst_send)
    xfirst = project(
        attended, out_weight, jnp.concatenate([(1 - zh) * 4 + roles, zh * 4 + roles])
    ).reshape(2, 4, STEPS * PROBS, CHUNK)
    zfirst_keep = project(attended, out_weight, half + zh * 4 + roles)
    both = reduce_x(xfirst)
    zsum = reduce_x(plus(zfirst_keep, got_z))
    xsum = plus(both[1], move_z(both[0]))

    pair = jnp.stack([move_z(xsum), xsum])
    xparts = gather_x(pair)
    zparts = jnp.stack(gather_x(zsum))
    zother = move_z(zparts)
    kx = [x ^ 2, x ^ 1, 3 - x, x]
    mixed = jnp.zeros((STEPS * PROBS, 16 * CHUNK), jnp.bfloat16)
    for r in range(4):
        for k, kz in ((0, 1 - zh), (1, zh)):
            mixed = lax.dynamic_update_slice(mixed, xparts[r][k], (0, (kz * 4 + kx[r]) * CHUNK))
    for r in range(4):
        mixed = lax.dynamic_update_slice(mixed, zparts[r], (0, (half + zh * 4 + kx[r]) * CHUNK))
    for r in range(4):
        mixed = lax.dynamic_update_slice(
            mixed, zother[r], (0, (half + (1 - zh) * 4 + kx[r]) * CHUNK)
        )
    mixed = jnp.transpose(mixed.reshape(STEPS, PROBS, 16 * CHUNK), (1, 0, 2))[None]

    share = PROBS // BRANCHES
    sent = sent.reshape(8, 2, share, SPAN, 2 * HD)
    keep = lax.dynamic_index_in_dim(sent, core, 1, keepdims=False)
    other = swap_core(lax.dynamic_index_in_dim(sent, 1 - core, 1, keepdims=False))
    merged = jnp.stack([keep, other], 1)
    hops = [(0, 0)] + NEAR + FAR
    got = []
    for dz, dy in hops:
        piece = lax.dynamic_index_in_dim(merged, chip_of(me, dz, dy) // 2, 0, keepdims=False)
        got.append(move_chip(piece, dz, dy) if (dz, dy) != (0, 0) else piece)
    owners = jnp.stack(
        [chip_of(me, dz, -dy) + c for dz, dy in hops for c in (core, 1 - core)]
    )
    mine_starts = jnp.take(lax.dynamic_slice_in_dim(starts, me * share, share, 0), owners, axis=1)
    mine_lengths = jnp.take(
        lax.dynamic_slice_in_dim(span_lengths, me * share, share, 0), owners, axis=1
    )
    target = jnp.where(
        slot < mine_lengths[:, :, None], mine_starts[:, :, None] + slot, -1
    ).reshape(share, 1, BRANCHES * SPAN)
    joined_keys, joined_values = join(target, got)
    return mixed, joined_keys, joined_values


def solution(mesh):
    return jax.shard_map(
        shards,
        mesh=mesh,
        in_specs=(
            P("branch", None, None, "head"),
            P("branch", None, None, "head"),
            P("branch", None, None, "head"),
            P("branch", "head"),
            P("branch", "head"),
            P("branch", None, None, "head"),
            P("branch", None, None, "head"),
            P(),
            P(),
            P("branch", None, None),
            P("head", None),
        ),
        out_specs=(
            P("branch", None, None, None),
            P("branch", None, "head"),
            P("branch", None, "head"),
        ),
        check_vma=False,
    )
```

```python
import functools
import math

import jax
import jax.numpy as jnp
from jax import lax
from jax.experimental import pallas as pl
from jax.experimental.pallas import tpu as pltpu
from jax.sharding import PartitionSpec as P

HEADS = 64
KVH = 8
HD = 128
GROUP = HEADS // KVH
STEPS = 3
SPAN = 64
BRANCHES = 16
QBLOCKS = 4
PROBS = 64
QP = PROBS // QBLOCKS
PIECES = STEPS * GROUP
TILE = PIECES * QP
P_DEV = 512
CHUNK = 512

rope_base = 500000.0
masked_score = -1e30
SCALE2 = math.log2(math.e) / math.sqrt(HD)
VMEM = 60 * 1024 * 1024
LIGHT = pl.CostEstimate(flops=0, bytes_accessed=0, transcendentals=0)


def params(grid_rank=1):
    return pltpu.CompilerParams(
        dimension_semantics=("arbitrary",) * grid_rank, vmem_limit_bytes=VMEM
    )


def tables(position):
    half = HD // 2
    exponent = jnp.arange(half, dtype=jnp.float32) * (2.0 / HD)
    frequency = jnp.exp(-math.log(rope_base) * exponent)
    angle = position.astype(jnp.float32)[..., None] * frequency
    cosine = jnp.cos(angle)
    sine = jnp.sin(angle)
    return jnp.concatenate([cosine, cosine], -1), jnp.concatenate([-sine, sine], -1)


def turn(values, cosine, sine):
    return values * cosine + pltpu.roll(values, HD // 2, values.ndim - 1) * sine


def with_ones(values):
    return jnp.concatenate([values, jnp.ones_like(values)], 1)


def dot_nt(a, b):
    return lax.dot_general(a, b, (((1,), (1,)), ((), ())), preferred_element_type=jnp.float32)


def span_kernel(
    len_ref, me_ref, q_ref, qcos_ref, qsin_ref, nk_ref, nv_ref, sk_ref, sv_ref, kcos_ref, ksin_ref,
    q_out, m_out, acc_out, sent_out,
):
    first = pl.program_id(0) * QP
    lane = lax.broadcasted_iota(jnp.int32, (1, QP * SPAN), 1)
    code = jnp.full((1, QP * SPAN), -1, jnp.int32)
    for p in range(QP):
        live = len_ref[first + p, me_ref[0]]
        code = jnp.where((lane >= p * SPAN) & (lane < p * SPAN + live), p, code)
    pieces = []
    for g in range(GROUP):
        for s in range(STEPS):
            lanes = slice(g * HD, (g + 1) * HD)
            raw = q_ref[s, :, lanes].astype(jnp.float32)
            rotated = turn(raw, qcos_ref[s], qsin_ref[s]).astype(jnp.bfloat16)
            q_out[s, :, lanes] = rotated
            pieces.append(rotated)
    query = jnp.concatenate(pieces, 0)
    fresh = [
        turn(nk_ref[s].astype(jnp.float32), qcos_ref[s], qsin_ref[s]).astype(jnp.bfloat16)
        for s in range(STEPS)
    ]
    pad = jnp.zeros((HD - STEPS * QP, HD), jnp.bfloat16)
    fresh_keys = jnp.concatenate(fresh + [pad], 0)
    fresh_vals = jnp.concatenate([nv_ref[s] for s in range(STEPS)] + [pad], 0)
    span_keys = sk_ref[...].reshape(QP * SPAN, HD)
    span_vals = sv_ref[...].reshape(QP * SPAN, HD)
    span_aug = with_ones(span_vals)
    fresh_aug = with_ones(fresh_vals)
    rows = 128
    for r0 in range(0, TILE, rows):
        q = query[r0 : r0 + rows]
        row = lax.broadcasted_iota(jnp.int32, (rows, 1), 0) + r0
        prob = row & (QP - 1)
        piece = row >> 4
        step = piece - 3 * ((piece * 22) >> 6)
        s1 = jnp.where(code == prob, dot_nt(q, span_keys), masked_score)
        lane = lax.broadcasted_iota(jnp.int32, (1, HD), 1)
        ok = ((lane & (QP - 1)) == prob) & ((lane >> 4) <= step)
        s2 = jnp.where(ok, dot_nt(q, fresh_keys), masked_score)
        top = jnp.maximum(s1.max(1, keepdims=True), s2.max(1, keepdims=True)) * SCALE2
        p1 = jnp.exp2(s1 * SCALE2 - top).astype(jnp.bfloat16)
        p2 = jnp.exp2(s2 * SCALE2 - top).astype(jnp.bfloat16)
        m_out[0, r0 : r0 + rows, :] = jnp.broadcast_to(top, (rows, HD))
        acc_out[0, r0 : r0 + rows, :] = jnp.dot(
            p1, span_aug, preferred_element_type=jnp.float32
        ) + jnp.dot(p2, fresh_aug, preferred_element_type=jnp.float32)
    keys = sk_ref[...].astype(jnp.float32)
    kcos = kcos_ref[...][:, None, :]
    ksin = ksin_ref[...][:, None, :]
    sent_out[:, :, :HD] = turn(keys, kcos, ksin).astype(jnp.bfloat16)
    sent_out[:, :, HD:] = sv_ref[...]


def span_part(
    lengths, me, queries, qcos, qsin, new_keys, new_values, span_keys, span_values, kcos, ksin
):
    three = lambda width: pl.BlockSpec((STEPS, QP, width), lambda i, *_: (0, i, 0))
    span = lambda width: pl.BlockSpec((QP, SPAN, width), lambda i, *_: (i, 0, 0))
    state = lambda width: pl.BlockSpec((1, TILE, width), lambda i, *_: (i, 0, 0))
    wide = GROUP * HD
    return pl.pallas_call(
        span_kernel,
        grid_spec=pltpu.PrefetchScalarGridSpec(
            num_scalar_prefetch=2,
            grid=(QBLOCKS,),
            in_specs=[
                three(wide), three(HD), three(HD), three(HD), three(HD), span(HD), span(HD),
                pl.BlockSpec((QP, HD), lambda i, *_: (i, 0)),
                pl.BlockSpec((QP, HD), lambda i, *_: (i, 0)),
            ],
            out_specs=[three(wide), state(HD), state(2 * HD), span(2 * HD)],
        ),
        out_shape=[
            jax.ShapeDtypeStruct((STEPS, PROBS, wide), jnp.bfloat16),
            jax.ShapeDtypeStruct((QBLOCKS, TILE, HD), jnp.float32),
            jax.ShapeDtypeStruct((QBLOCKS, TILE, 2 * HD), jnp.float32),
            jax.ShapeDtypeStruct((PROBS, SPAN, 2 * HD), jnp.bfloat16),
        ],
        compiler_params=params(),
        cost_estimate=LIGHT,
    )(lengths, me, queries, qcos, qsin, new_keys, new_values, span_keys, span_values, kcos, ksin)


def pack_kernel(keys_ref, vals_ref, out):
    for c in range(0, P_DEV, HD):
        out[c : c + HD, :] = keys_ref[c : c + HD, :].T
    out[P_DEV:, :] = vals_ref[...]


def pack_block(keys, vals):
    return pl.pallas_call(
        pack_kernel,
        out_shape=jax.ShapeDtypeStruct((2 * P_DEV, HD), jnp.bfloat16),
        compiler_params=pltpu.CompilerParams(vmem_limit_bytes=VMEM),
        cost_estimate=LIGHT,
    )(keys, vals)


def attend(picks, valid, kv, qs, m_ref, acc_ref):
    rows = 128
    keys = []
    vals = []
    for k in picks:
        flat = jnp.concatenate([kv[k, c : c + HD, :] for c in range(0, P_DEV, HD)], 1)
        keys.append(jnp.concatenate([flat, flat], 0))
        vals.append(with_ones(kv[k, P_DEV:, :]))
    for r0 in range(0, TILE, rows):
        at = slice(r0, r0 + rows)
        query = qs[at, :]
        old = m_ref[at, :]
        scores = [jnp.dot(query, key, preferred_element_type=jnp.float32) for key in keys]
        top = old
        for value, ok in zip(scores, valid):
            best = value.max(1, keepdims=True)
            top = jnp.maximum(top, best if ok is None else jnp.where(ok, best, masked_score))
        factor = jnp.exp2(old - top)
        total = acc_ref[at, :] * jnp.concatenate([factor, factor], 1)
        for value, val, ok in zip(scores, vals, valid):
            base = top if ok is None else jnp.where(ok, top, -masked_score)
            weights = jnp.concatenate(
                [
                    jnp.exp2(value[:, c : c + HD] - base).astype(jnp.bfloat16)
                    for c in range(0, P_DEV, HD)
                ],
                1,
            )
            total = total + jnp.dot(weights, val, preferred_element_type=jnp.float32)
        m_ref[at, :] = top
        acc_ref[at, :] = total


def attend_active(places, pat_ref, me_ref, picked, kv, qs, m_ref, acc_ref):
    i = pl.program_id(0)
    me = me_ref[0]
    for k in range(len(places) + 4):
        picked[k] = 0
    count = jnp.int32(0)
    for k, (dz, dy, other) in enumerate(places):
        picked[count] = k
        owner = chip_of(me, dz, -dy) + ((me & 1) ^ other)
        count = count + jnp.where(pat_ref[i, owner] > 0, 1, 0)
    fours = (count + 1) // 4

    def four(t, carry):
        base = 4 * t
        attend(
            [picked[base + k] for k in range(4)],
            [None, None, None, base + 3 < count],
            kv, qs, m_ref, acc_ref,
        )
        return carry

    lax.fori_loop(0, fours, four, 0)

    @pl.when(4 * fours < count)
    def _():
        base = 4 * fours
        attend(
            [picked[base], picked[base + 1]], [None, base + 1 < count], kv, qs, m_ref, acc_ref
        )


def load_state(q_ref, m_in, acc_in, qs, m_ref, acc_ref):
    for g in range(GROUP):
        for s in range(STEPS):
            at = (g * STEPS + s) * QP
            scaled = q_ref[s, :, g * HD : (g + 1) * HD].astype(jnp.float32) * SCALE2
            high = scaled.astype(jnp.bfloat16)
            qs[at : at + QP, :HD] = high
            qs[at : at + QP, HD:] = (scaled - high.astype(jnp.float32)).astype(jnp.bfloat16)
    m_ref[...] = m_in[0]
    acc_ref[...] = acc_in[0]


def fetch(blocks, kv, sems):
    copies = []
    for k, ref in enumerate(blocks):
        count = ref.shape[0]
        copies.append(
            pltpu.make_async_copy(ref, kv.at[pl.ds(k * count, count)], sems.at[k])
        )
    return copies


def prompt_kernel(
    places, pat_ref, me_ref, q_ref, m_in, acc_in, first, second, m_out, acc_out,
    qs, kv, picked, sems,
):
    i = pl.program_id(0)
    copies = fetch([first, second], kv, sems)

    @pl.when(i == 0)
    def _():
        for copy in copies:
            copy.start()

    m_ref, acc_ref = m_out.at[0], acc_out.at[0]
    load_state(q_ref, m_in, acc_in, qs, m_ref, acc_ref)

    @pl.when(i == 0)
    def _():
        for copy in copies:
            copy.wait()

    attend_active(places, pat_ref, me_ref, picked, kv, qs, m_ref, acc_ref)


def final_kernel(
    places, groups, pat_ref, me_ref, head_ref, q_ref, m_in, acc_in, first, second, weight, *refs
):
    outs = refs[: len(groups)]
    qs, m_ref, acc_ref, kv, picked, att, w_s, o_s, sems, w_sems, o_sems = refs[len(groups) :]
    i = pl.program_id(0)
    copies = fetch([first, second], kv, sems)
    chunks = [(k, j, chunk) for k, group in enumerate(groups) for j, chunk in enumerate(group)]

    def weight_copy(n):
        k, j, (base, far, role) = chunks[n]
        at = pl.multiple_of(column(head_ref[0], base, far, role) * CHUNK, CHUNK)
        return pltpu.make_async_copy(
            weight.at[:, pl.ds(at, CHUNK)], w_s.at[n], w_sems.at[n]
        )

    def out_copy(n):
        k, j, _ = chunks[n]
        return pltpu.make_async_copy(o_s.at[n], outs[k].at[j], o_sems.at[n])

    @pl.when(i == 0)
    def _():
        for copy in copies:
            copy.start()
        for n in range(len(chunks)):
            weight_copy(n).start()

    load_state(q_ref, m_in, acc_in, qs, m_ref, acc_ref)

    @pl.when(i == 0)
    def _():
        for copy in copies:
            copy.wait()

    attend_active(places, pat_ref, me_ref, picked, kv, qs, m_ref, acc_ref)
    done = (acc_ref[:, :HD] / acc_ref[:, HD:]).astype(jnp.bfloat16)
    for g in range(GROUP):
        for s in range(STEPS):
            at = (g * STEPS + s) * QP
            row = pl.multiple_of(s * PROBS + i * QP, QP)
            att[pl.ds(row, QP), g * HD : (g + 1) * HD] = done[at : at + QP]

    @pl.when(i == QBLOCKS - 1)
    def _():
        for n in range(len(chunks)):
            weight_copy(n).wait()
            o_s[n] = jnp.dot(
                att[...], w_s[n], preferred_element_type=jnp.float32
            ).astype(jnp.bfloat16)
            out_copy(n).start()
        for n in range(len(chunks)):
            out_copy(n).wait()


def prompt_specs():
    wide = GROUP * HD
    three = pl.BlockSpec((STEPS, QP, wide), lambda i, *_: (0, i, 0))
    state = lambda width: pl.BlockSpec((1, TILE, width), lambda i, *_: (i, 0, 0))
    return three, state(HD), state(2 * HD)


def prompt_part(pattern, me, places, query, top, accum, first, second):
    three, narrow, twice = prompt_specs()
    anywhere = pl.BlockSpec(memory_space=pl.ANY)
    return pl.pallas_call(
        functools.partial(prompt_kernel, places),
        grid_spec=pltpu.PrefetchScalarGridSpec(
            num_scalar_prefetch=2,
            grid=(QBLOCKS,),
            in_specs=[three, narrow, twice, anywhere, anywhere],
            out_specs=[narrow, twice],
            scratch_shapes=[
                pltpu.VMEM((TILE, 2 * HD), jnp.bfloat16),
                pltpu.VMEM((len(places), 2 * P_DEV, HD), jnp.bfloat16),
                pltpu.SMEM((len(places) + 4,), jnp.int32),
                pltpu.SemaphoreType.DMA((2,)),
            ],
        ),
        out_shape=[
            jax.ShapeDtypeStruct((QBLOCKS, TILE, HD), jnp.float32),
            jax.ShapeDtypeStruct((QBLOCKS, TILE, 2 * HD), jnp.float32),
        ],
        compiler_params=params(),
        cost_estimate=LIGHT,
    )(pattern, me, query, top, accum, first, second)


def final_part(pattern, me, head, places, groups, query, top, accum, first, second, weight):
    three, narrow, twice = prompt_specs()
    anywhere = pl.BlockSpec(memory_space=pl.ANY)
    rows = STEPS * PROBS
    depth = weight.shape[0]
    chunks = sum(len(group) for group in groups)
    return pl.pallas_call(
        functools.partial(final_kernel, places, groups),
        grid_spec=pltpu.PrefetchScalarGridSpec(
            num_scalar_prefetch=3,
            grid=(QBLOCKS,),
            in_specs=[three, narrow, twice, anywhere, anywhere, anywhere],
            out_specs=[anywhere] * len(groups),
            scratch_shapes=[
                pltpu.VMEM((TILE, 2 * HD), jnp.bfloat16),
                pltpu.VMEM((TILE, HD), jnp.float32),
                pltpu.VMEM((TILE, 2 * HD), jnp.float32),
                pltpu.VMEM((len(places), 2 * P_DEV, HD), jnp.bfloat16),
                pltpu.SMEM((len(places) + 4,), jnp.int32),
                pltpu.VMEM((rows, GROUP * HD), jnp.bfloat16),
                pltpu.VMEM((chunks, depth, CHUNK), jnp.bfloat16),
                pltpu.VMEM((chunks, rows, CHUNK), jnp.bfloat16),
                pltpu.SemaphoreType.DMA((2,)),
                pltpu.SemaphoreType.DMA((chunks,)),
                pltpu.SemaphoreType.DMA((chunks,)),
            ],
        ),
        out_shape=[
            jax.ShapeDtypeStruct((len(group), rows, CHUNK), jnp.bfloat16) for group in groups
        ],
        compiler_params=params(),
        cost_estimate=LIGHT,
    )(pattern, me, head, query, top, accum, first, second, weight)


def flip(r):
    return (0x36 >> (2 * r)) & 3


def column(head, base, far, r):
    return base + (((head // 4) ^ far) * 4) + ((head & 3) ^ flip(r))


def assemble_kernel(counts, given, cols, *refs):
    sources, out = refs[given : given + len(counts)], refs[-1]
    i = pl.program_id(0)
    base = 0
    for count, ref in zip(counts, sources):

        @pl.when((i >= base) & (i < base + count))
        def _(ref=ref, base=base):
            out[...] = ref[0]

        base += count


def assemble(head, place_of, sources, earlier=None):
    rows = sources[0].shape[1]
    counts = [value.shape[0] for value in sources]
    bases = [sum(counts[:k]) for k in range(len(counts))]
    given = [] if earlier is None else [earlier]

    def place(base, count):
        return pl.BlockSpec(
            (1, rows, CHUNK), lambda i, head: (jnp.clip(i - base, 0, count - 1), 0, 0)
        )

    return pl.pallas_call(
        functools.partial(assemble_kernel, counts, len(given)),
        grid_spec=pltpu.PrefetchScalarGridSpec(
            num_scalar_prefetch=1,
            grid=(sum(counts),),
            in_specs=[pl.BlockSpec(memory_space=pl.ANY)] * len(given)
            + [place(base, count) for base, count in zip(bases, counts)],
            out_specs=pl.BlockSpec((rows, CHUNK), lambda i, head: (0, place_of(head[0], i))),
        ),
        out_shape=jax.ShapeDtypeStruct((rows, 16 * CHUNK), jnp.bfloat16),
        input_output_aliases={} if earlier is None else {1: 0},
        compiler_params=params(),
        cost_estimate=LIGHT,
    )(head, *given, *sources)


def join_kernel(first_ref, begin_ref, len_ref, source, keys_out, vals_out):
    problem = first_ref[0] + pl.program_id(0)
    total = BRANCHES * SPAN
    flat = source[:, 0].reshape(total, 2 * HD)
    lane = lax.broadcasted_iota(jnp.int32, (1, total), 1)
    target = jnp.full((1, total), -1, jnp.int32)
    for b in range(BRANCHES):
        live = (lane >= b * SPAN) & (lane < b * SPAN + len_ref[problem, b])
        begin = begin_ref[problem, b] - P_DEV * BRANCHES - b * SPAN
        target = jnp.where(live, lane + begin, target)
    rows = 256
    for r0 in range(0, total, rows):
        slot = lax.broadcasted_iota(jnp.int32, (rows, 1), 0) + r0
        pick = jnp.where(target == slot, 1.0, 0.0).astype(jnp.bfloat16)
        got = jnp.dot(pick, flat, preferred_element_type=jnp.float32).astype(jnp.bfloat16)
        keys_out[0, r0 : r0 + rows, :] = got[:, :HD]
        vals_out[0, r0 : r0 + rows, :] = got[:, HD:]


def join(first, begins, lengths, source):
    share = source.shape[1]
    total = BRANCHES * SPAN
    out = pl.BlockSpec((1, total, HD), lambda i, *_: (i, 0, 0))
    shape = jax.ShapeDtypeStruct((share, total, HD), jnp.bfloat16)
    return pl.pallas_call(
        join_kernel,
        grid_spec=pltpu.PrefetchScalarGridSpec(
            num_scalar_prefetch=3,
            grid=(share,),
            in_specs=[pl.BlockSpec((BRANCHES, 1, SPAN, 2 * HD), lambda i, *_: (0, i, 0, 0))],
            out_specs=[out, out],
        ),
        out_shape=[shape, shape],
        compiler_params=params(),
        cost_estimate=LIGHT,
    )(first, begins, lengths, source)


def chip_of(branch, dz, dy):
    return ((branch // 8) ^ dz) * 8 + ((branch // 2 + dy) % 4) * 2


def move_chip(value, dz, dy):
    perm = [(b, chip_of(b, dz, dy) + b % 2) for b in range(BRANCHES)]
    return lax.ppermute(value, "branch", perm)


def swap_core(value):
    return lax.ppermute(value, "branch", [(b, b ^ 1) for b in range(BRANCHES)])


def move_x(value, flip):
    return lax.ppermute(value, "head", [(h, h ^ flip) for h in range(KVH)])


def move_roles(o, p, q):
    return move_x(p, 1), move_x(q, 3), move_x(o, 2)


def add(*values):
    total = values[0].astype(jnp.float32)
    for value in values[1:]:
        total = total + value.astype(jnp.float32)
    return total.astype(jnp.bfloat16)


def after(value, *others):
    return lax.optimization_barrier((value, others))[0]


def shards(
    queries, new_keys, new_values, prompt_keys, prompt_values, span_keys, span_values,
    span_lengths, join_offsets, pattern, out_weight,
):
    me = lax.axis_index("branch")
    one = me.reshape(1)
    head = lax.axis_index("head").reshape(1)
    prompt_len = P_DEV * BRANCHES
    share = PROBS // BRANCHES

    own = pack_block(prompt_keys, prompt_values)
    above = move_chip(own, 1, 0)
    near = [own, above, move_chip(own, 0, 1), move_chip(own, 0, 3)]
    near_at = [(0, 0), (1, 0), (0, 1), (0, 3)]
    far = [move_chip(own, 0, 2)] + [move_chip(above, 0, dy) for dy in (1, 3, 2)]
    far_at = [(0, 2), (1, 1), (1, 3), (1, 2)]

    near_stack = jnp.stack(near)
    near_other = swap_core(near_stack)

    lengths = lax.dynamic_slice_in_dim(span_lengths, me, 1, 1)[:, 0]
    shift = lax.dynamic_slice_in_dim(join_offsets, me, 1, 1)[:, 0] - prompt_len
    position = prompt_len + lengths[None, :] + jnp.arange(STEPS, dtype=jnp.int32)[:, None]
    qcos, qsin = tables(position)
    kcos, ksin = tables(shift)
    query, top, accum, sent = span_part(
        span_lengths,
        one,
        after(jnp.transpose(queries[0], (1, 0, 2)), near_stack),
        qcos,
        qsin,
        jnp.transpose(new_keys[0], (1, 0, 2)),
        jnp.transpose(new_values[0], (1, 0, 2)),
        span_keys[0],
        span_values[0],
        kcos,
        ksin,
    )

    pattern = pattern[0]
    near_places = [(dz, dy, other) for other in (0, 1) for dz, dy in near_at]
    far_places = [(dz, dy, other) for other in (0, 1) for dz, dy in far_at]
    top, accum = prompt_part(
        pattern, one, near_places, query, top, accum, near_stack, near_other
    )
    far_stack = jnp.stack(after(far, top))
    far_other = swap_core(far_stack)

    half = 8
    roles = range(4)
    groups = [[(half, 1, r) for r in roles]]
    groups += [[(0, far, r) for far in (1, 0)] for r in roles]
    groups += [[(half, 0, r) for r in roles]]
    zsend, xo, xp, xq, xx, zkeep = final_part(
        pattern, one, head, far_places, groups, query, top, accum, far_stack, far_other, out_weight
    )
    got_z = move_x(zsend, 4)
    got_x = move_roles(xo, xp, xq)
    got_x = after(got_x, got_z)
    xsend = add(xx[0], *[got[0] for got in got_x])
    got_x_z = move_x(xsend, 4)
    got_z = after(got_z, xsend)
    zo, zp, zq, zx = [add(zkeep[r], got_z[r]) for r in range(4)]
    sent = after(sent, zx).reshape(BRANCHES, share, SPAN, 2 * HD)
    gathered = lax.all_to_all(sent, "branch", 0, 0, tiled=True)
    zsum = add(zx, *move_roles(zo, zp, zq))
    xsum = add(xx[1], *[got[1] for got in got_x], got_x_z)

    zsum = after(zsum, xsum)
    zp, zq, zo = move_roles(zsum, zsum, zsum)
    pair = jnp.stack([move_x(xsum, 4), xsum])
    xp, xq, xo = move_roles(pair, pair, pair)
    joined_keys, joined_values = join(
        (me * share).reshape(1), join_offsets, span_lengths, after(gathered, pair)
    )
    zfour = jnp.stack(after([zo, zp, zq, zsum], joined_keys))
    zother = move_x(zfour, 4)
    mixed = assemble(
        head,
        lambda h, i: jnp.where(i < 8, column(h, 0, 1 - (i & 1), i >> 1), column(h, half, 0, i - 8)),
        [xo, xp, xq, pair, zfour],
    )
    mixed = assemble(head, lambda h, i: column(h, half, 1, i), [zother], mixed)
    mixed = jnp.transpose(mixed.reshape(STEPS, PROBS, 16 * CHUNK), (1, 0, 2))[None]
    return mixed, joined_keys, joined_values


def solution(mesh):
    return jax.shard_map(
        shards,
        mesh=mesh,
        in_specs=(
            P("branch", None, None, "head"),
            P("branch", None, None, "head"),
            P("branch", None, None, "head"),
            P("branch", "head"),
            P("branch", "head"),
            P("branch", None, None, "head"),
            P("branch", None, None, "head"),
            P(),
            P(),
            P("branch", None, None),
            P("head", None),
        ),
        out_specs=(
            P("branch", None, None, None),
            P("branch", None, "head"),
            P("branch", None, "head"),
        ),
        check_vma=False,
    )
```

```python
import functools
import math

import jax
import jax.numpy as jnp
import numpy as np
from jax import lax
from jax.experimental import pallas as pl
from jax.experimental.pallas import tpu as pltpu
from jax.sharding import PartitionSpec as P

HEADS = 64
KVH = 8
HD = 128
GROUP = HEADS // KVH
STEPS = 3
SPAN = 64
BRANCHES = 16
QBLOCKS = 4
PROBS = 64
QP = PROBS // QBLOCKS
PIECES = STEPS * GROUP
TILE = PIECES * QP
P_DEV = 512
CHUNK = 512

rope_base = 500000.0
masked_score = -1e30
SCALE2 = math.log2(math.e) / math.sqrt(HD)
VMEM = 60 * 1024 * 1024
LIGHT = pl.CostEstimate(flops=0, bytes_accessed=0, transcendentals=0)


def params(grid_rank=1):
    return pltpu.CompilerParams(
        dimension_semantics=("arbitrary",) * grid_rank, vmem_limit_bytes=VMEM
    )


def tables(position):
    half = HD // 2
    exponent = np.arange(half) * (2.0 / HD)
    frequency = np.tile(np.exp(-math.log(rope_base) * exponent), 2).astype(np.float32)
    sign = np.repeat(np.float32([-1.0, 1.0]), half)
    angle = position.astype(jnp.float32)[..., None] * frequency
    return jnp.cos(angle), jnp.sin(angle) * sign


def turn(values, cosine, sine):
    return values * cosine + pltpu.roll(values, HD // 2, values.ndim - 1) * sine


def with_ones(values):
    return jnp.concatenate([values, jnp.ones_like(values)], 1)


def dot(a, b):
    return jnp.dot(a, b, preferred_element_type=jnp.float32)


def span_kernel(
    len_ref, me_ref, q_ref, cos_ref, sin_ref, nk_ref, nv_ref, sk_ref, sv_ref,
    q_out, m_out, acc_out, sent_out,
):
    first = pl.program_id(0) * QP
    lane = lax.broadcasted_iota(jnp.int32, (1, QP * SPAN), 1)
    code = jnp.full((1, QP * SPAN), -1, jnp.int32)
    for p in range(QP):
        live = len_ref[me_ref[0], first + p]
        code = jnp.where((lane >= p * SPAN) & (lane < p * SPAN + live), p, code)
    pieces = []
    for g in range(GROUP):
        for s in range(STEPS):
            lanes = slice(g * HD, (g + 1) * HD)
            raw = q_ref[s, :, lanes].astype(jnp.float32)
            rotated = turn(raw, cos_ref[s], sin_ref[s]).astype(jnp.bfloat16)
            q_out[s, :, lanes] = rotated
            pieces.append(rotated)
    query = jnp.concatenate(pieces, 0)
    fresh = [
        turn(nk_ref[s].astype(jnp.float32), cos_ref[s], sin_ref[s]).astype(jnp.bfloat16)
        for s in range(STEPS)
    ]
    pad = jnp.zeros((HD - STEPS * QP, HD), jnp.bfloat16)
    fresh_keys = jnp.concatenate(fresh + [pad], 0)
    fresh_vals = jnp.concatenate([nv_ref[s] for s in range(STEPS)] + [pad], 0)
    span_keys = sk_ref[...].reshape(QP * SPAN, HD)
    span_vals = sv_ref[...].reshape(QP * SPAN, HD)
    span_aug = with_ones(span_vals)
    fresh_aug = with_ones(fresh_vals)
    span_turned = span_keys.T
    fresh_turned = fresh_keys.T
    rows = 128
    for r0 in range(0, TILE, rows):
        q = query[r0 : r0 + rows]
        row = lax.broadcasted_iota(jnp.int32, (rows, 1), 0) + r0
        prob = row & (QP - 1)
        piece = row >> 4
        step = piece - 3 * ((piece * 22) >> 6)
        s1 = jnp.where(code == prob, dot(q, span_turned), masked_score)
        lane = lax.broadcasted_iota(jnp.int32, (1, HD), 1)
        ok = ((lane & (QP - 1)) == prob) & ((lane >> 4) <= step)
        s2 = jnp.where(ok, dot(q, fresh_turned), masked_score)
        top = jnp.maximum(s1.max(1, keepdims=True), s2.max(1, keepdims=True)) * SCALE2
        p1 = jnp.exp2(s1 * SCALE2 - top).astype(jnp.bfloat16)
        p2 = jnp.exp2(s2 * SCALE2 - top).astype(jnp.bfloat16)
        m_out[0, r0 : r0 + rows, :] = jnp.broadcast_to(top, (rows, HD))
        acc_out[0, r0 : r0 + rows, :] = jnp.dot(
            p1, span_aug, preferred_element_type=jnp.float32
        ) + jnp.dot(p2, fresh_aug, preferred_element_type=jnp.float32)
    keys = sk_ref[...].astype(jnp.float32)
    kcos = cos_ref[STEPS][:, None, :]
    ksin = sin_ref[STEPS][:, None, :]
    sent_out[:, :, :HD] = turn(keys, kcos, ksin).astype(jnp.bfloat16)
    sent_out[:, :, HD:] = sv_ref[...]


def span_part(
    lengths, me, queries, cosine, sine, new_keys, new_values, span_keys, span_values
):
    three = lambda width: pl.BlockSpec((STEPS, QP, width), lambda i, *_: (0, i, 0))
    span = lambda width: pl.BlockSpec((QP, SPAN, width), lambda i, *_: (i, 0, 0))
    table = pl.BlockSpec((STEPS + 1, QP, HD), lambda i, *_: (0, i, 0))
    state = lambda width: pl.BlockSpec((1, TILE, width), lambda i, *_: (i, 0, 0))
    wide = GROUP * HD
    return pl.pallas_call(
        span_kernel,
        grid_spec=pltpu.PrefetchScalarGridSpec(
            num_scalar_prefetch=2,
            grid=(QBLOCKS,),
            in_specs=[
                three(wide), table, table, three(HD), three(HD), span(HD), span(HD),
            ],
            out_specs=[three(wide), state(HD), state(2 * HD), span(2 * HD)],
        ),
        out_shape=[
            jax.ShapeDtypeStruct((STEPS, PROBS, wide), jnp.bfloat16),
            jax.ShapeDtypeStruct((QBLOCKS, TILE, HD), jnp.float32),
            jax.ShapeDtypeStruct((QBLOCKS, TILE, 2 * HD), jnp.float32),
            jax.ShapeDtypeStruct((PROBS, SPAN, 2 * HD), jnp.bfloat16),
        ],
        compiler_params=params(),
        cost_estimate=LIGHT,
    )(lengths, me, queries, cosine, sine, new_keys, new_values, span_keys, span_values)


def pack_kernel(keys_ref, vals_ref, out):
    for c in range(0, P_DEV, HD):
        out[c : c + HD, :] = keys_ref[c : c + HD, :].T
    out[P_DEV:, :] = vals_ref[...]


def pack_block(keys, vals):
    return pl.pallas_call(
        pack_kernel,
        out_shape=jax.ShapeDtypeStruct((2 * P_DEV, HD), jnp.bfloat16),
        compiler_params=pltpu.CompilerParams(vmem_limit_bytes=VMEM),
        cost_estimate=LIGHT,
    )(keys, vals)


def attend(picks, valid, kv, qs, m_ref, acc_ref):
    rows = 128
    keys = []
    vals = []
    for k in picks:
        flat = jnp.concatenate([kv[k, c : c + HD, :] for c in range(0, P_DEV, HD)], 1)
        keys.append(jnp.concatenate([flat, flat], 0))
        vals.append(with_ones(kv[k, P_DEV:, :]))
    for r0 in range(0, TILE, rows):
        at = slice(r0, r0 + rows)
        query = qs[at, :]
        old = m_ref[at, :]
        scores = [jnp.dot(query, key, preferred_element_type=jnp.float32) for key in keys]
        top = old
        for value, ok in zip(scores, valid):
            best = value.max(1, keepdims=True)
            top = jnp.maximum(top, best if ok is None else jnp.where(ok, best, masked_score))
        factor = jnp.exp2(old - top)
        total = acc_ref[at, :] * jnp.concatenate([factor, factor], 1)
        for value, val, ok in zip(scores, vals, valid):
            base = top if ok is None else jnp.where(ok, top, -masked_score)
            weights = jnp.concatenate(
                [
                    jnp.exp2(value[:, c : c + HD] - base).astype(jnp.bfloat16)
                    for c in range(0, P_DEV, HD)
                ],
                1,
            )
            total = total + jnp.dot(weights, val, preferred_element_type=jnp.float32)
        m_ref[at, :] = top
        acc_ref[at, :] = total


def attend_active(places, pat_ref, me_ref, picked, kv, qs, m_ref, acc_ref):
    i = pl.program_id(0)
    me = me_ref[0]
    for k in range(len(places) + 4):
        picked[k] = 0
    count = jnp.int32(0)
    for k, (dz, dy, other) in enumerate(places):
        picked[count] = k
        owner = chip_of(me, dz, -dy) + ((me & 1) ^ other)
        count = count + jnp.where(pat_ref[i, owner] > 0, 1, 0)
    fours = (count + 1) // 4

    def four(t, carry):
        base = 4 * t
        attend(
            [picked[base + k] for k in range(4)],
            [None, None, None, base + 3 < count],
            kv, qs, m_ref, acc_ref,
        )
        return carry

    lax.fori_loop(0, fours, four, 0)

    @pl.when(4 * fours < count)
    def _():
        base = 4 * fours
        attend(
            [picked[base], picked[base + 1]], [None, base + 1 < count], kv, qs, m_ref, acc_ref
        )


def load_state(q_ref, m_in, acc_in, qs, m_ref, acc_ref):
    for g in range(GROUP):
        for s in range(STEPS):
            at = (g * STEPS + s) * QP
            scaled = q_ref[s, :, g * HD : (g + 1) * HD].astype(jnp.float32) * SCALE2
            high = scaled.astype(jnp.bfloat16)
            qs[at : at + QP, :HD] = high
            qs[at : at + QP, HD:] = (scaled - high.astype(jnp.float32)).astype(jnp.bfloat16)
    m_ref[...] = m_in[0]
    acc_ref[...] = acc_in[0]


def fetch(blocks, kv, sems):
    copies = []
    for k, ref in enumerate(blocks):
        count = ref.shape[0]
        copies.append(
            pltpu.make_async_copy(ref, kv.at[pl.ds(k * count, count)], sems.at[k])
        )
    return copies


def prompt_kernel(
    places, pat_ref, me_ref, q_ref, m_in, acc_in, first, second, m_out, acc_out,
    qs, kv, picked, sems,
):
    i = pl.program_id(0)
    copies = fetch([first, second], kv, sems)

    @pl.when(i == 0)
    def _():
        for copy in copies:
            copy.start()

    m_ref, acc_ref = m_out.at[0], acc_out.at[0]
    load_state(q_ref, m_in, acc_in, qs, m_ref, acc_ref)

    @pl.when(i == 0)
    def _():
        for copy in copies:
            copy.wait()

    attend_active(places, pat_ref, me_ref, picked, kv, qs, m_ref, acc_ref)


def final_kernel(
    places, groups, pat_ref, me_ref, head_ref, q_ref, m_in, acc_in, first, second, weight, *refs
):
    outs = refs[: len(groups)]
    qs, m_ref, acc_ref, kv, picked, att, w_s, o_s, sems, w_sems, o_sems = refs[len(groups) :]
    i = pl.program_id(0)
    copies = fetch([first, second], kv, sems)
    chunks = [(k, j, chunk) for k, group in enumerate(groups) for j, chunk in enumerate(group)]

    def weight_copy(n):
        k, j, (base, far, role) = chunks[n]
        at = pl.multiple_of(column(head_ref[0], base, far, role) * CHUNK, CHUNK)
        return pltpu.make_async_copy(
            weight.at[:, pl.ds(at, CHUNK)], w_s.at[n], w_sems.at[n]
        )

    def out_copy(n):
        k, j, _ = chunks[n]
        return pltpu.make_async_copy(o_s.at[n], outs[k].at[j], o_sems.at[n])

    @pl.when(i == 0)
    def _():
        for copy in copies:
            copy.start()
        for n in range(len(chunks)):
            weight_copy(n).start()

    load_state(q_ref, m_in, acc_in, qs, m_ref, acc_ref)

    @pl.when(i == 0)
    def _():
        for copy in copies:
            copy.wait()

    attend_active(places, pat_ref, me_ref, picked, kv, qs, m_ref, acc_ref)
    done = (acc_ref[:, :HD] / acc_ref[:, HD:]).astype(jnp.bfloat16)
    for g in range(GROUP):
        for s in range(STEPS):
            at = (g * STEPS + s) * QP
            row = pl.multiple_of(s * PROBS + i * QP, QP)
            att[pl.ds(row, QP), g * HD : (g + 1) * HD] = done[at : at + QP]

    @pl.when(i == QBLOCKS - 1)
    def _():
        for n in range(len(chunks)):
            weight_copy(n).wait()
            o_s[n] = jnp.dot(
                att[...], w_s[n], preferred_element_type=jnp.float32
            ).astype(jnp.bfloat16)
            out_copy(n).start()
        for n in range(len(chunks)):
            out_copy(n).wait()


def prompt_specs():
    wide = GROUP * HD
    three = pl.BlockSpec((STEPS, QP, wide), lambda i, *_: (0, i, 0))
    state = lambda width: pl.BlockSpec((1, TILE, width), lambda i, *_: (i, 0, 0))
    return three, state(HD), state(2 * HD)


def prompt_part(pattern, me, places, query, top, accum, first, second):
    three, narrow, twice = prompt_specs()
    anywhere = pl.BlockSpec(memory_space=pl.ANY)
    return pl.pallas_call(
        functools.partial(prompt_kernel, places),
        grid_spec=pltpu.PrefetchScalarGridSpec(
            num_scalar_prefetch=2,
            grid=(QBLOCKS,),
            in_specs=[three, narrow, twice, anywhere, anywhere],
            out_specs=[narrow, twice],
            scratch_shapes=[
                pltpu.VMEM((TILE, 2 * HD), jnp.bfloat16),
                pltpu.VMEM((len(places), 2 * P_DEV, HD), jnp.bfloat16),
                pltpu.SMEM((len(places) + 4,), jnp.int32),
                pltpu.SemaphoreType.DMA((2,)),
            ],
        ),
        out_shape=[
            jax.ShapeDtypeStruct((QBLOCKS, TILE, HD), jnp.float32),
            jax.ShapeDtypeStruct((QBLOCKS, TILE, 2 * HD), jnp.float32),
        ],
        compiler_params=params(),
        cost_estimate=LIGHT,
    )(pattern, me, query, top, accum, first, second)


def final_part(pattern, me, head, places, groups, query, top, accum, first, second, weight):
    three, narrow, twice = prompt_specs()
    anywhere = pl.BlockSpec(memory_space=pl.ANY)
    rows = STEPS * PROBS
    depth = weight.shape[0]
    chunks = sum(len(group) for group in groups)
    return pl.pallas_call(
        functools.partial(final_kernel, places, groups),
        grid_spec=pltpu.PrefetchScalarGridSpec(
            num_scalar_prefetch=3,
            grid=(QBLOCKS,),
            in_specs=[three, narrow, twice, anywhere, anywhere, anywhere],
            out_specs=[anywhere] * len(groups),
            scratch_shapes=[
                pltpu.VMEM((TILE, 2 * HD), jnp.bfloat16),
                pltpu.VMEM((TILE, HD), jnp.float32),
                pltpu.VMEM((TILE, 2 * HD), jnp.float32),
                pltpu.VMEM((len(places), 2 * P_DEV, HD), jnp.bfloat16),
                pltpu.SMEM((len(places) + 4,), jnp.int32),
                pltpu.VMEM((rows, GROUP * HD), jnp.bfloat16),
                pltpu.VMEM((chunks, depth, CHUNK), jnp.bfloat16),
                pltpu.VMEM((chunks, rows, CHUNK), jnp.bfloat16),
                pltpu.SemaphoreType.DMA((2,)),
                pltpu.SemaphoreType.DMA((chunks,)),
                pltpu.SemaphoreType.DMA((chunks,)),
            ],
        ),
        out_shape=[
            jax.ShapeDtypeStruct((len(group), rows, CHUNK), jnp.bfloat16) for group in groups
        ],
        compiler_params=params(),
        cost_estimate=LIGHT,
    )(pattern, me, head, query, top, accum, first, second, weight)


def flip(r):
    return (0x36 >> (2 * r)) & 3


def column(head, base, far, r):
    return base + (((head // 4) ^ far) * 4) + ((head & 3) ^ flip(r))


def chunk_at(head_ref, place):
    return pl.ds(pl.multiple_of(column(head_ref[0], *place) * CHUNK, CHUNK), CHUNK)


def assemble_kernel(places, head_ref, *refs):
    for ref, group in zip(refs[:-1], places):
        for j, place in enumerate(group):
            refs[-1][:, chunk_at(head_ref, place)] = ref[j]


def assemble(head, places, sources):
    rows = sources[0].shape[1]
    whole = lambda value: pl.BlockSpec(value.shape, lambda i, head: (0, 0, 0))
    return pl.pallas_call(
        functools.partial(assemble_kernel, places),
        grid_spec=pltpu.PrefetchScalarGridSpec(
            num_scalar_prefetch=1,
            grid=(1,),
            in_specs=[whole(value) for value in sources],
            out_specs=pl.BlockSpec((rows, 16 * CHUNK), lambda i, head: (0, 0)),
        ),
        out_shape=jax.ShapeDtypeStruct((rows, 16 * CHUNK), jnp.bfloat16),
        compiler_params=params(),
        cost_estimate=LIGHT,
    )(head, *sources)


def complete_kernel(places, head_ref, earlier, source, out, sems):
    copies = [
        pltpu.make_async_copy(source.at[j], out.at[:, chunk_at(head_ref, place)], sems.at[j])
        for j, place in enumerate(places)
    ]
    for copy in copies:
        copy.start()
    for copy in copies:
        copy.wait()


def complete(head, places, earlier, source):
    anywhere = pl.BlockSpec(memory_space=pl.ANY)
    return pl.pallas_call(
        functools.partial(complete_kernel, places),
        grid_spec=pltpu.PrefetchScalarGridSpec(
            num_scalar_prefetch=1,
            grid=(1,),
            in_specs=[anywhere, pl.BlockSpec(source.shape, lambda i, head: (0, 0, 0))],
            out_specs=anywhere,
            scratch_shapes=[pltpu.SemaphoreType.DMA((len(places),))],
        ),
        out_shape=jax.ShapeDtypeStruct(earlier.shape, earlier.dtype),
        input_output_aliases={1: 0},
        compiler_params=params(),
        cost_estimate=LIGHT,
    )(head, earlier, source)


def join_kernel(first_ref, begin_ref, len_ref, source, keys_out, vals_out):
    problem = first_ref[0] + pl.program_id(0)
    total = BRANCHES * SPAN
    flat = source[:, 0].reshape(total, 2 * HD)
    lane = lax.broadcasted_iota(jnp.int32, (1, total), 1)
    target = jnp.full((1, total), -1, jnp.int32)
    for b in range(BRANCHES):
        live = (lane >= b * SPAN) & (lane < b * SPAN + len_ref[b, problem])
        begin = begin_ref[b, problem] - P_DEV * BRANCHES - b * SPAN
        target = jnp.where(live, lane + begin, target)
    rows = 256
    for r0 in range(0, total, rows):
        slot = lax.broadcasted_iota(jnp.int32, (rows, 1), 0) + r0
        pick = jnp.where(target == slot, 1.0, 0.0).astype(jnp.bfloat16)
        got = jnp.dot(pick, flat, preferred_element_type=jnp.float32).astype(jnp.bfloat16)
        keys_out[0, r0 : r0 + rows, :] = got[:, :HD]
        vals_out[0, r0 : r0 + rows, :] = got[:, HD:]


def join(first, begins, lengths, source):
    share = source.shape[1]
    total = BRANCHES * SPAN
    out = pl.BlockSpec((1, total, HD), lambda i, *_: (i, 0, 0))
    shape = jax.ShapeDtypeStruct((share, total, HD), jnp.bfloat16)
    return pl.pallas_call(
        join_kernel,
        grid_spec=pltpu.PrefetchScalarGridSpec(
            num_scalar_prefetch=3,
            grid=(share,),
            in_specs=[pl.BlockSpec((BRANCHES, 1, SPAN, 2 * HD), lambda i, *_: (0, i, 0, 0))],
            out_specs=[out, out],
        ),
        out_shape=[shape, shape],
        compiler_params=params(),
        cost_estimate=LIGHT,
    )(first, begins, lengths, source)


def chip_of(branch, dz, dy):
    return ((branch // 8) ^ dz) * 8 + ((branch // 2 + dy) % 4) * 2


def move_chip(value, dz, dy):
    perm = [(b, chip_of(b, dz, dy) + b % 2) for b in range(BRANCHES)]
    return lax.ppermute(value, "branch", perm)


def swap_core(value):
    return lax.ppermute(value, "branch", [(b, b ^ 1) for b in range(BRANCHES)])


def move_x(value, flip):
    return lax.ppermute(value, "head", [(h, h ^ flip) for h in range(KVH)])


def move_roles(o, p, q):
    return move_x(p, 1), move_x(q, 3), move_x(o, 2)


def add(*values):
    total = values[0].astype(jnp.float32)
    for value in values[1:]:
        total = total + value.astype(jnp.float32)
    return total.astype(jnp.bfloat16)


def after(value, *others):
    return lax.optimization_barrier((value, others))[0]


def shards(
    queries, new_keys, new_values, prompt_keys, prompt_values, span_keys, span_values,
    span_lengths, join_offsets, pattern, out_weight,
):
    me = lax.axis_index("branch")
    one = me.reshape(1)
    head = lax.axis_index("head").reshape(1)
    prompt_len = P_DEV * BRANCHES
    share = PROBS // BRANCHES

    own = pack_block(prompt_keys, prompt_values)
    above = move_chip(own, 1, 0)
    across = move_chip(own, 0, 2)
    near = [own, above, move_chip(own, 0, 1), move_chip(own, 0, 3), across]
    near_at = [(0, 0), (1, 0), (0, 1), (0, 3), (0, 2)]
    far_at = [(1, 1), (1, 3), (1, 2)]

    lengths = span_lengths.T
    offsets = join_offsets.T
    live = lax.dynamic_slice_in_dim(lengths, me, 1, 0)
    shift = lax.dynamic_slice_in_dim(offsets, me, 1, 0) - prompt_len
    steps = jnp.arange(STEPS, dtype=jnp.int32)[:, None]
    cosine, sine = tables(jnp.concatenate([prompt_len + live + steps, shift]))
    query, top, accum, sent = span_part(
        lengths,
        one,
        jnp.transpose(queries[0], (1, 0, 2)),
        cosine,
        sine,
        jnp.transpose(new_keys[0], (1, 0, 2)),
        jnp.transpose(new_values[0], (1, 0, 2)),
        span_keys[0],
        span_values[0],
    )

    pattern = pattern[0]
    near_places = [(dz, dy, other) for other in (0, 1) for dz, dy in near_at]
    far_places = [(dz, dy, other) for other in (0, 1) for dz, dy in far_at]
    near = after(near, query)
    far = [move_chip(near[1], 0, 1), move_chip(near[1], 0, 3), move_chip(near[4], 1, 0)]
    near_stack = jnp.stack(near)
    near_other = swap_core(near_stack)
    sent = after(sent, near_stack).reshape(BRANCHES, share, SPAN, 2 * HD)
    gathered = lax.all_to_all(sent, "branch", 0, 0, tiled=True)
    top, accum = prompt_part(
        pattern, one, near_places, query, top, accum, near_stack, near_other
    )
    far_stack = jnp.stack(after(far, top))
    far_other = swap_core(far_stack)

    half = 8
    roles = range(4)
    groups = [[(half, 1, r) for r in roles]]
    groups += [[(0, far, r) for far in (1, 0)] for r in roles]
    groups += [[(half, 0, r) for r in roles]]
    zsend, xo, xp, xq, xx, zkeep = final_part(
        pattern, one, head, far_places, groups, query, top, accum, far_stack, far_other, out_weight
    )
    zsend, xo, xp, xq = after((zsend, xo, xp, xq), gathered)
    got_z = move_x(zsend, 4)
    got_x = move_roles(xo, xp, xq)
    got_x = after(got_x, got_z)
    xsend = add(xx[0], *[got[0] for got in got_x])
    got_x_z = move_x(xsend, 4)
    got_z = after(got_z, xsend)
    zo, zp, zq, zx = [add(zkeep[r], got_z[r]) for r in range(4)]
    zsum = add(zx, *move_roles(zo, zp, zq))
    xsum = add(xx[1], *[got[1] for got in got_x], got_x_z)

    zsum = after(zsum, xsum)
    zp, zq, zo = move_roles(zsum, zsum, zsum)
    pair = jnp.stack([move_x(xsum, 4), xsum])
    xp, xq, xo = move_roles(pair, pair, pair)
    joined_keys, joined_values = join(
        (me * share).reshape(1), offsets, lengths, after(gathered, pair)
    )
    zfour = jnp.stack(after([zo, zp, zq, zsum], joined_keys))
    zother = move_x(zfour, 4)
    both = [[(0, far, r) for far in (1, 0)] for r in roles]
    mixed = assemble(
        head, both + [[(half, 0, r) for r in roles]], [xo, xp, xq, pair, zfour]
    )
    mixed = complete(head, [(half, 1, r) for r in roles], mixed, zother)
    mixed = jnp.transpose(mixed.reshape(STEPS, PROBS, 16 * CHUNK), (1, 0, 2))[None]
    return mixed, joined_keys, joined_values


def solution(mesh):
    return jax.shard_map(
        shards,
        mesh=mesh,
        in_specs=(
            P("branch", None, None, "head"),
            P("branch", None, None, "head"),
            P("branch", None, None, "head"),
            P("branch", "head"),
            P("branch", "head"),
            P("branch", None, None, "head"),
            P("branch", None, None, "head"),
            P(),
            P(),
            P("branch", None, None),
            P("head", None),
        ),
        out_specs=(
            P("branch", None, None, None),
            P("branch", None, "head"),
            P("branch", None, "head"),
        ),
        check_vma=False,
    )
```

```python
import functools
import math

import jax
import jax.numpy as jnp
import numpy as np
from jax import lax
from jax.experimental import pallas as pl
from jax.experimental.pallas import tpu as pltpu
from jax.sharding import PartitionSpec as P

HEADS = 64
KVH = 8
HD = 128
GROUP = HEADS // KVH
STEPS = 3
SPAN = 64
BRANCHES = 16
QBLOCKS = 4
PROBS = 64
QP = PROBS // QBLOCKS
PIECES = STEPS * GROUP
TILE = PIECES * QP
P_DEV = 512
CHUNK = 512

rope_base = 500000.0
masked_score = -1e30
SCALE2 = math.log2(math.e) / math.sqrt(HD)
VMEM = 60 * 1024 * 1024
LIGHT = pl.CostEstimate(flops=0, bytes_accessed=0, transcendentals=0)


def params(grid_rank=1):
    return pltpu.CompilerParams(
        dimension_semantics=("arbitrary",) * grid_rank, vmem_limit_bytes=VMEM
    )


def tables(position):
    half = HD // 2
    exponent = np.arange(half) * (2.0 / HD)
    frequency = np.tile(np.exp(-math.log(rope_base) * exponent), 2).astype(np.float32)
    sign = np.repeat(np.float32([-1.0, 1.0]), half)
    angle = position.astype(jnp.float32)[..., None] * frequency
    return jnp.cos(angle), jnp.sin(angle) * sign


def turn(values, cosine, sine):
    return values * cosine + pltpu.roll(values, HD // 2, values.ndim - 1) * sine


def with_ones(values):
    return jnp.concatenate([values, jnp.ones_like(values)], 1)


def dot(a, b):
    return jnp.dot(a, b, preferred_element_type=jnp.float32)


def span_kernel(
    len_ref, me_ref, q_ref, cos_ref, sin_ref, nk_ref, nv_ref, sk_ref, sv_ref,
    q_out, m_out, acc_out, sent_out,
):
    first = pl.program_id(0) * QP
    lane = lax.broadcasted_iota(jnp.int32, (1, QP * SPAN), 1)
    code = jnp.full((1, QP * SPAN), -1, jnp.int32)
    for p in range(QP):
        live = len_ref[me_ref[0], first + p]
        code = jnp.where((lane >= p * SPAN) & (lane < p * SPAN + live), p, code)
    rotated = {}
    for g in range(GROUP):
        for s in range(STEPS):
            lanes = slice(g * HD, (g + 1) * HD)
            raw = q_ref[s, :, lanes].astype(jnp.float32)
            rotated[g, s] = turn(raw, cos_ref[s], sin_ref[s])
            q_out[s, :, lanes] = rotated[g, s].astype(jnp.bfloat16)
    fresh = [
        turn(nk_ref[s].astype(jnp.float32), cos_ref[s], sin_ref[s]).astype(jnp.bfloat16)
        for s in range(STEPS)
    ]
    pad = jnp.zeros((HD - STEPS * QP, HD), jnp.bfloat16)
    fresh_keys = jnp.concatenate(fresh + [pad], 0).T
    fresh_vals = with_ones(jnp.concatenate([nv_ref[s] for s in range(STEPS)] + [pad], 0))
    few = QP // 2
    rows = few * PIECES
    keys_of = few * SPAN
    row = lax.broadcasted_iota(jnp.int32, (rows, 1), 0)
    piece = row >> 3
    step = piece - 3 * ((piece * 22) >> 6)
    fresh_lane = lax.broadcasted_iota(jnp.int32, (1, HD), 1)
    for part in range(2):
        low = part * few
        prob = (row & (few - 1)) + low
        q = jnp.concatenate(
            [rotated[g, s][low : low + few] for g in range(GROUP) for s in range(STEPS)], 0
        ).astype(jnp.bfloat16)
        span_keys = sk_ref[low : low + few].reshape(keys_of, HD).T
        span_vals = with_ones(sv_ref[low : low + few].reshape(keys_of, HD))
        s1 = jnp.where(
            code[:, part * keys_of : (part + 1) * keys_of] == prob, dot(q, span_keys), masked_score
        )
        ok = ((fresh_lane & (QP - 1)) == prob) & ((fresh_lane >> 4) <= step)
        s2 = jnp.where(ok, dot(q, fresh_keys), masked_score)
        top = jnp.maximum(s1.max(1, keepdims=True), s2.max(1, keepdims=True)) * SCALE2
        p1 = jnp.exp2(s1 * SCALE2 - top).astype(jnp.bfloat16)
        p2 = jnp.exp2(s2 * SCALE2 - top).astype(jnp.bfloat16)
        total = dot(p1, span_vals) + dot(p2, fresh_vals)
        wide = jnp.broadcast_to(top, (rows, HD))
        for k in range(PIECES):
            m_out[0, k * QP + low : k * QP + low + few, :] = wide[k * few : (k + 1) * few]
            acc_out[0, k * QP + low : k * QP + low + few, :] = total[k * few : (k + 1) * few]
    keys = sk_ref[...].astype(jnp.float32)
    kcos = cos_ref[STEPS][:, None, :]
    ksin = sin_ref[STEPS][:, None, :]
    sent_out[:, :, :HD] = turn(keys, kcos, ksin).astype(jnp.bfloat16)
    sent_out[:, :, HD:] = sv_ref[...]


def span_part(
    lengths, me, queries, cosine, sine, new_keys, new_values, span_keys, span_values
):
    three = lambda width: pl.BlockSpec((STEPS, QP, width), lambda i, *_: (0, i, 0))
    span = lambda width: pl.BlockSpec((QP, SPAN, width), lambda i, *_: (i, 0, 0))
    table = pl.BlockSpec((STEPS + 1, QP, HD), lambda i, *_: (0, i, 0))
    state = lambda width: pl.BlockSpec((1, TILE, width), lambda i, *_: (i, 0, 0))
    wide = GROUP * HD
    return pl.pallas_call(
        span_kernel,
        grid_spec=pltpu.PrefetchScalarGridSpec(
            num_scalar_prefetch=2,
            grid=(QBLOCKS,),
            in_specs=[
                three(wide), table, table, three(HD), three(HD), span(HD), span(HD),
            ],
            out_specs=[three(wide), state(HD), state(2 * HD), span(2 * HD)],
        ),
        out_shape=[
            jax.ShapeDtypeStruct((STEPS, PROBS, wide), jnp.bfloat16),
            jax.ShapeDtypeStruct((QBLOCKS, TILE, HD), jnp.float32),
            jax.ShapeDtypeStruct((QBLOCKS, TILE, 2 * HD), jnp.float32),
            jax.ShapeDtypeStruct((PROBS, SPAN, 2 * HD), jnp.bfloat16),
        ],
        compiler_params=params(),
        cost_estimate=LIGHT,
    )(lengths, me, queries, cosine, sine, new_keys, new_values, span_keys, span_values)


def pack_kernel(keys_ref, vals_ref, out):
    for c in range(0, P_DEV, HD):
        out[c : c + HD, :] = keys_ref[c : c + HD, :].T
    out[P_DEV:, :] = vals_ref[...]


def pack_block(keys, vals):
    return pl.pallas_call(
        pack_kernel,
        out_shape=jax.ShapeDtypeStruct((2 * P_DEV, HD), jnp.bfloat16),
        compiler_params=pltpu.CompilerParams(vmem_limit_bytes=VMEM),
        cost_estimate=LIGHT,
    )(keys, vals)


def attend(picks, valid, kv, qs, m_ref, acc_ref):
    rows = 128
    keys = []
    vals = []
    for k in picks:
        flat = jnp.concatenate([kv[k, c : c + HD, :] for c in range(0, P_DEV, HD)], 1)
        keys.append(jnp.concatenate([flat, flat], 0))
        vals.append(with_ones(kv[k, P_DEV:, :]))
    for r0 in range(0, TILE, rows):
        at = slice(r0, r0 + rows)
        query = qs[at, :]
        old = m_ref[at, :]
        scores = [jnp.dot(query, key, preferred_element_type=jnp.float32) for key in keys]
        top = old
        for value, ok in zip(scores, valid):
            best = value.max(1, keepdims=True)
            top = jnp.maximum(top, best if ok is None else jnp.where(ok, best, masked_score))
        factor = jnp.exp2(old - top)
        total = acc_ref[at, :] * jnp.concatenate([factor, factor], 1)
        for value, val, ok in zip(scores, vals, valid):
            base = top if ok is None else jnp.where(ok, top, -masked_score)
            weights = jnp.concatenate(
                [
                    jnp.exp2(value[:, c : c + HD] - base).astype(jnp.bfloat16)
                    for c in range(0, P_DEV, HD)
                ],
                1,
            )
            total = total + jnp.dot(weights, val, preferred_element_type=jnp.float32)
        m_ref[at, :] = top
        acc_ref[at, :] = total


def attend_active(places, pat_ref, me_ref, picked, kv, qs, m_ref, acc_ref):
    i = pl.program_id(0)
    me = me_ref[0]
    for k in range(len(places) + 4):
        picked[k] = 0
    count = jnp.int32(0)
    for k, (dz, dy, other) in enumerate(places):
        picked[count] = k
        owner = chip_of(me, dz, -dy) + ((me & 1) ^ other)
        count = count + jnp.where(pat_ref[i, owner] > 0, 1, 0)
    fours = (count + 1) // 4

    def four(t, carry):
        base = 4 * t
        attend(
            [picked[base + k] for k in range(4)],
            [None, None, None, base + 3 < count],
            kv, qs, m_ref, acc_ref,
        )
        return carry

    lax.fori_loop(0, fours, four, 0)

    @pl.when(4 * fours < count)
    def _():
        base = 4 * fours
        attend(
            [picked[base], picked[base + 1]], [None, base + 1 < count], kv, qs, m_ref, acc_ref
        )


def load_state(q_ref, m_in, acc_in, qs, m_ref, acc_ref):
    for g in range(GROUP):
        for s in range(STEPS):
            at = (g * STEPS + s) * QP
            scaled = q_ref[s, :, g * HD : (g + 1) * HD].astype(jnp.float32) * SCALE2
            high = scaled.astype(jnp.bfloat16)
            qs[at : at + QP, :HD] = high
            qs[at : at + QP, HD:] = (scaled - high.astype(jnp.float32)).astype(jnp.bfloat16)
    m_ref[...] = m_in[0]
    acc_ref[...] = acc_in[0]


def prompt_kernel(
    places, groups, stacks, pat_ref, me_ref, head_ref, q_ref, m_in, acc_in, *refs
):
    blocks, weight, refs = refs[:stacks], refs[stacks], refs[stacks + 1 :]
    outs = refs[: len(groups)]
    qs, m_ref, acc_ref, kv, picked, att, w_s, o_s, sems, w_sems, o_sems = refs[len(groups) :]
    i = pl.program_id(0)
    count = len(places) // stacks
    copies = [
        pltpu.make_async_copy(ref, kv.at[pl.ds(k * count, count)], sems.at[k])
        for k, ref in enumerate(blocks)
    ]
    chunks = [(k, j, place) for k, group in enumerate(groups) for j, place in enumerate(group)]
    each = len(chunks) // QBLOCKS

    def weight_copy(n):
        return pltpu.make_async_copy(
            weight.at[:, chunk_at(head_ref, chunks[n][2])], w_s.at[n], w_sems.at[n]
        )

    def out_copy(n):
        k, j, _ = chunks[n]
        return pltpu.make_async_copy(o_s.at[n], outs[k].at[j], o_sems.at[n])

    @pl.when(i == 0)
    def _():
        for copy in copies:
            copy.start()

    load_state(q_ref, m_in, acc_in, qs, m_ref, acc_ref)

    @pl.when(i == 0)
    def _():
        for copy in copies:
            copy.wait()

    for step in range(QBLOCKS):

        @pl.when(i == step)
        def _(step=step):
            for n in range(step * each, (step + 1) * each):
                weight_copy(n).start()

    attend_active(places, pat_ref, me_ref, picked, kv, qs, m_ref, acc_ref)
    done = (acc_ref[:, :HD] / acc_ref[:, HD:]).astype(jnp.bfloat16)
    for g in range(GROUP):
        for s in range(STEPS):
            at = (g * STEPS + s) * QP
            row = pl.multiple_of(s * PROBS + i * QP, QP)
            att[pl.ds(row, QP), g * HD : (g + 1) * HD] = done[at : at + QP]

    @pl.when(i == QBLOCKS - 1)
    def _():
        for n in range(len(chunks)):
            weight_copy(n).wait()
            o_s[n] = dot(att[...], w_s[n]).astype(jnp.bfloat16)
            out_copy(n).start()
        for n in range(len(chunks)):
            out_copy(n).wait()


def prompt_part(pattern, me, head, places, groups, query, top, accum, stacks, weight):
    wide = GROUP * HD
    three = pl.BlockSpec((STEPS, QP, wide), lambda i, *_: (0, i, 0))
    state = lambda width: pl.BlockSpec((1, TILE, width), lambda i, *_: (i, 0, 0))
    anywhere = pl.BlockSpec(memory_space=pl.ANY)
    rows = STEPS * PROBS
    depth = weight.shape[0]
    chunks = sum(len(group) for group in groups)
    return pl.pallas_call(
        functools.partial(prompt_kernel, places, groups, len(stacks)),
        grid_spec=pltpu.PrefetchScalarGridSpec(
            num_scalar_prefetch=3,
            grid=(QBLOCKS,),
            in_specs=[three, state(HD), state(2 * HD)] + [anywhere] * (len(stacks) + 1),
            out_specs=[anywhere] * len(groups),
            scratch_shapes=[
                pltpu.VMEM((TILE, 2 * HD), jnp.bfloat16),
                pltpu.VMEM((TILE, HD), jnp.float32),
                pltpu.VMEM((TILE, 2 * HD), jnp.float32),
                pltpu.VMEM((len(places), 2 * P_DEV, HD), jnp.bfloat16),
                pltpu.SMEM((len(places) + 4,), jnp.int32),
                pltpu.VMEM((rows, wide), jnp.bfloat16),
                pltpu.VMEM((chunks, depth, CHUNK), jnp.bfloat16),
                pltpu.VMEM((chunks, rows, CHUNK), jnp.bfloat16),
                pltpu.SemaphoreType.DMA((len(stacks),)),
                pltpu.SemaphoreType.DMA((chunks,)),
                pltpu.SemaphoreType.DMA((chunks,)),
            ],
        ),
        out_shape=[
            jax.ShapeDtypeStruct((len(group), rows, CHUNK), jnp.bfloat16) for group in groups
        ],
        compiler_params=params(),
        cost_estimate=LIGHT,
    )(pattern, me, head, query, top, accum, *stacks, weight)


def flip(r):
    return (0x36 >> (2 * r)) & 3


def column(head, base, far, r):
    return base + (((head // 4) ^ far) * 4) + ((head & 3) ^ flip(r))


def chunk_at(head_ref, place):
    return pl.ds(pl.multiple_of(column(head_ref[0], *place) * CHUNK, CHUNK), CHUNK)


def assemble_kernel(places, head_ref, *refs):
    for ref, group in zip(refs[:-1], places):
        for j, place in enumerate(group):
            refs[-1][:, chunk_at(head_ref, place)] = ref[j]


def assemble(head, places, sources):
    rows = sources[0].shape[1]
    whole = lambda value: pl.BlockSpec(value.shape, lambda i, head: (0, 0, 0))
    return pl.pallas_call(
        functools.partial(assemble_kernel, places),
        grid_spec=pltpu.PrefetchScalarGridSpec(
            num_scalar_prefetch=1,
            grid=(1,),
            in_specs=[whole(value) for value in sources],
            out_specs=pl.BlockSpec((rows, 16 * CHUNK), lambda i, head: (0, 0)),
        ),
        out_shape=jax.ShapeDtypeStruct((rows, 16 * CHUNK), jnp.bfloat16),
        compiler_params=params(),
        cost_estimate=LIGHT,
    )(head, *sources)


def complete_kernel(places, head_ref, earlier, *refs):
    sources, out, sems = refs[:-2], refs[-2], refs[-1]
    copies = []
    for ref, group in zip(sources, places):
        for j, place in enumerate(group):
            copies.append(
                pltpu.make_async_copy(
                    ref.at[j], out.at[:, chunk_at(head_ref, place)], sems.at[len(copies)]
                )
            )
    for copy in copies:
        copy.start()
    for copy in copies:
        copy.wait()


def complete(head, places, earlier, sources):
    anywhere = pl.BlockSpec(memory_space=pl.ANY)
    return pl.pallas_call(
        functools.partial(complete_kernel, places),
        grid_spec=pltpu.PrefetchScalarGridSpec(
            num_scalar_prefetch=1,
            grid=(1,),
            in_specs=[anywhere]
            + [pl.BlockSpec(value.shape, lambda i, head: (0, 0, 0)) for value in sources],
            out_specs=anywhere,
            scratch_shapes=[pltpu.SemaphoreType.DMA((sum(len(g) for g in places),))],
        ),
        out_shape=jax.ShapeDtypeStruct(earlier.shape, earlier.dtype),
        input_output_aliases={1: 0},
        compiler_params=params(),
        cost_estimate=LIGHT,
    )(head, earlier, *sources)


def join_kernel(first_ref, begin_ref, len_ref, source, keys_out, vals_out):
    problem = first_ref[0] + pl.program_id(0)
    total = BRANCHES * SPAN
    flat = source[:, 0].reshape(total, 2 * HD)
    lane = lax.broadcasted_iota(jnp.int32, (1, total), 1)
    target = jnp.full((1, total), -1, jnp.int32)
    for b in range(BRANCHES):
        live = (lane >= b * SPAN) & (lane < b * SPAN + len_ref[b, problem])
        begin = begin_ref[b, problem] - P_DEV * BRANCHES - b * SPAN
        target = jnp.where(live, lane + begin, target)
    rows = 256
    for r0 in range(0, total, rows):
        slot = lax.broadcasted_iota(jnp.int32, (rows, 1), 0) + r0
        pick = jnp.where(target == slot, 1.0, 0.0).astype(jnp.bfloat16)
        got = jnp.dot(pick, flat, preferred_element_type=jnp.float32).astype(jnp.bfloat16)
        keys_out[0, r0 : r0 + rows, :] = got[:, :HD]
        vals_out[0, r0 : r0 + rows, :] = got[:, HD:]


def join(first, begins, lengths, source):
    share = source.shape[1]
    total = BRANCHES * SPAN
    out = pl.BlockSpec((1, total, HD), lambda i, *_: (i, 0, 0))
    shape = jax.ShapeDtypeStruct((share, total, HD), jnp.bfloat16)
    return pl.pallas_call(
        join_kernel,
        grid_spec=pltpu.PrefetchScalarGridSpec(
            num_scalar_prefetch=3,
            grid=(share,),
            in_specs=[pl.BlockSpec((BRANCHES, 1, SPAN, 2 * HD), lambda i, *_: (0, i, 0, 0))],
            out_specs=[out, out],
        ),
        out_shape=[shape, shape],
        compiler_params=params(),
        cost_estimate=LIGHT,
    )(first, begins, lengths, source)


def chip_of(branch, dz, dy):
    return ((branch // 8) ^ dz) * 8 + ((branch // 2 + dy) % 4) * 2


def move_chip(value, dz, dy):
    perm = [(b, chip_of(b, dz, dy) + b % 2) for b in range(BRANCHES)]
    return lax.ppermute(value, "branch", perm)


def swap_core(value):
    return lax.ppermute(value, "branch", [(b, b ^ 1) for b in range(BRANCHES)])


def move_x(value, flip):
    return lax.ppermute(value, "head", [(h, h ^ flip) for h in range(KVH)])


def move_roles(o, p, q):
    return move_x(p, 1), move_x(q, 3), move_x(o, 2)


def add(*values):
    total = values[0].astype(jnp.float32)
    for value in values[1:]:
        total = total + value.astype(jnp.float32)
    return total.astype(jnp.bfloat16)


def after(value, *others):
    return lax.optimization_barrier((value, others))[0]


def shards(
    queries, new_keys, new_values, prompt_keys, prompt_values, span_keys, span_values,
    span_lengths, join_offsets, pattern, out_weight,
):
    me = lax.axis_index("branch")
    one = me.reshape(1)
    head = lax.axis_index("head").reshape(1)
    prompt_len = P_DEV * BRANCHES
    share = PROBS // BRANCHES

    own = pack_block(prompt_keys, prompt_values)
    above = move_chip(own, 1, 0)
    near = [own, above, move_chip(own, 0, 1), move_chip(own, 0, 3)]
    near_at = [(0, 0), (1, 0), (0, 1), (0, 3)]
    across = move_chip(own, 0, 2)
    far_at = [(0, 2), (1, 1), (1, 3), (1, 2)]

    lengths = span_lengths.T
    offsets = join_offsets.T
    live = lax.dynamic_slice_in_dim(lengths, me, 1, 0)
    shift = lax.dynamic_slice_in_dim(offsets, me, 1, 0) - prompt_len
    steps = jnp.arange(STEPS, dtype=jnp.int32)[:, None]
    cosine, sine = tables(jnp.concatenate([prompt_len + live + steps, shift]))
    near = after(near, cosine)
    near_stack = jnp.stack(near)
    near_other = swap_core(near_stack)
    far = [across] + [move_chip(near[1], 0, dy) for dy in (1, 3, 2)]
    query, top, accum, sent = span_part(
        lengths,
        one,
        after(jnp.transpose(queries[0], (1, 0, 2)), near_stack),
        cosine,
        sine,
        jnp.transpose(new_keys[0], (1, 0, 2)),
        jnp.transpose(new_values[0], (1, 0, 2)),
        span_keys[0],
        span_values[0],
    )

    far_stack = jnp.stack(after(far, query, near_other))
    far_other = swap_core(far_stack)
    sent = after(sent, far_stack).reshape(BRANCHES, share, SPAN, 2 * HD)
    gathered = lax.all_to_all(sent, "branch", 0, 0, tiled=True)
    places = [(dz, dy, c) for at in (near_at, far_at) for c in (0, 1) for dz, dy in at]
    stacks = [near_stack, near_other, far_stack, far_other]

    half = 8
    roles = range(4)
    groups = [[(half, 1, r) for r in roles]]
    groups += [[(0, far, r) for far in (1, 0)] for r in roles]
    groups += [[(half, 0, r) for r in roles]]
    zsend, xo, xp, xq, xx, zkeep = prompt_part(
        pattern[0], one, head, places, groups, query, top, accum, stacks, out_weight
    )
    got_z = move_x(zsend, 4)
    got_x = move_roles(xo, xp, xq)
    got_x = after(got_x, got_z, gathered)
    xsend = add(xx[0], *[got[0] for got in got_x])
    got_x_z = move_x(xsend, 4)
    got_z = after(got_z, xsend)
    zo, zp, zq, zx = [add(zkeep[r], got_z[r]) for r in range(4)]
    zsum = add(zx, *move_roles(zo, zp, zq))
    xsum = add(xx[1], *[got[1] for got in got_x], got_x_z)

    zsum = after(zsum, xsum)
    zp, zq, zo = move_roles(zsum, zsum, zsum)
    pair = jnp.stack([move_x(xsum, 4), xsum])
    xp, xq, xo = move_roles(pair, pair, pair)
    zfour = jnp.stack(after([zo, zp, zq, zsum], pair))
    zother = move_x(zfour, 4)
    joined_keys, joined_values = join(
        (me * share).reshape(1), offsets, lengths, after(gathered, zfour)
    )
    both = [[(0, far, r) for far in (1, 0)] for r in roles]
    mixed = assemble(head, [both[3], [(half, 0, r) for r in roles]], after([pair, zfour], joined_keys))
    mixed = complete(
        head, [[(half, 1, r) for r in roles]] + both[:3], mixed, [zother, xo, xp, xq]
    )
    mixed = jnp.transpose(mixed.reshape(STEPS, PROBS, 16 * CHUNK), (1, 0, 2))[None]
    return mixed, joined_keys, joined_values


def solution(mesh):
    return jax.shard_map(
        shards,
        mesh=mesh,
        in_specs=(
            P("branch", None, None, "head"),
            P("branch", None, None, "head"),
            P("branch", None, None, "head"),
            P("branch", "head"),
            P("branch", "head"),
            P("branch", None, None, "head"),
            P("branch", None, None, "head"),
            P(),
            P(),
            P("branch", None, None),
            P("head", None),
        ),
        out_specs=(
            P("branch", None, None, None),
            P("branch", None, "head"),
            P("branch", None, "head"),
        ),
        check_vma=False,
    )
```

```python
import functools
import math

import jax
import jax.numpy as jnp
import numpy as np
from jax import lax
from jax.experimental import pallas as pl
from jax.experimental.pallas import tpu as pltpu
from jax.sharding import PartitionSpec as P

HEADS = 64
KVH = 8
HD = 128
GROUP = HEADS // KVH
STEPS = 3
SPAN = 64
BRANCHES = 16
QBLOCKS = 4
PROBS = 64
QP = PROBS // QBLOCKS
PIECES = STEPS * GROUP
TILE = PIECES * QP
P_DEV = 512
CHUNK = 512

rope_base = 500000.0
masked_score = -1e30
SCALE2 = math.log2(math.e) / math.sqrt(HD)
VMEM = 60 * 1024 * 1024
LIGHT = pl.CostEstimate(flops=0, bytes_accessed=0, transcendentals=0)


def params(grid_rank=1):
    return pltpu.CompilerParams(
        dimension_semantics=("arbitrary",) * grid_rank, vmem_limit_bytes=VMEM
    )


def tables(position):
    half = HD // 2
    exponent = np.arange(half) * (2.0 / HD)
    frequency = np.tile(np.exp(-math.log(rope_base) * exponent), 2).astype(np.float32)
    sign = np.repeat(np.float32([-1.0, 1.0]), half)
    angle = position.astype(jnp.float32)[..., None] * frequency
    return jnp.cos(angle), jnp.sin(angle) * sign


def turn(values, cosine, sine):
    return values * cosine + pltpu.roll(values, HD // 2, values.ndim - 1) * sine


def with_ones(values):
    return jnp.concatenate([values, jnp.ones_like(values)], 1)


def dot(a, b):
    return jnp.dot(a, b, preferred_element_type=jnp.float32)


def span_kernel(
    len_ref, me_ref, q_ref, cos_ref, sin_ref, nk_ref, nv_ref, sk_ref, sv_ref,
    q_out, m_out, acc_out, sent_out,
):
    first = pl.program_id(0) * QP
    lane = lax.broadcasted_iota(jnp.int32, (1, QP * SPAN), 1)
    code = jnp.full((1, QP * SPAN), -1, jnp.int32)
    for p in range(QP):
        live = len_ref[me_ref[0], first + p]
        code = jnp.where((lane >= p * SPAN) & (lane < p * SPAN + live), p, code)
    rotated = {}
    for g in range(GROUP):
        for s in range(STEPS):
            lanes = slice(g * HD, (g + 1) * HD)
            raw = q_ref[s, :, lanes].astype(jnp.float32)
            rotated[g, s] = turn(raw, cos_ref[s], sin_ref[s])
            q_out[s, :, lanes] = rotated[g, s].astype(jnp.bfloat16)
    fresh = [
        turn(nk_ref[s].astype(jnp.float32), cos_ref[s], sin_ref[s]).astype(jnp.bfloat16)
        for s in range(STEPS)
    ]
    pad = jnp.zeros((HD - STEPS * QP, HD), jnp.bfloat16)
    fresh_keys = jnp.concatenate(fresh + [pad], 0).T
    fresh_vals = with_ones(jnp.concatenate([nv_ref[s] for s in range(STEPS)] + [pad], 0))
    few = QP // 2
    rows = few * PIECES
    keys_of = few * SPAN
    row = lax.broadcasted_iota(jnp.int32, (rows, 1), 0)
    piece = row >> 3
    step = piece - 3 * ((piece * 22) >> 6)
    fresh_lane = lax.broadcasted_iota(jnp.int32, (1, HD), 1)
    for part in range(2):
        low = part * few
        prob = (row & (few - 1)) + low
        q = jnp.concatenate(
            [rotated[g, s][low : low + few] for g in range(GROUP) for s in range(STEPS)], 0
        ).astype(jnp.bfloat16)
        span_keys = sk_ref[low : low + few].reshape(keys_of, HD).T
        span_vals = with_ones(sv_ref[low : low + few].reshape(keys_of, HD))
        s1 = jnp.where(
            code[:, part * keys_of : (part + 1) * keys_of] == prob, dot(q, span_keys), masked_score
        )
        ok = ((fresh_lane & (QP - 1)) == prob) & ((fresh_lane >> 4) <= step)
        s2 = jnp.where(ok, dot(q, fresh_keys), masked_score)
        top = jnp.maximum(s1.max(1, keepdims=True), s2.max(1, keepdims=True)) * SCALE2
        p1 = jnp.exp2(s1 * SCALE2 - top).astype(jnp.bfloat16)
        p2 = jnp.exp2(s2 * SCALE2 - top).astype(jnp.bfloat16)
        total = dot(p1, span_vals) + dot(p2, fresh_vals)
        wide = jnp.broadcast_to(top, (rows, HD))
        for k in range(PIECES):
            m_out[0, k * QP + low : k * QP + low + few, :] = wide[k * few : (k + 1) * few]
            acc_out[0, k * QP + low : k * QP + low + few, :] = total[k * few : (k + 1) * few]
    keys = sk_ref[...].astype(jnp.float32)
    kcos = cos_ref[STEPS][:, None, :]
    ksin = sin_ref[STEPS][:, None, :]
    sent_out[:, :, :HD] = turn(keys, kcos, ksin).astype(jnp.bfloat16)
    sent_out[:, :, HD:] = sv_ref[...]


def span_part(
    lengths, me, queries, cosine, sine, new_keys, new_values, span_keys, span_values
):
    three = lambda width: pl.BlockSpec((STEPS, QP, width), lambda i, *_: (0, i, 0))
    span = lambda width: pl.BlockSpec((QP, SPAN, width), lambda i, *_: (i, 0, 0))
    table = pl.BlockSpec((STEPS + 1, QP, HD), lambda i, *_: (0, i, 0))
    state = lambda width: pl.BlockSpec((1, TILE, width), lambda i, *_: (i, 0, 0))
    wide = GROUP * HD
    return pl.pallas_call(
        span_kernel,
        grid_spec=pltpu.PrefetchScalarGridSpec(
            num_scalar_prefetch=2,
            grid=(QBLOCKS,),
            in_specs=[
                three(wide), table, table, three(HD), three(HD), span(HD), span(HD),
            ],
            out_specs=[three(wide), state(HD), state(2 * HD), span(2 * HD)],
        ),
        out_shape=[
            jax.ShapeDtypeStruct((STEPS, PROBS, wide), jnp.bfloat16),
            jax.ShapeDtypeStruct((QBLOCKS, TILE, HD), jnp.float32),
            jax.ShapeDtypeStruct((QBLOCKS, TILE, 2 * HD), jnp.float32),
            jax.ShapeDtypeStruct((PROBS, SPAN, 2 * HD), jnp.bfloat16),
        ],
        compiler_params=params(),
        cost_estimate=LIGHT,
    )(lengths, me, queries, cosine, sine, new_keys, new_values, span_keys, span_values)


def pack_kernel(keys_ref, vals_ref, out):
    for c in range(0, P_DEV, HD):
        out[c : c + HD, :] = keys_ref[c : c + HD, :].T
    out[P_DEV:, :] = vals_ref[...]


def pack_block(keys, vals):
    return pl.pallas_call(
        pack_kernel,
        out_shape=jax.ShapeDtypeStruct((2 * P_DEV, HD), jnp.bfloat16),
        compiler_params=pltpu.CompilerParams(vmem_limit_bytes=VMEM),
        cost_estimate=LIGHT,
    )(keys, vals)


def attend(picks, valid, kv, qs, m_ref, acc_ref):
    rows = 128
    keys = []
    vals = []
    for k in picks:
        flat = jnp.concatenate([kv[k, c : c + HD, :] for c in range(0, P_DEV, HD)], 1)
        keys.append(jnp.concatenate([flat, flat], 0))
        vals.append(with_ones(kv[k, P_DEV:, :]))
    for r0 in range(0, TILE, rows):
        at = slice(r0, r0 + rows)
        query = qs[at, :]
        old = m_ref[at, :]
        scores = [jnp.dot(query, key, preferred_element_type=jnp.float32) for key in keys]
        top = old
        for value, ok in zip(scores, valid):
            best = value.max(1, keepdims=True)
            top = jnp.maximum(top, best if ok is None else jnp.where(ok, best, masked_score))
        factor = jnp.exp2(old - top)
        total = acc_ref[at, :] * jnp.concatenate([factor, factor], 1)
        for value, val, ok in zip(scores, vals, valid):
            base = top if ok is None else jnp.where(ok, top, -masked_score)
            weights = jnp.concatenate(
                [
                    jnp.exp2(value[:, c : c + HD] - base).astype(jnp.bfloat16)
                    for c in range(0, P_DEV, HD)
                ],
                1,
            )
            total = total + jnp.dot(weights, val, preferred_element_type=jnp.float32)
        m_ref[at, :] = top
        acc_ref[at, :] = total


def attend_active(places, pat_ref, me_ref, picked, kv, qs, m_ref, acc_ref):
    i = pl.program_id(0)
    me = me_ref[0]
    for k in range(len(places) + 4):
        picked[k] = 0
    count = jnp.int32(0)
    for k, (dz, dy, other) in enumerate(places):
        picked[count] = k
        owner = chip_of(me, dz, -dy) + ((me & 1) ^ other)
        count = count + jnp.where(pat_ref[i, owner] > 0, 1, 0)
    fours = (count + 1) // 4

    def four(t, carry):
        base = 4 * t
        attend(
            [picked[base + k] for k in range(4)],
            [None, None, None, base + 3 < count],
            kv, qs, m_ref, acc_ref,
        )
        return carry

    lax.fori_loop(0, fours, four, 0)

    @pl.when(4 * fours < count)
    def _():
        base = 4 * fours
        attend(
            [picked[base], picked[base + 1]], [None, base + 1 < count], kv, qs, m_ref, acc_ref
        )


def load_state(q_ref, m_in, acc_in, qs, m_ref, acc_ref):
    for g in range(GROUP):
        for s in range(STEPS):
            at = (g * STEPS + s) * QP
            scaled = q_ref[s, :, g * HD : (g + 1) * HD].astype(jnp.float32) * SCALE2
            high = scaled.astype(jnp.bfloat16)
            qs[at : at + QP, :HD] = high
            qs[at : at + QP, HD:] = (scaled - high.astype(jnp.float32)).astype(jnp.bfloat16)
    m_ref[...] = m_in[0]
    acc_ref[...] = acc_in[0]


def prompt_kernel(
    places, groups, stacks, pat_ref, me_ref, head_ref, q_ref, m_in, acc_in, *refs
):
    blocks, weight, refs = refs[:stacks], refs[stacks], refs[stacks + 1 :]
    outs, att = refs[: len(groups)], refs[len(groups)]
    qs, m_ref, acc_ref, kv, picked, w_s, o_s, sems, w_sems, o_sems = refs[len(groups) + 1 :]
    i = pl.program_id(0)
    sizes = [ref.shape[0] for ref in blocks]
    copies = [
        pltpu.make_async_copy(ref, kv.at[pl.ds(sum(sizes[:k]), sizes[k])], sems.at[k])
        for k, ref in enumerate(blocks)
    ]
    chunks = [(k, j, place) for k, group in enumerate(groups) for j, place in enumerate(group)]
    each = -(-len(chunks) // QBLOCKS)

    def weight_copy(n):
        return pltpu.make_async_copy(
            weight.at[:, chunk_at(head_ref, chunks[n][2])], w_s.at[n], w_sems.at[n]
        )

    def out_copy(n):
        k, j, _ = chunks[n]
        return pltpu.make_async_copy(o_s.at[n], outs[k].at[j], o_sems.at[n])

    @pl.when(i == 0)
    def _():
        for copy in copies:
            copy.start()

    load_state(q_ref, m_in, acc_in, qs, m_ref, acc_ref)

    @pl.when(i == 0)
    def _():
        for copy in copies:
            copy.wait()

    for step in range(QBLOCKS):

        @pl.when(i == step)
        def _(step=step):
            for n in range(step * each, min((step + 1) * each, len(chunks))):
                weight_copy(n).start()

    attend_active(places, pat_ref, me_ref, picked, kv, qs, m_ref, acc_ref)
    done = (acc_ref[:, :HD] / acc_ref[:, HD:]).astype(jnp.bfloat16)
    for g in range(GROUP):
        for s in range(STEPS):
            at = (g * STEPS + s) * QP
            row = pl.multiple_of(s * PROBS + i * QP, QP)
            att[pl.ds(row, QP), g * HD : (g + 1) * HD] = done[at : at + QP]

    @pl.when(i == QBLOCKS - 1)
    def _():
        for n in range(len(chunks)):
            weight_copy(n).wait()
            o_s[n] = dot(att[...], w_s[n]).astype(jnp.bfloat16)
            out_copy(n).start()
        for n in range(len(chunks)):
            out_copy(n).wait()


def prompt_part(pattern, me, head, places, groups, query, top, accum, stacks, weight):
    wide = GROUP * HD
    three = pl.BlockSpec((STEPS, QP, wide), lambda i, *_: (0, i, 0))
    state = lambda width: pl.BlockSpec((1, TILE, width), lambda i, *_: (i, 0, 0))
    anywhere = pl.BlockSpec(memory_space=pl.ANY)
    rows = STEPS * PROBS
    depth = weight.shape[0]
    chunks = sum(len(group) for group in groups)
    return pl.pallas_call(
        functools.partial(prompt_kernel, places, groups, len(stacks)),
        grid_spec=pltpu.PrefetchScalarGridSpec(
            num_scalar_prefetch=3,
            grid=(QBLOCKS,),
            in_specs=[three, state(HD), state(2 * HD)] + [anywhere] * (len(stacks) + 1),
            out_specs=[anywhere] * len(groups) + [pl.BlockSpec((rows, wide), lambda i, *_: (0, 0))],
            scratch_shapes=[
                pltpu.VMEM((TILE, 2 * HD), jnp.bfloat16),
                pltpu.VMEM((TILE, HD), jnp.float32),
                pltpu.VMEM((TILE, 2 * HD), jnp.float32),
                pltpu.VMEM((len(places), 2 * P_DEV, HD), jnp.bfloat16),
                pltpu.SMEM((len(places) + 4,), jnp.int32),
                pltpu.VMEM((chunks, depth, CHUNK), jnp.bfloat16),
                pltpu.VMEM((chunks, rows, CHUNK), jnp.bfloat16),
                pltpu.SemaphoreType.DMA((len(stacks),)),
                pltpu.SemaphoreType.DMA((chunks,)),
                pltpu.SemaphoreType.DMA((chunks,)),
            ],
        ),
        out_shape=[
            jax.ShapeDtypeStruct((len(group), rows, CHUNK), jnp.bfloat16) for group in groups
        ]
        + [jax.ShapeDtypeStruct((rows, wide), jnp.bfloat16)],
        compiler_params=params(),
        cost_estimate=LIGHT,
    )(pattern, me, head, query, top, accum, *stacks, weight)


def flip(r):
    return (0x36 >> (2 * r)) & 3


def column(head, base, far, r):
    return base + (((head // 4) ^ far) * 4) + ((head & 3) ^ flip(r))


def project_kernel(places, head_ref, a_ref, w_ref, out):
    out[0] = dot(a_ref[...], w_ref[...]).astype(jnp.bfloat16)


def project(attended, weight, head, places):
    rows, depth = attended.shape

    def chunk(i, head):
        found = jnp.int32(0)
        for k, place in enumerate(places):
            found = jnp.where(i == k, column(head[0], *place), found)
        return (0, found)

    return pl.pallas_call(
        functools.partial(project_kernel, places),
        grid_spec=pltpu.PrefetchScalarGridSpec(
            num_scalar_prefetch=1,
            grid=(len(places),),
            in_specs=[
                pl.BlockSpec((rows, depth), lambda i, head: (0, 0)),
                pl.BlockSpec((depth, CHUNK), chunk),
            ],
            out_specs=pl.BlockSpec((1, rows, CHUNK), lambda i, head: (i, 0, 0)),
        ),
        out_shape=jax.ShapeDtypeStruct((len(places), rows, CHUNK), jnp.bfloat16),
        compiler_params=params(),
        cost_estimate=LIGHT,
    )(head, attended, weight)


def chunk_at(head_ref, place):
    return pl.ds(pl.multiple_of(column(head_ref[0], *place) * CHUNK, CHUNK), CHUNK)


def assemble_kernel(places, head_ref, *refs):
    for ref, group in zip(refs[:-1], places):
        for j, place in enumerate(group):
            refs[-1][:, chunk_at(head_ref, place)] = ref[j]


def assemble(head, places, sources):
    rows = sources[0].shape[1]
    whole = lambda value: pl.BlockSpec(value.shape, lambda i, head: (0, 0, 0))
    return pl.pallas_call(
        functools.partial(assemble_kernel, places),
        grid_spec=pltpu.PrefetchScalarGridSpec(
            num_scalar_prefetch=1,
            grid=(1,),
            in_specs=[whole(value) for value in sources],
            out_specs=pl.BlockSpec((rows, 16 * CHUNK), lambda i, head: (0, 0)),
        ),
        out_shape=jax.ShapeDtypeStruct((rows, 16 * CHUNK), jnp.bfloat16),
        compiler_params=params(),
        cost_estimate=LIGHT,
    )(head, *sources)


def complete_kernel(places, head_ref, earlier, *refs):
    sources, out, sems = refs[:-2], refs[-2], refs[-1]
    copies = []
    for ref, group in zip(sources, places):
        for j, place in enumerate(group):
            copies.append(
                pltpu.make_async_copy(
                    ref.at[j], out.at[:, chunk_at(head_ref, place)], sems.at[len(copies)]
                )
            )
    for copy in copies:
        copy.start()
    for copy in copies:
        copy.wait()


def complete(head, places, earlier, sources):
    anywhere = pl.BlockSpec(memory_space=pl.ANY)
    return pl.pallas_call(
        functools.partial(complete_kernel, places),
        grid_spec=pltpu.PrefetchScalarGridSpec(
            num_scalar_prefetch=1,
            grid=(1,),
            in_specs=[anywhere]
            + [pl.BlockSpec(value.shape, lambda i, head: (0, 0, 0)) for value in sources],
            out_specs=anywhere,
            scratch_shapes=[pltpu.SemaphoreType.DMA((sum(len(g) for g in places),))],
        ),
        out_shape=jax.ShapeDtypeStruct(earlier.shape, earlier.dtype),
        input_output_aliases={1: 0},
        compiler_params=params(),
        cost_estimate=LIGHT,
    )(head, earlier, *sources)


def join_kernel(first_ref, begin_ref, len_ref, source, keys_out, vals_out):
    problem = first_ref[0] + pl.program_id(0)
    total = BRANCHES * SPAN
    flat = source[:, 0].reshape(total, 2 * HD)
    lane = lax.broadcasted_iota(jnp.int32, (1, total), 1)
    target = jnp.full((1, total), -1, jnp.int32)
    for b in range(BRANCHES):
        live = (lane >= b * SPAN) & (lane < b * SPAN + len_ref[b, problem])
        begin = begin_ref[b, problem] - P_DEV * BRANCHES - b * SPAN
        target = jnp.where(live, lane + begin, target)
    rows = 256
    for r0 in range(0, total, rows):
        slot = lax.broadcasted_iota(jnp.int32, (rows, 1), 0) + r0
        pick = jnp.where(target == slot, 1.0, 0.0).astype(jnp.bfloat16)
        got = jnp.dot(pick, flat, preferred_element_type=jnp.float32).astype(jnp.bfloat16)
        keys_out[0, r0 : r0 + rows, :] = got[:, :HD]
        vals_out[0, r0 : r0 + rows, :] = got[:, HD:]


def join(first, begins, lengths, source):
    share = source.shape[1]
    total = BRANCHES * SPAN
    out = pl.BlockSpec((1, total, HD), lambda i, *_: (i, 0, 0))
    shape = jax.ShapeDtypeStruct((share, total, HD), jnp.bfloat16)
    return pl.pallas_call(
        join_kernel,
        grid_spec=pltpu.PrefetchScalarGridSpec(
            num_scalar_prefetch=3,
            grid=(share,),
            in_specs=[pl.BlockSpec((BRANCHES, 1, SPAN, 2 * HD), lambda i, *_: (0, i, 0, 0))],
            out_specs=[out, out],
        ),
        out_shape=[shape, shape],
        compiler_params=params(),
        cost_estimate=LIGHT,
    )(first, begins, lengths, source)


def chip_of(branch, dz, dy):
    return ((branch // 8) ^ dz) * 8 + ((branch // 2 + dy) % 4) * 2


def move_chip(value, dz, dy):
    perm = [(b, chip_of(b, dz, dy) + b % 2) for b in range(BRANCHES)]
    return lax.ppermute(value, "branch", perm)


def swap_core(value):
    return lax.ppermute(value, "branch", [(b, b ^ 1) for b in range(BRANCHES)])


def move_x(value, flip):
    return lax.ppermute(value, "head", [(h, h ^ flip) for h in range(KVH)])


def move_roles(o, p, q):
    return move_x(p, 1), move_x(q, 3), move_x(o, 2)


def add(*values):
    total = values[0].astype(jnp.float32)
    for value in values[1:]:
        total = total + value.astype(jnp.float32)
    return total.astype(jnp.bfloat16)


def after(value, *others):
    return lax.optimization_barrier((value, others))[0]


def shards(
    queries, new_keys, new_values, prompt_keys, prompt_values, span_keys, span_values,
    span_lengths, join_offsets, pattern, out_weight,
):
    me = lax.axis_index("branch")
    one = me.reshape(1)
    head = lax.axis_index("head").reshape(1)
    prompt_len = P_DEV * BRANCHES
    share = PROBS // BRANCHES

    own = pack_block(prompt_keys, prompt_values)
    near_at = [(0, 0), (1, 0), (0, 1), (0, 3), (0, 2)]
    near = [own] + [move_chip(own, dz, dy) for dz, dy in near_at[1:]]
    far_at = [(1, 1), (1, 3), (1, 2)]

    lengths = span_lengths.T
    offsets = join_offsets.T
    live = lax.dynamic_slice_in_dim(lengths, me, 1, 0)
    shift = lax.dynamic_slice_in_dim(offsets, me, 1, 0) - prompt_len
    steps = jnp.arange(STEPS, dtype=jnp.int32)[:, None]
    cosine, sine = tables(jnp.concatenate([prompt_len + live + steps, shift]))
    near = after(near, cosine)
    near_stack = jnp.stack(near)
    near_other = swap_core(near_stack)
    far = [move_chip(near[1], 0, 1), move_chip(near[1], 0, 3), move_chip(near[4], 1, 0)]
    query, top, accum, sent = span_part(
        lengths,
        one,
        after(jnp.transpose(queries[0], (1, 0, 2)), near_stack),
        cosine,
        sine,
        jnp.transpose(new_keys[0], (1, 0, 2)),
        jnp.transpose(new_values[0], (1, 0, 2)),
        span_keys[0],
        span_values[0],
    )

    far_stack = jnp.stack(after(far, query, near_other))
    far_other = swap_core(far_stack)
    sent = after(sent, far_stack).reshape(BRANCHES, share, SPAN, 2 * HD)
    gathered = lax.all_to_all(sent, "branch", 0, 0, tiled=True)
    places = [(dz, dy, c) for at in (near_at, far_at) for c in (0, 1) for dz, dy in at]
    stacks = [near_stack, near_other, far_stack, far_other]

    half = 8
    roles = range(4)
    both = [[(0, far, r) for far in (1, 0)] for r in roles]
    zhere = [(half, 0, r) for r in roles]
    zthere = [(half, 1, r) for r in roles]
    zsend, xo, xp, xq, attended = prompt_part(
        pattern[0], one, head, places, [zthere] + both[:3], query, top, accum, stacks, out_weight
    )
    got_z = move_x(zsend, 4)
    got_x = move_roles(xo, xp, xq)
    kept = project(attended, out_weight, head, zhere + both[3])
    got_z = after(got_z, got_x)
    zo, zp, zq, zx = [add(kept[r], got_z[r]) for r in range(4)]
    got_zx = move_roles(zo, zp, zq)
    got_x = after(got_x, zx, gathered)
    xsum = add(kept[4:], *got_x)
    zsum = add(zx, *after(got_zx, xsum))

    pair = add(xsum, move_x(xsum, 4)[::-1])
    zp, zq, zo = move_roles(zsum, zsum, zsum)
    xp, xq, xo = move_roles(pair, pair, pair)
    zfour = jnp.stack(after([zo, zp, zq, zsum], pair))
    zother = move_x(zfour, 4)
    joined_keys, joined_values = join(
        (me * share).reshape(1), offsets, lengths, after(gathered, zfour)
    )
    mixed = assemble(head, [both[3], zhere], after([pair, zfour], joined_keys))
    mixed = complete(head, [zthere] + both[:3], mixed, [zother, xo, xp, xq])
    mixed = jnp.transpose(mixed.reshape(STEPS, PROBS, 16 * CHUNK), (1, 0, 2))[None]
    return mixed, joined_keys, joined_values


def solution(mesh):
    return jax.shard_map(
        shards,
        mesh=mesh,
        in_specs=(
            P("branch", None, None, "head"),
            P("branch", None, None, "head"),
            P("branch", None, None, "head"),
            P("branch", "head"),
            P("branch", "head"),
            P("branch", None, None, "head"),
            P("branch", None, None, "head"),
            P(),
            P(),
            P("branch", None, None),
            P("head", None),
        ),
        out_specs=(
            P("branch", None, None, None),
            P("branch", None, "head"),
            P("branch", None, "head"),
        ),
        check_vma=False,
    )
```

```python
import functools
import math

import jax
import jax.numpy as jnp
import numpy as np
from jax import lax
from jax.experimental import pallas as pl
from jax.experimental.pallas import tpu as pltpu
from jax.sharding import PartitionSpec as P

HEADS = 64
KVH = 8
HD = 128
GROUP = HEADS // KVH
STEPS = 3
SPAN = 64
BRANCHES = 16
QBLOCKS = 4
PROBS = 64
QP = PROBS // QBLOCKS
PIECES = STEPS * GROUP
TILE = PIECES * QP
P_DEV = 512
CHUNK = 512

rope_base = 500000.0
masked_score = -1e30
SCALE2 = math.log2(math.e) / math.sqrt(HD)
VMEM = 60 * 1024 * 1024
PART = 46 * 1024 * 1024
LITTLE = 24 * 1024 * 1024
LIGHT = pl.CostEstimate(flops=0, bytes_accessed=0, transcendentals=0)


def params(limit=VMEM):
    return pltpu.CompilerParams(dimension_semantics=("arbitrary",), vmem_limit_bytes=limit)


def tables(position):
    half = HD // 2
    exponent = np.arange(half) * (2.0 / HD)
    frequency = np.tile(np.exp(-math.log(rope_base) * exponent), 2).astype(np.float32)
    sign = np.repeat(np.float32([-1.0, 1.0]), half)
    angle = position.astype(jnp.float32)[..., None] * frequency
    return jnp.cos(angle), jnp.sin(angle) * sign


def turn(values, cosine, sine):
    return values * cosine + pltpu.roll(values, HD // 2, values.ndim - 1) * sine


def with_ones(values):
    return jnp.concatenate([values, jnp.ones_like(values)], 1)


def dot(a, b):
    return jnp.dot(a, b, preferred_element_type=jnp.float32)


def span_kernel(
    len_ref, me_ref, q_ref, cos_ref, sin_ref, nk_ref, nv_ref, sk_ref, sv_ref,
    q_out, m_out, acc_out, sent_out,
):
    first = pl.program_id(0) * QP
    lane = lax.broadcasted_iota(jnp.int32, (1, QP * SPAN), 1)
    code = jnp.full((1, QP * SPAN), -1, jnp.int32)
    for p in range(QP):
        live = len_ref[me_ref[0], first + p]
        code = jnp.where((lane >= p * SPAN) & (lane < p * SPAN + live), p, code)
    rotated = {}
    for g in range(GROUP):
        for s in range(STEPS):
            lanes = slice(g * HD, (g + 1) * HD)
            raw = q_ref[s, :, lanes].astype(jnp.float32)
            rotated[g, s] = turn(raw, cos_ref[s], sin_ref[s])
            q_out[s, :, lanes] = rotated[g, s].astype(jnp.bfloat16)
    fresh = [
        turn(nk_ref[s].astype(jnp.float32), cos_ref[s], sin_ref[s]).astype(jnp.bfloat16)
        for s in range(STEPS)
    ]
    pad = jnp.zeros((HD - STEPS * QP, HD), jnp.bfloat16)
    fresh_keys = jnp.concatenate(fresh + [pad], 0).T
    fresh_vals = with_ones(jnp.concatenate([nv_ref[s] for s in range(STEPS)] + [pad], 0))
    few = QP // 2
    rows = few * PIECES
    keys_of = few * SPAN
    row = lax.broadcasted_iota(jnp.int32, (rows, 1), 0)
    piece = row >> 3
    step = piece - 3 * ((piece * 22) >> 6)
    fresh_lane = lax.broadcasted_iota(jnp.int32, (1, HD), 1)
    for part in range(2):
        low = part * few
        prob = (row & (few - 1)) + low
        q = jnp.concatenate(
            [rotated[g, s][low : low + few] for g in range(GROUP) for s in range(STEPS)], 0
        ).astype(jnp.bfloat16)
        span_keys = sk_ref[low : low + few].reshape(keys_of, HD).T
        span_vals = with_ones(sv_ref[low : low + few].reshape(keys_of, HD))
        s1 = jnp.where(
            code[:, part * keys_of : (part + 1) * keys_of] == prob, dot(q, span_keys), masked_score
        )
        ok = ((fresh_lane & (QP - 1)) == prob) & ((fresh_lane >> 4) <= step)
        s2 = jnp.where(ok, dot(q, fresh_keys), masked_score)
        top = jnp.maximum(s1.max(1, keepdims=True), s2.max(1, keepdims=True)) * SCALE2
        p1 = jnp.exp2(s1 * SCALE2 - top).astype(jnp.bfloat16)
        p2 = jnp.exp2(s2 * SCALE2 - top).astype(jnp.bfloat16)
        total = dot(p1, span_vals) + dot(p2, fresh_vals)
        wide = jnp.broadcast_to(top, (rows, HD))
        for k in range(PIECES):
            m_out[0, k * QP + low : k * QP + low + few, :] = wide[k * few : (k + 1) * few]
            acc_out[0, k * QP + low : k * QP + low + few, :] = total[k * few : (k + 1) * few]
    keys = sk_ref[...].astype(jnp.float32)
    kcos = cos_ref[STEPS][:, None, :]
    ksin = sin_ref[STEPS][:, None, :]
    sent_out[:, :, :HD] = turn(keys, kcos, ksin).astype(jnp.bfloat16)
    sent_out[:, :, HD:] = sv_ref[...]


def span_part(
    lengths, me, queries, cosine, sine, new_keys, new_values, span_keys, span_values
):
    three = lambda width: pl.BlockSpec((STEPS, QP, width), lambda i, *_: (0, i, 0))
    span = lambda width: pl.BlockSpec((QP, SPAN, width), lambda i, *_: (i, 0, 0))
    table = pl.BlockSpec((STEPS + 1, QP, HD), lambda i, *_: (0, i, 0))
    state = lambda width: pl.BlockSpec((1, TILE, width), lambda i, *_: (i, 0, 0))
    wide = GROUP * HD
    return pl.pallas_call(
        span_kernel,
        grid_spec=pltpu.PrefetchScalarGridSpec(
            num_scalar_prefetch=2,
            grid=(QBLOCKS,),
            in_specs=[
                three(wide), table, table, three(HD), three(HD), span(HD), span(HD),
            ],
            out_specs=[three(wide), state(HD), state(2 * HD), span(2 * HD)],
        ),
        out_shape=[
            jax.ShapeDtypeStruct((STEPS, PROBS, wide), jnp.bfloat16),
            jax.ShapeDtypeStruct((QBLOCKS, TILE, HD), jnp.float32),
            jax.ShapeDtypeStruct((QBLOCKS, TILE, 2 * HD), jnp.float32),
            jax.ShapeDtypeStruct((PROBS, SPAN, 2 * HD), jnp.bfloat16),
        ],
        compiler_params=params(),
        cost_estimate=LIGHT,
    )(lengths, me, queries, cosine, sine, new_keys, new_values, span_keys, span_values)


def pack_kernel(keys_ref, vals_ref, out):
    for c in range(0, P_DEV, HD):
        out[c : c + HD, :] = keys_ref[c : c + HD, :].T
    out[P_DEV:, :] = vals_ref[...]


def pack_block(keys, vals):
    return pl.pallas_call(
        pack_kernel,
        out_shape=jax.ShapeDtypeStruct((2 * P_DEV, HD), jnp.bfloat16),
        compiler_params=pltpu.CompilerParams(vmem_limit_bytes=VMEM),
        cost_estimate=LIGHT,
    )(keys, vals)


def attend(picks, valid, kv, qs, m_ref, acc_ref):
    rows = 128
    keys = []
    vals = []
    for k in picks:
        flat = jnp.concatenate([kv[k, c : c + HD, :] for c in range(0, P_DEV, HD)], 1)
        keys.append(jnp.concatenate([flat, flat], 0))
        vals.append(with_ones(kv[k, P_DEV:, :]))
    for r0 in range(0, TILE, rows):
        at = slice(r0, r0 + rows)
        query = qs[at, :]
        old = m_ref[at, :]
        scores = [jnp.dot(query, key, preferred_element_type=jnp.float32) for key in keys]
        top = old
        for value, ok in zip(scores, valid):
            best = value.max(1, keepdims=True)
            top = jnp.maximum(top, best if ok is None else jnp.where(ok, best, masked_score))
        factor = jnp.exp2(old - top)
        total = acc_ref[at, :] * jnp.concatenate([factor, factor], 1)
        for value, val, ok in zip(scores, vals, valid):
            base = top if ok is None else jnp.where(ok, top, -masked_score)
            weights = jnp.concatenate(
                [
                    jnp.exp2(value[:, c : c + HD] - base).astype(jnp.bfloat16)
                    for c in range(0, P_DEV, HD)
                ],
                1,
            )
            total = total + jnp.dot(weights, val, preferred_element_type=jnp.float32)
        m_ref[at, :] = top
        acc_ref[at, :] = total


def attend_active(places, pat_ref, me_ref, picked, kv, qs, m_ref, acc_ref):
    i = pl.program_id(0)
    me = me_ref[0]
    for k in range(len(places) + 4):
        picked[k] = 0
    count = jnp.int32(0)
    for k, (dz, dy, other) in enumerate(places):
        picked[count] = k
        owner = chip_of(me, dz, -dy) + ((me & 1) ^ other)
        count = count + jnp.where(pat_ref[i, owner] > 0, 1, 0)
    fours = (count + 1) // 4

    def four(t, carry):
        base = 4 * t
        attend(
            [picked[base + k] for k in range(4)],
            [None, None, None, base + 3 < count],
            kv, qs, m_ref, acc_ref,
        )
        return carry

    lax.fori_loop(0, fours, four, 0)

    @pl.when(4 * fours < count)
    def _():
        base = 4 * fours
        attend(
            [picked[base], picked[base + 1]], [None, base + 1 < count], kv, qs, m_ref, acc_ref
        )


def load_state(q_ref, m_in, acc_in, qs, m_ref, acc_ref):
    for g in range(GROUP):
        for s in range(STEPS):
            at = (g * STEPS + s) * QP
            scaled = q_ref[s, :, g * HD : (g + 1) * HD].astype(jnp.float32) * SCALE2
            high = scaled.astype(jnp.bfloat16)
            qs[at : at + QP, :HD] = high
            qs[at : at + QP, HD:] = (scaled - high.astype(jnp.float32)).astype(jnp.bfloat16)
    m_ref[...] = m_in[0]
    acc_ref[...] = acc_in[0]


def prompt_kernel(
    places, groups, stacks, pat_ref, me_ref, head_ref, q_ref, m_in, acc_in, *refs
):
    blocks, weight, refs = refs[:stacks], refs[stacks], refs[stacks + 1 :]
    outs, att = refs[: len(groups)], refs[len(groups)]
    qs, m_ref, acc_ref, kv, picked, w_s, o_s, sems, w_sems, o_sems = refs[len(groups) + 1 :]
    i = pl.program_id(0)
    sizes = [ref.shape[0] for ref in blocks]
    copies = [
        pltpu.make_async_copy(ref, kv.at[pl.ds(sum(sizes[:k]), sizes[k])], sems.at[k])
        for k, ref in enumerate(blocks)
    ]
    chunks = [(k, j, place) for k, group in enumerate(groups) for j, place in enumerate(group)]
    each = -(-len(chunks) // QBLOCKS)

    def weight_copy(n):
        return pltpu.make_async_copy(
            weight.at[:, chunk_at(head_ref, chunks[n][2])], w_s.at[n], w_sems.at[n]
        )

    def out_copy(n):
        k, j, _ = chunks[n]
        return pltpu.make_async_copy(o_s.at[n], outs[k].at[j], o_sems.at[n])

    @pl.when(i == 0)
    def _():
        for copy in copies:
            copy.start()

    load_state(q_ref, m_in, acc_in, qs, m_ref, acc_ref)

    @pl.when(i == 0)
    def _():
        for copy in copies:
            copy.wait()

    for step in range(QBLOCKS):

        @pl.when(i == step)
        def _(step=step):
            for n in range(step * each, min((step + 1) * each, len(chunks))):
                weight_copy(n).start()

    attend_active(places, pat_ref, me_ref, picked, kv, qs, m_ref, acc_ref)
    done = (acc_ref[:, :HD] / acc_ref[:, HD:]).astype(jnp.bfloat16)
    for g in range(GROUP):
        for s in range(STEPS):
            at = (g * STEPS + s) * QP
            row = pl.multiple_of(s * PROBS + i * QP, QP)
            att[pl.ds(row, QP), g * HD : (g + 1) * HD] = done[at : at + QP]

    @pl.when(i == QBLOCKS - 1)
    def _():
        for n in range(len(chunks)):
            weight_copy(n).wait()
            o_s[n] = dot(att[...], w_s[n]).astype(jnp.bfloat16)
            out_copy(n).start()
        for n in range(len(chunks)):
            out_copy(n).wait()


def prompt_part(pattern, me, head, places, groups, query, top, accum, stacks, weight):
    wide = GROUP * HD
    three = pl.BlockSpec((STEPS, QP, wide), lambda i, *_: (0, i, 0))
    state = lambda width: pl.BlockSpec((1, TILE, width), lambda i, *_: (i, 0, 0))
    anywhere = pl.BlockSpec(memory_space=pl.ANY)
    rows = STEPS * PROBS
    depth = weight.shape[0]
    chunks = sum(len(group) for group in groups)
    return pl.pallas_call(
        functools.partial(prompt_kernel, places, groups, len(stacks)),
        grid_spec=pltpu.PrefetchScalarGridSpec(
            num_scalar_prefetch=3,
            grid=(QBLOCKS,),
            in_specs=[three, state(HD), state(2 * HD)] + [anywhere] * (len(stacks) + 1),
            out_specs=[anywhere] * len(groups) + [pl.BlockSpec((rows, wide), lambda i, *_: (0, 0))],
            scratch_shapes=[
                pltpu.VMEM((TILE, 2 * HD), jnp.bfloat16),
                pltpu.VMEM((TILE, HD), jnp.float32),
                pltpu.VMEM((TILE, 2 * HD), jnp.float32),
                pltpu.VMEM((len(places), 2 * P_DEV, HD), jnp.bfloat16),
                pltpu.SMEM((len(places) + 4,), jnp.int32),
                pltpu.VMEM((chunks, depth, CHUNK), jnp.bfloat16),
                pltpu.VMEM((chunks, rows, CHUNK), jnp.bfloat16),
                pltpu.SemaphoreType.DMA((len(stacks),)),
                pltpu.SemaphoreType.DMA((chunks,)),
                pltpu.SemaphoreType.DMA((chunks,)),
            ],
        ),
        out_shape=[
            jax.ShapeDtypeStruct((len(group), rows, CHUNK), jnp.bfloat16) for group in groups
        ]
        + [jax.ShapeDtypeStruct((rows, wide), jnp.bfloat16)],
        compiler_params=params(),
        cost_estimate=LIGHT,
    )(pattern, me, head, query, top, accum, *stacks, weight)


def flip(r):
    return (0x36 >> (2 * r)) & 3


def column(head, base, far, r):
    return base + (((head // 4) ^ far) * 4) + ((head & 3) ^ flip(r))


def project_kernel(places, head_ref, a_ref, w_ref, out):
    out[0] = dot(a_ref[...], w_ref[...]).astype(jnp.bfloat16)


def project(attended, weight, head, places):
    rows, depth = attended.shape

    def chunk(i, head):
        found = jnp.int32(0)
        for k, place in enumerate(places):
            found = jnp.where(i == k, column(head[0], *place), found)
        return (0, found)

    return pl.pallas_call(
        functools.partial(project_kernel, places),
        grid_spec=pltpu.PrefetchScalarGridSpec(
            num_scalar_prefetch=1,
            grid=(len(places),),
            in_specs=[
                pl.BlockSpec((rows, depth), lambda i, head: (0, 0)),
                pl.BlockSpec((depth, CHUNK), chunk),
            ],
            out_specs=pl.BlockSpec((1, rows, CHUNK), lambda i, head: (i, 0, 0)),
        ),
        out_shape=jax.ShapeDtypeStruct((len(places), rows, CHUNK), jnp.bfloat16),
        compiler_params=params(PART),
        cost_estimate=LIGHT,
    )(head, attended, weight)


def chunk_at(head_ref, place):
    return pl.ds(pl.multiple_of(column(head_ref[0], *place) * CHUNK, CHUNK), CHUNK)


def assemble_kernel(places, head_ref, *refs):
    for ref, group in zip(refs[:-1], places):
        for j, place in enumerate(group):
            refs[-1][:, chunk_at(head_ref, place)] = ref[j]


def assemble(head, places, sources):
    rows = sources[0].shape[1]
    whole = lambda value: pl.BlockSpec(value.shape, lambda i, head: (0, 0, 0))
    return pl.pallas_call(
        functools.partial(assemble_kernel, places),
        grid_spec=pltpu.PrefetchScalarGridSpec(
            num_scalar_prefetch=1,
            grid=(1,),
            in_specs=[whole(value) for value in sources],
            out_specs=pl.BlockSpec((rows, 16 * CHUNK), lambda i, head: (0, 0)),
        ),
        out_shape=jax.ShapeDtypeStruct((rows, 16 * CHUNK), jnp.bfloat16),
        compiler_params=params(LITTLE),
        cost_estimate=LIGHT,
    )(head, *sources)


def complete_kernel(places, head_ref, earlier, *refs):
    sources, out, sems = refs[:-2], refs[-2], refs[-1]
    copies = []
    for ref, group in zip(sources, places):
        for j, place in enumerate(group):
            copies.append(
                pltpu.make_async_copy(
                    ref.at[j], out.at[:, chunk_at(head_ref, place)], sems.at[len(copies)]
                )
            )
    for copy in copies:
        copy.start()
    for copy in copies:
        copy.wait()


def complete(head, places, earlier, sources):
    anywhere = pl.BlockSpec(memory_space=pl.ANY)
    return pl.pallas_call(
        functools.partial(complete_kernel, places),
        grid_spec=pltpu.PrefetchScalarGridSpec(
            num_scalar_prefetch=1,
            grid=(1,),
            in_specs=[anywhere]
            + [pl.BlockSpec(value.shape, lambda i, head: (0, 0, 0)) for value in sources],
            out_specs=anywhere,
            scratch_shapes=[pltpu.SemaphoreType.DMA((sum(len(g) for g in places),))],
        ),
        out_shape=jax.ShapeDtypeStruct(earlier.shape, earlier.dtype),
        input_output_aliases={1: 0},
        compiler_params=params(LITTLE),
        cost_estimate=LIGHT,
    )(head, earlier, *sources)


def join_kernel(first_ref, begin_ref, len_ref, source, keys_out, vals_out):
    problem = first_ref[0] + pl.program_id(0)
    total = BRANCHES * SPAN
    flat = source[:, 0].reshape(total, 2 * HD)
    lane = lax.broadcasted_iota(jnp.int32, (1, total), 1)
    target = jnp.full((1, total), -1, jnp.int32)
    for b in range(BRANCHES):
        live = (lane >= b * SPAN) & (lane < b * SPAN + len_ref[b, problem])
        begin = begin_ref[b, problem] - P_DEV * BRANCHES - b * SPAN
        target = jnp.where(live, lane + begin, target)
    rows = 256
    for r0 in range(0, total, rows):
        slot = lax.broadcasted_iota(jnp.int32, (rows, 1), 0) + r0
        pick = jnp.where(target == slot, 1.0, 0.0).astype(jnp.bfloat16)
        got = jnp.dot(pick, flat, preferred_element_type=jnp.float32).astype(jnp.bfloat16)
        keys_out[0, r0 : r0 + rows, :] = got[:, :HD]
        vals_out[0, r0 : r0 + rows, :] = got[:, HD:]


def join(first, begins, lengths, source):
    share = source.shape[1]
    total = BRANCHES * SPAN
    out = pl.BlockSpec((1, total, HD), lambda i, *_: (i, 0, 0))
    shape = jax.ShapeDtypeStruct((share, total, HD), jnp.bfloat16)
    return pl.pallas_call(
        join_kernel,
        grid_spec=pltpu.PrefetchScalarGridSpec(
            num_scalar_prefetch=3,
            grid=(share,),
            in_specs=[pl.BlockSpec((BRANCHES, 1, SPAN, 2 * HD), lambda i, *_: (0, i, 0, 0))],
            out_specs=[out, out],
        ),
        out_shape=[shape, shape],
        compiler_params=params(LITTLE),
        cost_estimate=LIGHT,
    )(first, begins, lengths, source)


def chip_of(branch, dz, dy):
    return ((branch // 8) ^ dz) * 8 + ((branch // 2 + dy) % 4) * 2


def move_chip(value, dz, dy):
    perm = [(b, chip_of(b, dz, dy) + b % 2) for b in range(BRANCHES)]
    return lax.ppermute(value, "branch", perm)


def swap_core(value):
    return lax.ppermute(value, "branch", [(b, b ^ 1) for b in range(BRANCHES)])


def move_x(value, flip):
    return lax.ppermute(value, "head", [(h, h ^ flip) for h in range(KVH)])


def move_roles(o, p, q):
    return move_x(p, 1), move_x(q, 3), move_x(o, 2)


def add(*values):
    total = values[0].astype(jnp.float32)
    for value in values[1:]:
        total = total + value.astype(jnp.float32)
    return total.astype(jnp.bfloat16)


def after(value, *others):
    return lax.optimization_barrier((value, others))[0]


def shards(
    queries, new_keys, new_values, prompt_keys, prompt_values, span_keys, span_values,
    span_lengths, join_offsets, pattern, out_weight,
):
    me = lax.axis_index("branch")
    one = me.reshape(1)
    head = lax.axis_index("head").reshape(1)
    prompt_len = P_DEV * BRANCHES
    share = PROBS // BRANCHES

    own = pack_block(prompt_keys, prompt_values)
    near_at = [(0, 0), (1, 0), (0, 1), (0, 3), (0, 2)]
    near = [own] + [move_chip(own, dz, dy) for dz, dy in near_at[1:]]
    far_at = [(1, 1), (1, 3), (1, 2)]

    lengths = span_lengths.T
    offsets = join_offsets.T
    live = lax.dynamic_slice_in_dim(lengths, me, 1, 0)
    shift = lax.dynamic_slice_in_dim(offsets, me, 1, 0) - prompt_len
    steps = jnp.arange(STEPS, dtype=jnp.int32)[:, None]
    cosine, sine = tables(jnp.concatenate([prompt_len + live + steps, shift]))
    query, top, accum, sent = span_part(
        lengths,
        one,
        jnp.transpose(queries[0], (1, 0, 2)),
        cosine,
        sine,
        jnp.transpose(new_keys[0], (1, 0, 2)),
        jnp.transpose(new_values[0], (1, 0, 2)),
        span_keys[0],
        span_values[0],
    )

    near = after(near, query)
    near_stack = jnp.stack(near)
    near_other = swap_core(near_stack)
    far = [move_chip(near[1], 0, 1), move_chip(near[1], 0, 3), move_chip(near[4], 1, 0)]
    far_stack = jnp.stack(after(far, near_other))
    far_other = swap_core(far_stack)
    sent = after(sent, far[0]).reshape(BRANCHES, share, SPAN, 2 * HD)
    gathered = lax.all_to_all(sent, "branch", 0, 0, tiled=True)
    places = [(dz, dy, c) for at in (near_at, far_at) for c in (0, 1) for dz, dy in at]
    stacks = [near_stack, near_other, far_stack, far_other]

    half = 8
    roles = range(4)
    both = [[(0, far, r) for far in (1, 0)] for r in roles]
    zhere = [(half, 0, r) for r in roles]
    zthere = [(half, 1, r) for r in roles]
    zsend, xo, xp, xq, attended = prompt_part(
        pattern[0], one, head, places, [zthere] + both[:3], query, top, accum, stacks, out_weight
    )
    got_z = move_x(zsend, 4)
    got_x = move_roles(xo, xp, xq)
    kept = project(attended, out_weight, head, zhere + both[3])
    got_z = after(got_z, got_x)
    zo, zp, zq, zx = [add(kept[r], got_z[r]) for r in range(4)]
    got_zx = move_roles(zo, zp, zq)
    got_x = after(got_x, zx, gathered)
    xsum = add(kept[4:], *got_x)
    zsum = add(zx, *after(got_zx, xsum))

    pair = add(xsum, move_x(xsum, 4)[::-1])
    zp, zq, zo = move_roles(zsum, zsum, zsum)
    xp, xq, xo = move_roles(pair, pair, pair)
    zfour = jnp.stack(after([zo, zp, zq, zsum], pair))
    zother = move_x(zfour, 4)
    joined_keys, joined_values = join(
        (me * share).reshape(1), offsets, lengths, after(gathered, zfour)
    )
    mixed = assemble(head, [both[3], zhere], after([pair, zfour], joined_keys))
    mixed = complete(head, [zthere] + both[:3], mixed, [zother, xo, xp, xq])
    mixed = jnp.transpose(mixed.reshape(STEPS, PROBS, 16 * CHUNK), (1, 0, 2))[None]
    return mixed, joined_keys, joined_values


def solution(mesh):
    return jax.shard_map(
        shards,
        mesh=mesh,
        in_specs=(
            P("branch", None, None, "head"),
            P("branch", None, None, "head"),
            P("branch", None, None, "head"),
            P("branch", "head"),
            P("branch", "head"),
            P("branch", None, None, "head"),
            P("branch", None, None, "head"),
            P(),
            P(),
            P("branch", None, None),
            P("head", None),
        ),
        out_specs=(
            P("branch", None, None, None),
            P("branch", None, "head"),
            P("branch", None, "head"),
        ),
        check_vma=False,
    )
```

```python
import functools
import math

import jax
import jax.numpy as jnp
import numpy as np
from jax import lax
from jax.experimental import pallas as pl
from jax.experimental.pallas import tpu as pltpu
from jax.sharding import PartitionSpec as P

HEADS = 64
KVH = 8
HD = 128
GROUP = HEADS // KVH
STEPS = 3
SPAN = 64
BRANCHES = 16
QBLOCKS = 4
PROBS = 64
QP = PROBS // QBLOCKS
PIECES = STEPS * GROUP
TILE = PIECES * QP
P_DEV = 512
CHUNK = 512

rope_base = 500000.0
masked_score = -1e30
SCALE2 = math.log2(math.e) / math.sqrt(HD)
VMEM = 60 * 1024 * 1024
PART = 46 * 1024 * 1024
LITTLE = 24 * 1024 * 1024
LIGHT = pl.CostEstimate(flops=0, bytes_accessed=0, transcendentals=0)


def params(limit=VMEM):
    return pltpu.CompilerParams(dimension_semantics=("arbitrary",), vmem_limit_bytes=limit)


def tables(position):
    half = HD // 2
    exponent = np.arange(half) * (2.0 / HD)
    frequency = np.tile(np.exp(-math.log(rope_base) * exponent), 2).astype(np.float32)
    sign = np.repeat(np.float32([-1.0, 1.0]), half)
    angle = position.astype(jnp.float32)[..., None] * frequency
    return jnp.cos(angle), jnp.sin(angle) * sign


def turn(values, cosine, sine):
    return values * cosine + pltpu.roll(values, HD // 2, values.ndim - 1) * sine


def with_ones(values):
    return jnp.concatenate([values, jnp.ones_like(values)], 1)


def dot(a, b):
    return jnp.dot(a, b, preferred_element_type=jnp.float32)


def span_kernel(
    len_ref, me_ref, q_ref, cos_ref, sin_ref, nk_ref, nv_ref, sk_ref, sv_ref,
    q_out, m_out, acc_out, sent_out,
):
    first = pl.program_id(0) * QP
    lane = lax.broadcasted_iota(jnp.int32, (1, QP * SPAN), 1)
    code = jnp.full((1, QP * SPAN), -1, jnp.int32)
    for p in range(QP):
        live = len_ref[me_ref[0], first + p]
        code = jnp.where((lane >= p * SPAN) & (lane < p * SPAN + live), p, code)
    rotated = {}
    for g in range(GROUP):
        for s in range(STEPS):
            lanes = slice(g * HD, (g + 1) * HD)
            raw = q_ref[s, :, lanes].astype(jnp.float32)
            rotated[g, s] = turn(raw, cos_ref[s], sin_ref[s])
            q_out[s, :, lanes] = rotated[g, s].astype(jnp.bfloat16)
    fresh = [
        turn(nk_ref[s].astype(jnp.float32), cos_ref[s], sin_ref[s]).astype(jnp.bfloat16)
        for s in range(STEPS)
    ]
    pad = jnp.zeros((HD - STEPS * QP, HD), jnp.bfloat16)
    fresh_keys = jnp.concatenate(fresh + [pad], 0).T
    fresh_vals = with_ones(jnp.concatenate([nv_ref[s] for s in range(STEPS)] + [pad], 0))
    few = QP // 2
    rows = few * PIECES
    keys_of = few * SPAN
    row = lax.broadcasted_iota(jnp.int32, (rows, 1), 0)
    piece = row >> 3
    step = piece - 3 * ((piece * 22) >> 6)
    fresh_lane = lax.broadcasted_iota(jnp.int32, (1, HD), 1)
    for part in range(2):
        low = part * few
        prob = (row & (few - 1)) + low
        q = jnp.concatenate(
            [rotated[g, s][low : low + few] for g in range(GROUP) for s in range(STEPS)], 0
        ).astype(jnp.bfloat16)
        span_keys = sk_ref[low : low + few].reshape(keys_of, HD).T
        span_vals = with_ones(sv_ref[low : low + few].reshape(keys_of, HD))
        s1 = jnp.where(
            code[:, part * keys_of : (part + 1) * keys_of] == prob, dot(q, span_keys), masked_score
        )
        ok = ((fresh_lane & (QP - 1)) == prob) & ((fresh_lane >> 4) <= step)
        s2 = jnp.where(ok, dot(q, fresh_keys), masked_score)
        top = jnp.maximum(s1.max(1, keepdims=True), s2.max(1, keepdims=True)) * SCALE2
        p1 = jnp.exp2(s1 * SCALE2 - top).astype(jnp.bfloat16)
        p2 = jnp.exp2(s2 * SCALE2 - top).astype(jnp.bfloat16)
        total = dot(p1, span_vals) + dot(p2, fresh_vals)
        wide = jnp.broadcast_to(top, (rows, HD))
        for k in range(PIECES):
            m_out[0, k * QP + low : k * QP + low + few, :] = wide[k * few : (k + 1) * few]
            acc_out[0, k * QP + low : k * QP + low + few, :] = total[k * few : (k + 1) * few]
    keys = sk_ref[...].astype(jnp.float32)
    kcos = cos_ref[STEPS][:, None, :]
    ksin = sin_ref[STEPS][:, None, :]
    sent_out[:, :, :HD] = turn(keys, kcos, ksin).astype(jnp.bfloat16)
    sent_out[:, :, HD:] = sv_ref[...]


def span_part(
    lengths, me, queries, cosine, sine, new_keys, new_values, span_keys, span_values
):
    three = lambda width: pl.BlockSpec((STEPS, QP, width), lambda i, *_: (0, i, 0))
    span = lambda width: pl.BlockSpec((QP, SPAN, width), lambda i, *_: (i, 0, 0))
    table = pl.BlockSpec((STEPS + 1, QP, HD), lambda i, *_: (0, i, 0))
    state = lambda width: pl.BlockSpec((1, TILE, width), lambda i, *_: (i, 0, 0))
    wide = GROUP * HD
    return pl.pallas_call(
        span_kernel,
        grid_spec=pltpu.PrefetchScalarGridSpec(
            num_scalar_prefetch=2,
            grid=(QBLOCKS,),
            in_specs=[
                three(wide), table, table, three(HD), three(HD), span(HD), span(HD),
            ],
            out_specs=[three(wide), state(HD), state(2 * HD), span(2 * HD)],
        ),
        out_shape=[
            jax.ShapeDtypeStruct((STEPS, PROBS, wide), jnp.bfloat16),
            jax.ShapeDtypeStruct((QBLOCKS, TILE, HD), jnp.float32),
            jax.ShapeDtypeStruct((QBLOCKS, TILE, 2 * HD), jnp.float32),
            jax.ShapeDtypeStruct((PROBS, SPAN, 2 * HD), jnp.bfloat16),
        ],
        compiler_params=params(),
        cost_estimate=LIGHT,
    )(lengths, me, queries, cosine, sine, new_keys, new_values, span_keys, span_values)


def pack_kernel(keys_ref, vals_ref, out):
    for c in range(0, P_DEV, HD):
        out[c : c + HD, :] = keys_ref[c : c + HD, :].T
    out[P_DEV:, :] = vals_ref[...]


def pack_block(keys, vals):
    return pl.pallas_call(
        pack_kernel,
        out_shape=jax.ShapeDtypeStruct((2 * P_DEV, HD), jnp.bfloat16),
        compiler_params=pltpu.CompilerParams(vmem_limit_bytes=VMEM),
        cost_estimate=LIGHT,
    )(keys, vals)


def attend(picks, valid, kv, qs, m_ref, acc_ref):
    rows = 128
    keys = []
    vals = []
    for k in picks:
        flat = jnp.concatenate([kv[k, c : c + HD, :] for c in range(0, P_DEV, HD)], 1)
        keys.append(jnp.concatenate([flat, flat], 0))
        vals.append(with_ones(kv[k, P_DEV:, :]))
    for r0 in range(0, TILE, rows):
        at = slice(r0, r0 + rows)
        query = qs[at, :]
        old = m_ref[at, :]
        scores = [jnp.dot(query, key, preferred_element_type=jnp.float32) for key in keys]
        top = old
        for value, ok in zip(scores, valid):
            best = value.max(1, keepdims=True)
            top = jnp.maximum(top, best if ok is None else jnp.where(ok, best, masked_score))
        factor = jnp.exp2(old - top)
        total = acc_ref[at, :] * jnp.concatenate([factor, factor], 1)
        for value, val, ok in zip(scores, vals, valid):
            base = top if ok is None else jnp.where(ok, top, -masked_score)
            weights = jnp.concatenate(
                [
                    jnp.exp2(value[:, c : c + HD] - base).astype(jnp.bfloat16)
                    for c in range(0, P_DEV, HD)
                ],
                1,
            )
            total = total + jnp.dot(weights, val, preferred_element_type=jnp.float32)
        m_ref[at, :] = top
        acc_ref[at, :] = total


def attend_active(places, pat_ref, me_ref, picked, kv, qs, m_ref, acc_ref):
    i = pl.program_id(0)
    me = me_ref[0]
    for k in range(len(places) + 4):
        picked[k] = 0
    count = jnp.int32(0)
    for k, (dz, dy, other) in enumerate(places):
        picked[count] = k
        owner = chip_of(me, dz, -dy) + ((me & 1) ^ other)
        count = count + jnp.where(pat_ref[i, owner] > 0, 1, 0)
    fours = (count + 1) // 4

    def four(t, carry):
        base = 4 * t
        attend(
            [picked[base + k] for k in range(4)],
            [None, None, None, base + 3 < count],
            kv, qs, m_ref, acc_ref,
        )
        return carry

    lax.fori_loop(0, fours, four, 0)

    @pl.when(4 * fours < count)
    def _():
        base = 4 * fours
        attend(
            [picked[base], picked[base + 1]], [None, base + 1 < count], kv, qs, m_ref, acc_ref
        )


def load_state(q_ref, m_in, acc_in, qs, m_ref, acc_ref):
    for g in range(GROUP):
        for s in range(STEPS):
            at = (g * STEPS + s) * QP
            scaled = q_ref[s, :, g * HD : (g + 1) * HD].astype(jnp.float32) * SCALE2
            high = scaled.astype(jnp.bfloat16)
            qs[at : at + QP, :HD] = high
            qs[at : at + QP, HD:] = (scaled - high.astype(jnp.float32)).astype(jnp.bfloat16)
    m_ref[...] = m_in[0]
    acc_ref[...] = acc_in[0]


def prompt_kernel(
    places, groups, stacks, pat_ref, me_ref, head_ref, q_ref, m_in, acc_in, *refs
):
    blocks, weight, refs = refs[:stacks], refs[stacks], refs[stacks + 1 :]
    outs, att = refs[: len(groups)], refs[len(groups)]
    qs, m_ref, acc_ref, kv, picked, w_s, o_s, sems, w_sems, o_sems = refs[len(groups) + 1 :]
    i = pl.program_id(0)
    sizes = [ref.shape[0] for ref in blocks]
    copies = [
        pltpu.make_async_copy(ref, kv.at[pl.ds(sum(sizes[:k]), sizes[k])], sems.at[k])
        for k, ref in enumerate(blocks)
    ]
    chunks = [(k, j, place) for k, group in enumerate(groups) for j, place in enumerate(group)]
    each = -(-len(chunks) // QBLOCKS)

    def weight_copy(n):
        return pltpu.make_async_copy(
            weight.at[:, chunk_at(head_ref, chunks[n][2])], w_s.at[n], w_sems.at[n]
        )

    def out_copy(n):
        k, j, _ = chunks[n]
        return pltpu.make_async_copy(o_s.at[n], outs[k].at[j], o_sems.at[n])

    @pl.when(i == 0)
    def _():
        for copy in copies:
            copy.start()

    load_state(q_ref, m_in, acc_in, qs, m_ref, acc_ref)

    @pl.when(i == 0)
    def _():
        for copy in copies:
            copy.wait()

    for step in range(QBLOCKS):

        @pl.when(i == step)
        def _(step=step):
            for n in range(step * each, min((step + 1) * each, len(chunks))):
                weight_copy(n).start()

    attend_active(places, pat_ref, me_ref, picked, kv, qs, m_ref, acc_ref)
    done = (acc_ref[:, :HD] / acc_ref[:, HD:]).astype(jnp.bfloat16)
    for g in range(GROUP):
        for s in range(STEPS):
            at = (g * STEPS + s) * QP
            row = pl.multiple_of(s * PROBS + i * QP, QP)
            att[pl.ds(row, QP), g * HD : (g + 1) * HD] = done[at : at + QP]

    @pl.when(i == QBLOCKS - 1)
    def _():
        for n in range(len(chunks)):
            weight_copy(n).wait()
            o_s[n] = dot(att[...], w_s[n]).astype(jnp.bfloat16)
            out_copy(n).start()
        for n in range(len(chunks)):
            out_copy(n).wait()


def prompt_part(pattern, me, head, places, groups, query, top, accum, stacks, weight):
    wide = GROUP * HD
    three = pl.BlockSpec((STEPS, QP, wide), lambda i, *_: (0, i, 0))
    state = lambda width: pl.BlockSpec((1, TILE, width), lambda i, *_: (i, 0, 0))
    anywhere = pl.BlockSpec(memory_space=pl.ANY)
    rows = STEPS * PROBS
    depth = weight.shape[0]
    chunks = sum(len(group) for group in groups)
    return pl.pallas_call(
        functools.partial(prompt_kernel, places, groups, len(stacks)),
        grid_spec=pltpu.PrefetchScalarGridSpec(
            num_scalar_prefetch=3,
            grid=(QBLOCKS,),
            in_specs=[three, state(HD), state(2 * HD)] + [anywhere] * (len(stacks) + 1),
            out_specs=[anywhere] * len(groups) + [pl.BlockSpec((rows, wide), lambda i, *_: (0, 0))],
            scratch_shapes=[
                pltpu.VMEM((TILE, 2 * HD), jnp.bfloat16),
                pltpu.VMEM((TILE, HD), jnp.float32),
                pltpu.VMEM((TILE, 2 * HD), jnp.float32),
                pltpu.VMEM((len(places), 2 * P_DEV, HD), jnp.bfloat16),
                pltpu.SMEM((len(places) + 4,), jnp.int32),
                pltpu.VMEM((chunks, depth, CHUNK), jnp.bfloat16),
                pltpu.VMEM((chunks, rows, CHUNK), jnp.bfloat16),
                pltpu.SemaphoreType.DMA((len(stacks),)),
                pltpu.SemaphoreType.DMA((chunks,)),
                pltpu.SemaphoreType.DMA((chunks,)),
            ],
        ),
        out_shape=[
            jax.ShapeDtypeStruct((len(group), rows, CHUNK), jnp.bfloat16) for group in groups
        ]
        + [jax.ShapeDtypeStruct((rows, wide), jnp.bfloat16)],
        compiler_params=params(),
        cost_estimate=LIGHT,
    )(pattern, me, head, query, top, accum, *stacks, weight)


def flip(r):
    return (0x36 >> (2 * r)) & 3


def column(head, base, far, r):
    return base + (((head // 4) ^ far) * 4) + ((head & 3) ^ flip(r))


def project_kernel(places, head_ref, a_ref, w_ref, out):
    out[0] = dot(a_ref[...], w_ref[...]).astype(jnp.bfloat16)


def project(attended, weight, head, places):
    rows, depth = attended.shape

    def chunk(i, head):
        found = jnp.int32(0)
        for k, place in enumerate(places):
            found = jnp.where(i == k, column(head[0], *place), found)
        return (0, found)

    return pl.pallas_call(
        functools.partial(project_kernel, places),
        grid_spec=pltpu.PrefetchScalarGridSpec(
            num_scalar_prefetch=1,
            grid=(len(places),),
            in_specs=[
                pl.BlockSpec((rows, depth), lambda i, head: (0, 0)),
                pl.BlockSpec((depth, CHUNK), chunk),
            ],
            out_specs=pl.BlockSpec((1, rows, CHUNK), lambda i, head: (i, 0, 0)),
        ),
        out_shape=jax.ShapeDtypeStruct((len(places), rows, CHUNK), jnp.bfloat16),
        compiler_params=params(PART),
        cost_estimate=LIGHT,
    )(head, attended, weight)


def chunk_at(head_ref, place):
    return pl.ds(pl.multiple_of(column(head_ref[0], *place) * CHUNK, CHUNK), CHUNK)


def assemble_kernel(places, head_ref, *refs):
    for ref, group in zip(refs[:-1], places):
        for j, place in enumerate(group):
            refs[-1][:, chunk_at(head_ref, place)] = ref[j]


def assemble(head, places, sources):
    rows = sources[0].shape[1]
    whole = lambda value: pl.BlockSpec(value.shape, lambda i, head: (0, 0, 0))
    return pl.pallas_call(
        functools.partial(assemble_kernel, places),
        grid_spec=pltpu.PrefetchScalarGridSpec(
            num_scalar_prefetch=1,
            grid=(1,),
            in_specs=[whole(value) for value in sources],
            out_specs=pl.BlockSpec((rows, 16 * CHUNK), lambda i, head: (0, 0)),
        ),
        out_shape=jax.ShapeDtypeStruct((rows, 16 * CHUNK), jnp.bfloat16),
        compiler_params=params(LITTLE),
        cost_estimate=LIGHT,
    )(head, *sources)


def complete_kernel(places, head_ref, earlier, *refs):
    sources, out, sems = refs[:-2], refs[-2], refs[-1]
    copies = []
    for ref, group in zip(sources, places):
        for j, place in enumerate(group):
            copies.append(
                pltpu.make_async_copy(
                    ref.at[j], out.at[:, chunk_at(head_ref, place)], sems.at[len(copies)]
                )
            )
    for copy in copies:
        copy.start()
    for copy in copies:
        copy.wait()


def complete(head, places, earlier, sources):
    anywhere = pl.BlockSpec(memory_space=pl.ANY)
    return pl.pallas_call(
        functools.partial(complete_kernel, places),
        grid_spec=pltpu.PrefetchScalarGridSpec(
            num_scalar_prefetch=1,
            grid=(1,),
            in_specs=[anywhere]
            + [pl.BlockSpec(value.shape, lambda i, head: (0, 0, 0)) for value in sources],
            out_specs=anywhere,
            scratch_shapes=[pltpu.SemaphoreType.DMA((sum(len(g) for g in places),))],
        ),
        out_shape=jax.ShapeDtypeStruct(earlier.shape, earlier.dtype),
        input_output_aliases={1: 0},
        compiler_params=params(LITTLE),
        cost_estimate=LIGHT,
    )(head, earlier, *sources)


def join_kernel(first_ref, begin_ref, len_ref, source, keys_out, vals_out):
    problem = first_ref[0] + pl.program_id(0)
    total = BRANCHES * SPAN
    flat = source[:, 0].reshape(total, 2 * HD)
    lane = lax.broadcasted_iota(jnp.int32, (1, total), 1)
    target = jnp.full((1, total), -1, jnp.int32)
    for b in range(BRANCHES):
        live = (lane >= b * SPAN) & (lane < b * SPAN + len_ref[b, problem])
        begin = begin_ref[b, problem] - P_DEV * BRANCHES - b * SPAN
        target = jnp.where(live, lane + begin, target)
    rows = 256
    for r0 in range(0, total, rows):
        slot = lax.broadcasted_iota(jnp.int32, (rows, 1), 0) + r0
        pick = jnp.where(target == slot, 1.0, 0.0).astype(jnp.bfloat16)
        got = jnp.dot(pick, flat, preferred_element_type=jnp.float32).astype(jnp.bfloat16)
        keys_out[0, r0 : r0 + rows, :] = got[:, :HD]
        vals_out[0, r0 : r0 + rows, :] = got[:, HD:]


def join(first, begins, lengths, source):
    share = source.shape[1]
    total = BRANCHES * SPAN
    out = pl.BlockSpec((1, total, HD), lambda i, *_: (i, 0, 0))
    shape = jax.ShapeDtypeStruct((share, total, HD), jnp.bfloat16)
    return pl.pallas_call(
        join_kernel,
        grid_spec=pltpu.PrefetchScalarGridSpec(
            num_scalar_prefetch=3,
            grid=(share,),
            in_specs=[pl.BlockSpec((BRANCHES, 1, SPAN, 2 * HD), lambda i, *_: (0, i, 0, 0))],
            out_specs=[out, out],
        ),
        out_shape=[shape, shape],
        compiler_params=params(LITTLE),
        cost_estimate=LIGHT,
    )(first, begins, lengths, source)


def chip_of(branch, dz, dy):
    return ((branch // 8) ^ dz) * 8 + ((branch // 2 + dy) % 4) * 2


def move_chip(value, dz, dy):
    perm = [(b, chip_of(b, dz, dy) + b % 2) for b in range(BRANCHES)]
    return lax.ppermute(value, "branch", perm)


def swap_core(value):
    return lax.ppermute(value, "branch", [(b, b ^ 1) for b in range(BRANCHES)])


def move_x(value, flip):
    return lax.ppermute(value, "head", [(h, h ^ flip) for h in range(KVH)])


def move_roles(o, p, q):
    return move_x(p, 1), move_x(q, 3), move_x(o, 2)


def add(*values):
    total = values[0].astype(jnp.float32)
    for value in values[1:]:
        total = total + value.astype(jnp.float32)
    return total.astype(jnp.bfloat16)


def after(value, *others):
    return lax.optimization_barrier((value, others))[0]


def shards(
    queries, new_keys, new_values, prompt_keys, prompt_values, span_keys, span_values,
    span_lengths, join_offsets, pattern, out_weight,
):
    me = lax.axis_index("branch")
    one = me.reshape(1)
    head = lax.axis_index("head").reshape(1)
    prompt_len = P_DEV * BRANCHES
    share = PROBS // BRANCHES

    own = pack_block(prompt_keys, prompt_values)
    near_at = [(0, 0), (1, 0), (0, 1), (0, 3)]
    far_at = [(0, 2), (1, 1), (1, 3), (1, 2)]
    near = [own] + [move_chip(own, dz, dy) for dz, dy in near_at[1:]]
    far = [move_chip(own, 0, 2)] + [move_chip(near[1], 0, dy) for _, dy in far_at[1:]]

    lengths = span_lengths.T
    offsets = join_offsets.T
    live = lax.dynamic_slice_in_dim(lengths, me, 1, 0)
    shift = lax.dynamic_slice_in_dim(offsets, me, 1, 0) - prompt_len
    steps = jnp.arange(STEPS, dtype=jnp.int32)[:, None]
    cosine, sine = tables(jnp.concatenate([prompt_len + live + steps, shift]))
    query, top, accum, sent = span_part(
        lengths,
        one,
        jnp.transpose(queries[0], (1, 0, 2)),
        cosine,
        sine,
        jnp.transpose(new_keys[0], (1, 0, 2)),
        jnp.transpose(new_values[0], (1, 0, 2)),
        span_keys[0],
        span_values[0],
    )

    near, far = after((near, far), query)
    near_stack, far_stack = jnp.stack(near), jnp.stack(far)
    near_other, far_other = swap_core(near_stack), swap_core(far_stack)
    sent = after(sent, near_stack, far_stack).reshape(BRANCHES, share, SPAN, 2 * HD)
    gathered = lax.all_to_all(sent, "branch", 0, 0, tiled=True)
    places = [(dz, dy, c) for at in (near_at, far_at) for c in (0, 1) for dz, dy in at]
    stacks = [near_stack, near_other, far_stack, far_other]

    half = 8
    roles = range(4)
    both = [[(0, far, r) for far in (1, 0)] for r in roles]
    zhere = [(half, 0, r) for r in roles]
    zthere = [(half, 1, r) for r in roles]
    zsend, xo, xp, xq, attended = prompt_part(
        pattern[0], one, head, places, [zthere] + both[:3], query, top, accum, stacks, out_weight
    )
    got_z = move_x(zsend, 4)
    got_x = move_roles(xo, xp, xq)
    kept = project(attended, out_weight, head, zhere + both[3])
    got_z = after(got_z, got_x)
    zo, zp, zq, zx = [add(kept[r], got_z[r]) for r in range(4)]
    got_zx = move_roles(zo, zp, zq)
    got_x = after(got_x, zx, gathered)
    xsum = add(kept[4:], *got_x)
    zsum = add(zx, *after(got_zx, xsum))

    pair = add(xsum, move_x(xsum, 4)[::-1])
    zp, zq, zo = move_roles(zsum, zsum, zsum)
    xp, xq, xo = move_roles(pair, pair, pair)
    zfour = jnp.stack(after([zo, zp, zq, zsum], pair))
    zother = move_x(zfour, 4)
    joined_keys, joined_values = join(
        (me * share).reshape(1), offsets, lengths, after(gathered, zfour)
    )
    mixed = assemble(head, [both[3], zhere], after([pair, zfour], joined_keys))
    mixed = complete(head, [zthere] + both[:3], mixed, [zother, xo, xp, xq])
    mixed = jnp.transpose(mixed.reshape(STEPS, PROBS, 16 * CHUNK), (1, 0, 2))[None]
    return mixed, joined_keys, joined_values


def solution(mesh):
    return jax.shard_map(
        shards,
        mesh=mesh,
        in_specs=(
            P("branch", None, None, "head"),
            P("branch", None, None, "head"),
            P("branch", None, None, "head"),
            P("branch", "head"),
            P("branch", "head"),
            P("branch", None, None, "head"),
            P("branch", None, None, "head"),
            P(),
            P(),
            P("branch", None, None),
            P("head", None),
        ),
        out_specs=(
            P("branch", None, None, None),
            P("branch", None, "head"),
            P("branch", None, "head"),
        ),
        check_vma=False,
    )
```

```python
import functools
import math

import jax
import jax.numpy as jnp
import numpy as np
from jax import lax
from jax.experimental import pallas as pl
from jax.experimental.pallas import tpu as pltpu
from jax.sharding import PartitionSpec as P

HEADS = 64
KVH = 8
HD = 128
GROUP = HEADS // KVH
STEPS = 3
SPAN = 64
BRANCHES = 16
QBLOCKS = 4
PROBS = 64
QP = PROBS // QBLOCKS
PIECES = STEPS * GROUP
TILE = PIECES * QP
P_DEV = 512
CHUNK = 512

rope_base = 500000.0
masked_score = -1e30
SCALE2 = math.log2(math.e) / math.sqrt(HD)
VMEM = 60 * 1024 * 1024
PART = 46 * 1024 * 1024
LITTLE = 24 * 1024 * 1024
LIGHT = pl.CostEstimate(flops=0, bytes_accessed=0, transcendentals=0)


def params(limit=VMEM):
    return pltpu.CompilerParams(dimension_semantics=("arbitrary",), vmem_limit_bytes=limit)


def tables(position):
    half = HD // 2
    exponent = np.arange(half) * (2.0 / HD)
    frequency = np.tile(np.exp(-math.log(rope_base) * exponent), 2).astype(np.float32)
    sign = np.repeat(np.float32([-1.0, 1.0]), half)
    angle = position.astype(jnp.float32)[..., None] * frequency
    return jnp.cos(angle), jnp.sin(angle) * sign


def turn(values, cosine, sine):
    return values * cosine + pltpu.roll(values, HD // 2, values.ndim - 1) * sine


def with_ones(values):
    return jnp.concatenate([values, jnp.ones_like(values)], 1)


def dot(a, b):
    return jnp.dot(a, b, preferred_element_type=jnp.float32)


def span_kernel(
    len_ref, me_ref, q_ref, cos_ref, sin_ref, nk_ref, nv_ref, sk_ref, sv_ref,
    q_out, m_out, acc_out, sent_out,
):
    first = pl.program_id(0) * QP
    lane = lax.broadcasted_iota(jnp.int32, (1, QP * SPAN), 1)
    code = jnp.full((1, QP * SPAN), -1, jnp.int32)
    for p in range(QP):
        live = len_ref[me_ref[0], first + p]
        code = jnp.where((lane >= p * SPAN) & (lane < p * SPAN + live), p, code)
    rotated = {}
    for g in range(GROUP):
        for s in range(STEPS):
            lanes = slice(g * HD, (g + 1) * HD)
            raw = q_ref[s, :, lanes].astype(jnp.float32)
            rotated[g, s] = turn(raw, cos_ref[s], sin_ref[s])
            q_out[s, :, lanes] = rotated[g, s].astype(jnp.bfloat16)
    fresh = [
        turn(nk_ref[s].astype(jnp.float32), cos_ref[s], sin_ref[s]).astype(jnp.bfloat16)
        for s in range(STEPS)
    ]
    pad = jnp.zeros((HD - STEPS * QP, HD), jnp.bfloat16)
    fresh_keys = jnp.concatenate(fresh + [pad], 0).T
    fresh_vals = with_ones(jnp.concatenate([nv_ref[s] for s in range(STEPS)] + [pad], 0))
    few = QP // 2
    rows = few * PIECES
    keys_of = few * SPAN
    row = lax.broadcasted_iota(jnp.int32, (rows, 1), 0)
    piece = row >> 3
    step = piece - 3 * ((piece * 22) >> 6)
    fresh_lane = lax.broadcasted_iota(jnp.int32, (1, HD), 1)
    for part in range(2):
        low = part * few
        prob = (row & (few - 1)) + low
        q = jnp.concatenate(
            [rotated[g, s][low : low + few] for g in range(GROUP) for s in range(STEPS)], 0
        ).astype(jnp.bfloat16)
        span_keys = sk_ref[low : low + few].reshape(keys_of, HD).T
        span_vals = with_ones(sv_ref[low : low + few].reshape(keys_of, HD))
        s1 = jnp.where(
            code[:, part * keys_of : (part + 1) * keys_of] == prob, dot(q, span_keys), masked_score
        )
        ok = ((fresh_lane & (QP - 1)) == prob) & ((fresh_lane >> 4) <= step)
        s2 = jnp.where(ok, dot(q, fresh_keys), masked_score)
        top = jnp.maximum(s1.max(1, keepdims=True), s2.max(1, keepdims=True)) * SCALE2
        p1 = jnp.exp2(s1 * SCALE2 - top).astype(jnp.bfloat16)
        p2 = jnp.exp2(s2 * SCALE2 - top).astype(jnp.bfloat16)
        total = dot(p1, span_vals) + dot(p2, fresh_vals)
        wide = jnp.broadcast_to(top, (rows, HD))
        for k in range(PIECES):
            m_out[0, k * QP + low : k * QP + low + few, :] = wide[k * few : (k + 1) * few]
            acc_out[0, k * QP + low : k * QP + low + few, :] = total[k * few : (k + 1) * few]
    keys = sk_ref[...].astype(jnp.float32)
    kcos = cos_ref[STEPS][:, None, :]
    ksin = sin_ref[STEPS][:, None, :]
    sent_out[:, :, :HD] = turn(keys, kcos, ksin).astype(jnp.bfloat16)
    sent_out[:, :, HD:] = sv_ref[...]


def span_part(
    lengths, me, queries, cosine, sine, new_keys, new_values, span_keys, span_values
):
    three = lambda width: pl.BlockSpec((STEPS, QP, width), lambda i, *_: (0, i, 0))
    span = lambda width: pl.BlockSpec((QP, SPAN, width), lambda i, *_: (i, 0, 0))
    table = pl.BlockSpec((STEPS + 1, QP, HD), lambda i, *_: (0, i, 0))
    state = lambda width: pl.BlockSpec((1, TILE, width), lambda i, *_: (i, 0, 0))
    wide = GROUP * HD
    return pl.pallas_call(
        span_kernel,
        grid_spec=pltpu.PrefetchScalarGridSpec(
            num_scalar_prefetch=2,
            grid=(QBLOCKS,),
            in_specs=[
                three(wide), table, table, three(HD), three(HD), span(HD), span(HD),
            ],
            out_specs=[three(wide), state(HD), state(2 * HD), span(2 * HD)],
        ),
        out_shape=[
            jax.ShapeDtypeStruct((STEPS, PROBS, wide), jnp.bfloat16),
            jax.ShapeDtypeStruct((QBLOCKS, TILE, HD), jnp.float32),
            jax.ShapeDtypeStruct((QBLOCKS, TILE, 2 * HD), jnp.float32),
            jax.ShapeDtypeStruct((PROBS, SPAN, 2 * HD), jnp.bfloat16),
        ],
        compiler_params=params(),
        cost_estimate=LIGHT,
    )(lengths, me, queries, cosine, sine, new_keys, new_values, span_keys, span_values)


def pack_kernel(keys_ref, vals_ref, out):
    for c in range(0, P_DEV, HD):
        out[c : c + HD, :] = keys_ref[c : c + HD, :].T
    out[P_DEV:, :] = vals_ref[...]


def pack_block(keys, vals):
    return pl.pallas_call(
        pack_kernel,
        out_shape=jax.ShapeDtypeStruct((2 * P_DEV, HD), jnp.bfloat16),
        compiler_params=pltpu.CompilerParams(vmem_limit_bytes=VMEM),
        cost_estimate=LIGHT,
    )(keys, vals)


def attend(picks, valid, kv, qs, m_ref, acc_ref):
    rows = 128
    keys = []
    vals = []
    for k in picks:
        flat = jnp.concatenate([kv[k, c : c + HD, :] for c in range(0, P_DEV, HD)], 1)
        keys.append(jnp.concatenate([flat, flat], 0))
        vals.append(with_ones(kv[k, P_DEV:, :]))
    for r0 in range(0, TILE, rows):
        at = slice(r0, r0 + rows)
        query = qs[at, :]
        old = m_ref[at, :]
        scores = [jnp.dot(query, key, preferred_element_type=jnp.float32) for key in keys]
        top = old
        for value, ok in zip(scores, valid):
            best = value.max(1, keepdims=True)
            top = jnp.maximum(top, best if ok is None else jnp.where(ok, best, masked_score))
        factor = jnp.exp2(old - top)
        total = acc_ref[at, :] * jnp.concatenate([factor, factor], 1)
        for value, val, ok in zip(scores, vals, valid):
            base = top if ok is None else jnp.where(ok, top, -masked_score)
            weights = jnp.concatenate(
                [
                    jnp.exp2(value[:, c : c + HD] - base).astype(jnp.bfloat16)
                    for c in range(0, P_DEV, HD)
                ],
                1,
            )
            total = total + jnp.dot(weights, val, preferred_element_type=jnp.float32)
        m_ref[at, :] = top
        acc_ref[at, :] = total


def attend_active(places, pat_ref, me_ref, picked, kv, qs, m_ref, acc_ref):
    i = pl.program_id(0)
    me = me_ref[0]
    for k in range(len(places) + 4):
        picked[k] = 0
    count = jnp.int32(0)
    for k, (dz, dy, other) in enumerate(places):
        picked[count] = k
        owner = chip_of(me, dz, -dy) + ((me & 1) ^ other)
        count = count + jnp.where(pat_ref[i, owner] > 0, 1, 0)
    fours = (count + 1) // 4

    def four(t, carry):
        base = 4 * t
        attend(
            [picked[base + k] for k in range(4)],
            [None, None, None, base + 3 < count],
            kv, qs, m_ref, acc_ref,
        )
        return carry

    lax.fori_loop(0, fours, four, 0)

    @pl.when(4 * fours < count)
    def _():
        base = 4 * fours
        attend(
            [picked[base], picked[base + 1]], [None, base + 1 < count], kv, qs, m_ref, acc_ref
        )


def load_state(q_ref, m_in, acc_in, qs, m_ref, acc_ref):
    for g in range(GROUP):
        for s in range(STEPS):
            at = (g * STEPS + s) * QP
            scaled = q_ref[s, :, g * HD : (g + 1) * HD].astype(jnp.float32) * SCALE2
            high = scaled.astype(jnp.bfloat16)
            qs[at : at + QP, :HD] = high
            qs[at : at + QP, HD:] = (scaled - high.astype(jnp.float32)).astype(jnp.bfloat16)
    m_ref[...] = m_in[0]
    acc_ref[...] = acc_in[0]


def prompt_kernel(
    places, groups, stacks, pat_ref, me_ref, head_ref, q_ref, m_in, acc_in, *refs
):
    blocks, weight, refs = refs[:stacks], refs[stacks], refs[stacks + 1 :]
    outs, att = refs[: len(groups)], refs[len(groups)]
    qs, m_ref, acc_ref, kv, picked, w_s, o_s, sems, w_sems, o_sems = refs[len(groups) + 1 :]
    i = pl.program_id(0)
    sizes = [ref.shape[0] for ref in blocks]
    copies = [
        pltpu.make_async_copy(ref, kv.at[pl.ds(sum(sizes[:k]), sizes[k])], sems.at[k])
        for k, ref in enumerate(blocks)
    ]
    chunks = [(k, j, place) for k, group in enumerate(groups) for j, place in enumerate(group)]
    each = -(-len(chunks) // QBLOCKS)

    def weight_copy(n):
        return pltpu.make_async_copy(
            weight.at[:, chunk_at(head_ref, chunks[n][2])], w_s.at[n], w_sems.at[n]
        )

    def out_copy(n):
        k, j, _ = chunks[n]
        return pltpu.make_async_copy(o_s.at[n], outs[k].at[j], o_sems.at[n])

    @pl.when(i == 0)
    def _():
        for copy in copies:
            copy.start()

    load_state(q_ref, m_in, acc_in, qs, m_ref, acc_ref)

    @pl.when(i == 0)
    def _():
        for copy in copies:
            copy.wait()

    for step in range(QBLOCKS):

        @pl.when(i == step)
        def _(step=step):
            for n in range(step * each, min((step + 1) * each, len(chunks))):
                weight_copy(n).start()

    attend_active(places, pat_ref, me_ref, picked, kv, qs, m_ref, acc_ref)
    done = (acc_ref[:, :HD] / acc_ref[:, HD:]).astype(jnp.bfloat16)
    for g in range(GROUP):
        for s in range(STEPS):
            at = (g * STEPS + s) * QP
            row = pl.multiple_of(s * PROBS + i * QP, QP)
            att[pl.ds(row, QP), g * HD : (g + 1) * HD] = done[at : at + QP]

    @pl.when(i == QBLOCKS - 1)
    def _():
        for n in range(len(chunks)):
            weight_copy(n).wait()
            o_s[n] = dot(att[...], w_s[n]).astype(jnp.bfloat16)
            out_copy(n).start()
        for n in range(len(chunks)):
            out_copy(n).wait()


def prompt_part(pattern, me, head, places, groups, query, top, accum, stacks, weight):
    wide = GROUP * HD
    three = pl.BlockSpec((STEPS, QP, wide), lambda i, *_: (0, i, 0))
    state = lambda width: pl.BlockSpec((1, TILE, width), lambda i, *_: (i, 0, 0))
    anywhere = pl.BlockSpec(memory_space=pl.ANY)
    rows = STEPS * PROBS
    depth = weight.shape[0]
    chunks = sum(len(group) for group in groups)
    return pl.pallas_call(
        functools.partial(prompt_kernel, places, groups, len(stacks)),
        grid_spec=pltpu.PrefetchScalarGridSpec(
            num_scalar_prefetch=3,
            grid=(QBLOCKS,),
            in_specs=[three, state(HD), state(2 * HD)] + [anywhere] * (len(stacks) + 1),
            out_specs=[anywhere] * len(groups) + [pl.BlockSpec((rows, wide), lambda i, *_: (0, 0))],
            scratch_shapes=[
                pltpu.VMEM((TILE, 2 * HD), jnp.bfloat16),
                pltpu.VMEM((TILE, HD), jnp.float32),
                pltpu.VMEM((TILE, 2 * HD), jnp.float32),
                pltpu.VMEM((len(places), 2 * P_DEV, HD), jnp.bfloat16),
                pltpu.SMEM((len(places) + 4,), jnp.int32),
                pltpu.VMEM((chunks, depth, CHUNK), jnp.bfloat16),
                pltpu.VMEM((chunks, rows, CHUNK), jnp.bfloat16),
                pltpu.SemaphoreType.DMA((len(stacks),)),
                pltpu.SemaphoreType.DMA((chunks,)),
                pltpu.SemaphoreType.DMA((chunks,)),
            ],
        ),
        out_shape=[
            jax.ShapeDtypeStruct((len(group), rows, CHUNK), jnp.bfloat16) for group in groups
        ]
        + [jax.ShapeDtypeStruct((rows, wide), jnp.bfloat16)],
        compiler_params=params(),
        cost_estimate=LIGHT,
    )(pattern, me, head, query, top, accum, *stacks, weight)


def flip(r):
    return (0x36 >> (2 * r)) & 3


def column(head, base, far, r):
    return base + (((head // 4) ^ far) * 4) + ((head & 3) ^ flip(r))


def project_kernel(places, head_ref, a_ref, w_ref, out):
    out[0] = dot(a_ref[...], w_ref[...]).astype(jnp.bfloat16)


def project(attended, weight, head, places):
    rows, depth = attended.shape

    def chunk(i, head):
        found = jnp.int32(0)
        for k, place in enumerate(places):
            found = jnp.where(i == k, column(head[0], *place), found)
        return (0, found)

    return pl.pallas_call(
        functools.partial(project_kernel, places),
        grid_spec=pltpu.PrefetchScalarGridSpec(
            num_scalar_prefetch=1,
            grid=(len(places),),
            in_specs=[
                pl.BlockSpec((rows, depth), lambda i, head: (0, 0)),
                pl.BlockSpec((depth, CHUNK), chunk),
            ],
            out_specs=pl.BlockSpec((1, rows, CHUNK), lambda i, head: (i, 0, 0)),
        ),
        out_shape=jax.ShapeDtypeStruct((len(places), rows, CHUNK), jnp.bfloat16),
        compiler_params=params(PART),
        cost_estimate=LIGHT,
    )(head, attended, weight)


def chunk_at(head_ref, place):
    return pl.ds(pl.multiple_of(column(head_ref[0], *place) * CHUNK, CHUNK), CHUNK)


def row_starts(places, refs):
    starts = []
    for k, group in enumerate(places):
        starts.append(refs[k].shape[1] if k and group == places[k - 1] else 0)
    return starts


def assemble_kernel(places, head_ref, *refs):
    for ref, group, row in zip(refs[:-1], places, row_starts(places, refs)):
        for j, place in enumerate(group):
            refs[-1][row : row + ref.shape[1], chunk_at(head_ref, place)] = ref[j]


def assemble(head, places, sources):
    rows = STEPS * PROBS
    whole = lambda value: pl.BlockSpec(value.shape, lambda i, head: (0, 0, 0))
    return pl.pallas_call(
        functools.partial(assemble_kernel, places),
        grid_spec=pltpu.PrefetchScalarGridSpec(
            num_scalar_prefetch=1,
            grid=(1,),
            in_specs=[whole(value) for value in sources],
            out_specs=pl.BlockSpec((rows, 16 * CHUNK), lambda i, head: (0, 0)),
        ),
        out_shape=jax.ShapeDtypeStruct((rows, 16 * CHUNK), jnp.bfloat16),
        compiler_params=params(LITTLE),
        cost_estimate=LIGHT,
    )(head, *sources)


def complete_kernel(places, head_ref, earlier, *refs):
    sources, out, sems = refs[:-2], refs[-2], refs[-1]
    copies = []
    for ref, group, row in zip(sources, places, row_starts(places, sources)):
        for j, place in enumerate(group):
            goal = out.at[row : row + ref.shape[1], chunk_at(head_ref, place)]
            copies.append(pltpu.make_async_copy(ref.at[j], goal, sems.at[len(copies)]))
    for copy in copies:
        copy.start()
    for copy in copies:
        copy.wait()


def complete(head, places, earlier, sources):
    anywhere = pl.BlockSpec(memory_space=pl.ANY)
    return pl.pallas_call(
        functools.partial(complete_kernel, places),
        grid_spec=pltpu.PrefetchScalarGridSpec(
            num_scalar_prefetch=1,
            grid=(1,),
            in_specs=[anywhere]
            + [pl.BlockSpec(value.shape, lambda i, head: (0, 0, 0)) for value in sources],
            out_specs=anywhere,
            scratch_shapes=[pltpu.SemaphoreType.DMA((sum(len(g) for g in places),))],
        ),
        out_shape=jax.ShapeDtypeStruct(earlier.shape, earlier.dtype),
        input_output_aliases={1: 0},
        compiler_params=params(LITTLE),
        cost_estimate=LIGHT,
    )(head, earlier, *sources)


def join_kernel(first_ref, begin_ref, len_ref, source, keys_out, vals_out):
    problem = first_ref[0] + pl.program_id(0)
    total = BRANCHES * SPAN
    flat = source[:, 0].reshape(total, 2 * HD)
    lane = lax.broadcasted_iota(jnp.int32, (1, total), 1)
    target = jnp.full((1, total), -1, jnp.int32)
    for b in range(BRANCHES):
        live = (lane >= b * SPAN) & (lane < b * SPAN + len_ref[b, problem])
        begin = begin_ref[b, problem] - P_DEV * BRANCHES - b * SPAN
        target = jnp.where(live, lane + begin, target)
    rows = 256
    for r0 in range(0, total, rows):
        slot = lax.broadcasted_iota(jnp.int32, (rows, 1), 0) + r0
        pick = jnp.where(target == slot, 1.0, 0.0).astype(jnp.bfloat16)
        got = jnp.dot(pick, flat, preferred_element_type=jnp.float32).astype(jnp.bfloat16)
        keys_out[0, r0 : r0 + rows, :] = got[:, :HD]
        vals_out[0, r0 : r0 + rows, :] = got[:, HD:]


def join(first, begins, lengths, source):
    share = source.shape[1]
    total = BRANCHES * SPAN
    out = pl.BlockSpec((1, total, HD), lambda i, *_: (i, 0, 0))
    shape = jax.ShapeDtypeStruct((share, total, HD), jnp.bfloat16)
    return pl.pallas_call(
        join_kernel,
        grid_spec=pltpu.PrefetchScalarGridSpec(
            num_scalar_prefetch=3,
            grid=(share,),
            in_specs=[pl.BlockSpec((BRANCHES, 1, SPAN, 2 * HD), lambda i, *_: (0, i, 0, 0))],
            out_specs=[out, out],
        ),
        out_shape=[shape, shape],
        compiler_params=params(LITTLE),
        cost_estimate=LIGHT,
    )(first, begins, lengths, source)


def chip_of(branch, dz, dy):
    return ((branch // 8) ^ dz) * 8 + ((branch // 2 + dy) % 4) * 2


def move_chip(value, dz, dy):
    perm = [(b, chip_of(b, dz, dy) + b % 2) for b in range(BRANCHES)]
    return lax.ppermute(value, "branch", perm)


def swap_core(value):
    return lax.ppermute(value, "branch", [(b, b ^ 1) for b in range(BRANCHES)])


def move_x(value, flip):
    return lax.ppermute(value, "head", [(h, h ^ flip) for h in range(KVH)])


def move_roles(o, p, q):
    return move_x(p, 1), move_x(q, 3), move_x(o, 2)


def add(*values):
    total = values[0].astype(jnp.float32)
    for value in values[1:]:
        total = total + value.astype(jnp.float32)
    return total.astype(jnp.bfloat16)


def after(value, *others):
    return lax.optimization_barrier((value, others))[0]


def shards(
    queries, new_keys, new_values, prompt_keys, prompt_values, span_keys, span_values,
    span_lengths, join_offsets, pattern, out_weight,
):
    me = lax.axis_index("branch")
    one = me.reshape(1)
    head = lax.axis_index("head").reshape(1)
    prompt_len = P_DEV * BRANCHES
    share = PROBS // BRANCHES

    own = pack_block(prompt_keys, prompt_values)
    near_at = [(0, 0), (1, 0), (0, 1), (0, 3)]
    far_at = [(0, 2), (1, 1), (1, 3), (1, 2)]
    near = [own] + [move_chip(own, dz, dy) for dz, dy in near_at[1:]]
    far = [move_chip(own, 0, 2)] + [move_chip(near[1], 0, dy) for _, dy in far_at[1:]]

    lengths = span_lengths.T
    offsets = join_offsets.T
    live = lax.dynamic_slice_in_dim(lengths, me, 1, 0)
    shift = lax.dynamic_slice_in_dim(offsets, me, 1, 0) - prompt_len
    steps = jnp.arange(STEPS, dtype=jnp.int32)[:, None]
    cosine, sine = tables(jnp.concatenate([prompt_len + live + steps, shift]))
    query, top, accum, sent = span_part(
        lengths,
        one,
        jnp.transpose(queries[0], (1, 0, 2)),
        cosine,
        sine,
        jnp.transpose(new_keys[0], (1, 0, 2)),
        jnp.transpose(new_values[0], (1, 0, 2)),
        span_keys[0],
        span_values[0],
    )

    near, far = after((near, far), query)
    near_stack, far_stack = jnp.stack(near), jnp.stack(far)
    near_other, far_other = swap_core(near_stack), swap_core(far_stack)
    sent = after(sent, near_stack, far_stack).reshape(BRANCHES, share, SPAN, 2 * HD)
    gathered = lax.all_to_all(sent, "branch", 0, 0, tiled=True)
    places = [(dz, dy, c) for at in (near_at, far_at) for c in (0, 1) for dz, dy in at]
    stacks = [near_stack, near_other, far_stack, far_other]

    half = 8
    roles = range(4)
    both = [[(0, far, r) for far in (1, 0)] for r in roles]
    zhere = [(half, 0, r) for r in roles]
    zthere = [(half, 1, r) for r in roles]
    zsend, xo, xp, xq, attended = prompt_part(
        pattern[0], one, head, places, [zthere] + both[:3], query, top, accum, stacks, out_weight
    )
    got_z = move_x(zsend, 4)
    got_x = move_roles(xo, xp, xq)
    kept = project(attended, out_weight, head, zhere + both[3])
    got_z = after(got_z, got_x)
    rows = STEPS * PROBS // 2
    halves = [slice(k, k + rows) for k in (0, rows)]
    zpart = [[add(kept[r][h], got_z[r][h]) for r in roles] for h in halves]
    got_zx = [move_roles(*part[:3]) for part in zpart]
    got_x = after(got_x, zpart[1][3], gathered)
    xsum = add(kept[4:], *got_x)
    got_zx[1] = after(got_zx[1], xsum)
    zsum = [add(part[3], *got) for part, got in zip(zpart, got_zx)]

    pair = add(xsum, move_x(xsum, 4)[::-1])
    zback = [move_roles(part, part, part) for part in zsum]
    zback[1] = after(zback[1], pair)
    zfour = [jnp.stack([zo, zp, zq, part]) for (zp, zq, zo), part in zip(zback, zsum)]
    zother = [move_x(part, 4) for part in zfour]
    xp, xq, xo = move_roles(pair, pair, pair)
    joined_keys, joined_values = join(
        (me * share).reshape(1), offsets, lengths, after(gathered, zfour[1])
    )
    mixed = assemble(head, [both[3], zhere, zhere], after([pair] + zfour, joined_keys))
    mixed = complete(head, [zthere, zthere] + both[:3], mixed, zother + [xo, xp, xq])
    mixed = jnp.transpose(mixed.reshape(STEPS, PROBS, 16 * CHUNK), (1, 0, 2))[None]
    return mixed, joined_keys, joined_values


def solution(mesh):
    return jax.shard_map(
        shards,
        mesh=mesh,
        in_specs=(
            P("branch", None, None, "head"),
            P("branch", None, None, "head"),
            P("branch", None, None, "head"),
            P("branch", "head"),
            P("branch", "head"),
            P("branch", None, None, "head"),
            P("branch", None, None, "head"),
            P(),
            P(),
            P("branch", None, None),
            P("head", None),
        ),
        out_specs=(
            P("branch", None, None, None),
            P("branch", None, "head"),
            P("branch", None, "head"),
        ),
        check_vma=False,
    )
```

```python
import functools
import math

import jax
import jax.numpy as jnp
import numpy as np
from jax import lax
from jax.experimental import pallas as pl
from jax.experimental.pallas import tpu as pltpu
from jax.sharding import PartitionSpec as P

HEADS = 64
KVH = 8
HD = 128
GROUP = HEADS // KVH
STEPS = 3
SPAN = 64
BRANCHES = 16
QBLOCKS = 4
PROBS = 64
QP = PROBS // QBLOCKS
PIECES = STEPS * GROUP
TILE = PIECES * QP
P_DEV = 512
CHUNK = 512

rope_base = 500000.0
masked_score = -1e30
SCALE2 = math.log2(math.e) / math.sqrt(HD)
VMEM = 60 * 1024 * 1024
PART = 46 * 1024 * 1024
LITTLE = 24 * 1024 * 1024
LIGHT = pl.CostEstimate(flops=0, bytes_accessed=0, transcendentals=0)


def params(limit=VMEM):
    return pltpu.CompilerParams(dimension_semantics=("arbitrary",), vmem_limit_bytes=limit)


def tables(position):
    half = HD // 2
    exponent = np.arange(half) * (2.0 / HD)
    frequency = np.tile(np.exp(-math.log(rope_base) * exponent), 2).astype(np.float32)
    sign = np.repeat(np.float32([-1.0, 1.0]), half)
    angle = position.astype(jnp.float32)[..., None] * frequency
    return jnp.cos(angle), jnp.sin(angle) * sign


def turn(values, cosine, sine):
    return values * cosine + pltpu.roll(values, HD // 2, values.ndim - 1) * sine


def with_ones(values):
    return jnp.concatenate([values, jnp.ones_like(values)], 1)


def dot(a, b):
    return jnp.dot(a, b, preferred_element_type=jnp.float32)


def span_kernel(
    len_ref, me_ref, q_ref, cos_ref, sin_ref, nk_ref, nv_ref, sk_ref, sv_ref,
    q_out, m_out, acc_out, sent_out,
):
    first = pl.program_id(0) * QP
    lane = lax.broadcasted_iota(jnp.int32, (1, QP * SPAN), 1)
    code = jnp.full((1, QP * SPAN), -1, jnp.int32)
    for p in range(QP):
        live = len_ref[me_ref[0], first + p]
        code = jnp.where((lane >= p * SPAN) & (lane < p * SPAN + live), p, code)
    rotated = {}
    for g in range(GROUP):
        for s in range(STEPS):
            lanes = slice(g * HD, (g + 1) * HD)
            raw = q_ref[s, :, lanes].astype(jnp.float32)
            rotated[g, s] = turn(raw, cos_ref[s], sin_ref[s])
            q_out[s, :, lanes] = rotated[g, s].astype(jnp.bfloat16)
    fresh = [
        turn(nk_ref[s].astype(jnp.float32), cos_ref[s], sin_ref[s]).astype(jnp.bfloat16)
        for s in range(STEPS)
    ]
    pad = jnp.zeros((HD - STEPS * QP, HD), jnp.bfloat16)
    fresh_keys = jnp.concatenate(fresh + [pad], 0).T
    fresh_vals = with_ones(jnp.concatenate([nv_ref[s] for s in range(STEPS)] + [pad], 0))
    few = QP // 2
    rows = few * PIECES
    keys_of = few * SPAN
    row = lax.broadcasted_iota(jnp.int32, (rows, 1), 0)
    piece = row >> 3
    step = piece - 3 * ((piece * 22) >> 6)
    fresh_lane = lax.broadcasted_iota(jnp.int32, (1, HD), 1)
    for part in range(2):
        low = part * few
        prob = (row & (few - 1)) + low
        q = jnp.concatenate(
            [rotated[g, s][low : low + few] for g in range(GROUP) for s in range(STEPS)], 0
        ).astype(jnp.bfloat16)
        span_keys = sk_ref[low : low + few].reshape(keys_of, HD).T
        span_vals = with_ones(sv_ref[low : low + few].reshape(keys_of, HD))
        s1 = jnp.where(
            code[:, part * keys_of : (part + 1) * keys_of] == prob, dot(q, span_keys), masked_score
        )
        ok = ((fresh_lane & (QP - 1)) == prob) & ((fresh_lane >> 4) <= step)
        s2 = jnp.where(ok, dot(q, fresh_keys), masked_score)
        top = jnp.maximum(s1.max(1, keepdims=True), s2.max(1, keepdims=True)) * SCALE2
        p1 = jnp.exp2(s1 * SCALE2 - top).astype(jnp.bfloat16)
        p2 = jnp.exp2(s2 * SCALE2 - top).astype(jnp.bfloat16)
        total = dot(p1, span_vals) + dot(p2, fresh_vals)
        wide = jnp.broadcast_to(top, (rows, HD))
        for k in range(PIECES):
            m_out[0, k * QP + low : k * QP + low + few, :] = wide[k * few : (k + 1) * few]
            acc_out[0, k * QP + low : k * QP + low + few, :] = total[k * few : (k + 1) * few]
    keys = sk_ref[...].astype(jnp.float32)
    kcos = cos_ref[STEPS][:, None, :]
    ksin = sin_ref[STEPS][:, None, :]
    sent_out[:, :, :HD] = turn(keys, kcos, ksin).astype(jnp.bfloat16)
    sent_out[:, :, HD:] = sv_ref[...]


def span_part(
    lengths, me, queries, cosine, sine, new_keys, new_values, span_keys, span_values
):
    three = lambda width: pl.BlockSpec((STEPS, QP, width), lambda i, *_: (0, i, 0))
    span = lambda width: pl.BlockSpec((QP, SPAN, width), lambda i, *_: (i, 0, 0))
    table = pl.BlockSpec((STEPS + 1, QP, HD), lambda i, *_: (0, i, 0))
    state = lambda width: pl.BlockSpec((1, TILE, width), lambda i, *_: (i, 0, 0))
    wide = GROUP * HD
    return pl.pallas_call(
        span_kernel,
        grid_spec=pltpu.PrefetchScalarGridSpec(
            num_scalar_prefetch=2,
            grid=(QBLOCKS,),
            in_specs=[
                three(wide), table, table, three(HD), three(HD), span(HD), span(HD),
            ],
            out_specs=[three(wide), state(HD), state(2 * HD), span(2 * HD)],
        ),
        out_shape=[
            jax.ShapeDtypeStruct((STEPS, PROBS, wide), jnp.bfloat16),
            jax.ShapeDtypeStruct((QBLOCKS, TILE, HD), jnp.float32),
            jax.ShapeDtypeStruct((QBLOCKS, TILE, 2 * HD), jnp.float32),
            jax.ShapeDtypeStruct((PROBS, SPAN, 2 * HD), jnp.bfloat16),
        ],
        compiler_params=params(),
        cost_estimate=LIGHT,
    )(lengths, me, queries, cosine, sine, new_keys, new_values, span_keys, span_values)


def pack_kernel(keys_ref, vals_ref, out):
    for c in range(0, P_DEV, HD):
        out[c : c + HD, :] = keys_ref[c : c + HD, :].T
    out[P_DEV:, :] = vals_ref[...]


def pack_block(keys, vals):
    return pl.pallas_call(
        pack_kernel,
        out_shape=jax.ShapeDtypeStruct((2 * P_DEV, HD), jnp.bfloat16),
        compiler_params=pltpu.CompilerParams(vmem_limit_bytes=VMEM),
        cost_estimate=LIGHT,
    )(keys, vals)


def attend(picks, valid, kv, qs, m_ref, acc_ref):
    rows = 128
    keys = []
    vals = []
    for k in picks:
        flat = jnp.concatenate([kv[k, c : c + HD, :] for c in range(0, P_DEV, HD)], 1)
        keys.append(jnp.concatenate([flat, flat], 0))
        vals.append(with_ones(kv[k, P_DEV:, :]))
    for r0 in range(0, TILE, rows):
        at = slice(r0, r0 + rows)
        query = qs[at, :]
        old = m_ref[at, :]
        scores = [jnp.dot(query, key, preferred_element_type=jnp.float32) for key in keys]
        top = old
        for value, ok in zip(scores, valid):
            best = value.max(1, keepdims=True)
            top = jnp.maximum(top, best if ok is None else jnp.where(ok, best, masked_score))
        factor = jnp.exp2(old - top)
        total = acc_ref[at, :] * jnp.concatenate([factor, factor], 1)
        for value, val, ok in zip(scores, vals, valid):
            base = top if ok is None else jnp.where(ok, top, -masked_score)
            weights = jnp.concatenate(
                [
                    jnp.exp2(value[:, c : c + HD] - base).astype(jnp.bfloat16)
                    for c in range(0, P_DEV, HD)
                ],
                1,
            )
            total = total + jnp.dot(weights, val, preferred_element_type=jnp.float32)
        m_ref[at, :] = top
        acc_ref[at, :] = total


def attend_active(places, pat_ref, me_ref, picked, kv, qs, m_ref, acc_ref):
    i = pl.program_id(0)
    me = me_ref[0]
    for k in range(len(places) + 4):
        picked[k] = 0
    count = jnp.int32(0)
    for k, (dz, dy, other) in enumerate(places):
        picked[count] = k
        owner = chip_of(me, dz, -dy) + ((me & 1) ^ other)
        count = count + jnp.where(pat_ref[i, owner] > 0, 1, 0)
    fours = (count + 1) // 4

    def four(t, carry):
        base = 4 * t
        attend(
            [picked[base + k] for k in range(4)],
            [None, None, None, base + 3 < count],
            kv, qs, m_ref, acc_ref,
        )
        return carry

    lax.fori_loop(0, fours, four, 0)

    @pl.when(4 * fours < count)
    def _():
        base = 4 * fours
        attend(
            [picked[base], picked[base + 1]], [None, base + 1 < count], kv, qs, m_ref, acc_ref
        )


def load_state(q_ref, m_in, acc_in, qs, m_ref, acc_ref):
    for g in range(GROUP):
        for s in range(STEPS):
            at = (g * STEPS + s) * QP
            scaled = q_ref[s, :, g * HD : (g + 1) * HD].astype(jnp.float32) * SCALE2
            high = scaled.astype(jnp.bfloat16)
            qs[at : at + QP, :HD] = high
            qs[at : at + QP, HD:] = (scaled - high.astype(jnp.float32)).astype(jnp.bfloat16)
    m_ref[...] = m_in[0]
    acc_ref[...] = acc_in[0]


def prompt_kernel(
    places, groups, stacks, pat_ref, me_ref, head_ref, q_ref, m_in, acc_in, *refs
):
    blocks, weight, refs = refs[:stacks], refs[stacks], refs[stacks + 1 :]
    outs, att = refs[: len(groups)], refs[len(groups)]
    qs, m_ref, acc_ref, kv, picked, w_s, o_s, sems, w_sems, o_sems = refs[len(groups) + 1 :]
    i = pl.program_id(0)
    sizes = [ref.shape[0] for ref in blocks]
    copies = [
        pltpu.make_async_copy(ref, kv.at[pl.ds(sum(sizes[:k]), sizes[k])], sems.at[k])
        for k, ref in enumerate(blocks)
    ]
    chunks = [(k, j, place) for k, group in enumerate(groups) for j, place in enumerate(group)]
    each = -(-len(chunks) // QBLOCKS)

    def weight_copy(n):
        return pltpu.make_async_copy(
            weight.at[:, chunk_at(head_ref, chunks[n][2])], w_s.at[n], w_sems.at[n]
        )

    def out_copy(n):
        k, j, _ = chunks[n]
        return pltpu.make_async_copy(o_s.at[n], outs[k].at[j], o_sems.at[n])

    @pl.when(i == 0)
    def _():
        for copy in copies:
            copy.start()

    load_state(q_ref, m_in, acc_in, qs, m_ref, acc_ref)

    @pl.when(i == 0)
    def _():
        for copy in copies:
            copy.wait()

    for step in range(QBLOCKS):

        @pl.when(i == step)
        def _(step=step):
            for n in range(step * each, min((step + 1) * each, len(chunks))):
                weight_copy(n).start()

    attend_active(places, pat_ref, me_ref, picked, kv, qs, m_ref, acc_ref)
    done = (acc_ref[:, :HD] / acc_ref[:, HD:]).astype(jnp.bfloat16)
    for g in range(GROUP):
        for s in range(STEPS):
            at = (g * STEPS + s) * QP
            row = pl.multiple_of(s * PROBS + i * QP, QP)
            att[pl.ds(row, QP), g * HD : (g + 1) * HD] = done[at : at + QP]

    @pl.when(i == QBLOCKS - 1)
    def _():
        for n in range(len(chunks)):
            weight_copy(n).wait()
            o_s[n] = dot(att[...], w_s[n]).astype(jnp.bfloat16)
            out_copy(n).start()
        for n in range(len(chunks)):
            out_copy(n).wait()


def prompt_part(pattern, me, head, places, groups, query, top, accum, stacks, weight):
    wide = GROUP * HD
    three = pl.BlockSpec((STEPS, QP, wide), lambda i, *_: (0, i, 0))
    state = lambda width: pl.BlockSpec((1, TILE, width), lambda i, *_: (i, 0, 0))
    anywhere = pl.BlockSpec(memory_space=pl.ANY)
    rows = STEPS * PROBS
    depth = weight.shape[0]
    chunks = sum(len(group) for group in groups)
    return pl.pallas_call(
        functools.partial(prompt_kernel, places, groups, len(stacks)),
        grid_spec=pltpu.PrefetchScalarGridSpec(
            num_scalar_prefetch=3,
            grid=(QBLOCKS,),
            in_specs=[three, state(HD), state(2 * HD)] + [anywhere] * (len(stacks) + 1),
            out_specs=[anywhere] * len(groups) + [pl.BlockSpec((rows, wide), lambda i, *_: (0, 0))],
            scratch_shapes=[
                pltpu.VMEM((TILE, 2 * HD), jnp.bfloat16),
                pltpu.VMEM((TILE, HD), jnp.float32),
                pltpu.VMEM((TILE, 2 * HD), jnp.float32),
                pltpu.VMEM((len(places), 2 * P_DEV, HD), jnp.bfloat16),
                pltpu.SMEM((len(places) + 4,), jnp.int32),
                pltpu.VMEM((chunks, depth, CHUNK), jnp.bfloat16),
                pltpu.VMEM((chunks, rows, CHUNK), jnp.bfloat16),
                pltpu.SemaphoreType.DMA((len(stacks),)),
                pltpu.SemaphoreType.DMA((chunks,)),
                pltpu.SemaphoreType.DMA((chunks,)),
            ],
        ),
        out_shape=[
            jax.ShapeDtypeStruct((len(group), rows, CHUNK), jnp.bfloat16) for group in groups
        ]
        + [jax.ShapeDtypeStruct((rows, wide), jnp.bfloat16)],
        compiler_params=params(),
        cost_estimate=LIGHT,
    )(pattern, me, head, query, top, accum, *stacks, weight)


def flip(r):
    return (0x36 >> (2 * r)) & 3


def column(head, base, far, r):
    return base + (((head // 4) ^ far) * 4) + ((head & 3) ^ flip(r))


def project_kernel(places, head_ref, a_ref, w_ref, out):
    out[0] = dot(a_ref[...], w_ref[...]).astype(jnp.bfloat16)


def project(attended, weight, head, places):
    rows, depth = attended.shape

    def chunk(i, head):
        found = jnp.int32(0)
        for k, place in enumerate(places):
            found = jnp.where(i == k, column(head[0], *place), found)
        return (0, found)

    return pl.pallas_call(
        functools.partial(project_kernel, places),
        grid_spec=pltpu.PrefetchScalarGridSpec(
            num_scalar_prefetch=1,
            grid=(len(places),),
            in_specs=[
                pl.BlockSpec((rows, depth), lambda i, head: (0, 0)),
                pl.BlockSpec((depth, CHUNK), chunk),
            ],
            out_specs=pl.BlockSpec((1, rows, CHUNK), lambda i, head: (i, 0, 0)),
        ),
        out_shape=jax.ShapeDtypeStruct((len(places), rows, CHUNK), jnp.bfloat16),
        compiler_params=params(PART),
        cost_estimate=LIGHT,
    )(head, attended, weight)


def chunk_at(head_ref, place):
    return pl.ds(pl.multiple_of(column(head_ref[0], *place) * CHUNK, CHUNK), CHUNK)


def row_starts(places, refs):
    starts = []
    for k, group in enumerate(places):
        starts.append(refs[k].shape[1] if k and group == places[k - 1] else 0)
    return starts


def assemble_kernel(places, head_ref, *refs):
    for ref, group, row in zip(refs[:-1], places, row_starts(places, refs)):
        for j, place in enumerate(group):
            refs[-1][row : row + ref.shape[1], chunk_at(head_ref, place)] = ref[j]


def assemble(head, places, sources):
    rows = STEPS * PROBS
    whole = lambda value: pl.BlockSpec(value.shape, lambda i, head: (0, 0, 0))
    return pl.pallas_call(
        functools.partial(assemble_kernel, places),
        grid_spec=pltpu.PrefetchScalarGridSpec(
            num_scalar_prefetch=1,
            grid=(1,),
            in_specs=[whole(value) for value in sources],
            out_specs=pl.BlockSpec((rows, 16 * CHUNK), lambda i, head: (0, 0)),
        ),
        out_shape=jax.ShapeDtypeStruct((rows, 16 * CHUNK), jnp.bfloat16),
        compiler_params=params(LITTLE),
        cost_estimate=LIGHT,
    )(head, *sources)


def complete_kernel(places, head_ref, earlier, *refs):
    sources, out, sems = refs[:-2], refs[-2], refs[-1]
    copies = []
    for ref, group, row in zip(sources, places, row_starts(places, sources)):
        for j, place in enumerate(group):
            goal = out.at[row : row + ref.shape[1], chunk_at(head_ref, place)]
            copies.append(pltpu.make_async_copy(ref.at[j], goal, sems.at[len(copies)]))
    for copy in copies:
        copy.start()
    for copy in copies:
        copy.wait()


def complete(head, places, earlier, sources):
    anywhere = pl.BlockSpec(memory_space=pl.ANY)
    return pl.pallas_call(
        functools.partial(complete_kernel, places),
        grid_spec=pltpu.PrefetchScalarGridSpec(
            num_scalar_prefetch=1,
            grid=(1,),
            in_specs=[anywhere]
            + [pl.BlockSpec(value.shape, lambda i, head: (0, 0, 0)) for value in sources],
            out_specs=anywhere,
            scratch_shapes=[pltpu.SemaphoreType.DMA((sum(len(g) for g in places),))],
        ),
        out_shape=jax.ShapeDtypeStruct(earlier.shape, earlier.dtype),
        input_output_aliases={1: 0},
        compiler_params=params(LITTLE),
        cost_estimate=LIGHT,
    )(head, earlier, *sources)


def join_kernel(first_ref, begin_ref, len_ref, source, keys_out, vals_out):
    problem = first_ref[0] + pl.program_id(0)
    total = BRANCHES * SPAN
    flat = source[:, 0].reshape(total, 2 * HD)
    lane = lax.broadcasted_iota(jnp.int32, (1, total), 1)
    target = jnp.full((1, total), -1, jnp.int32)
    for b in range(BRANCHES):
        live = (lane >= b * SPAN) & (lane < b * SPAN + len_ref[b, problem])
        begin = begin_ref[b, problem] - P_DEV * BRANCHES - b * SPAN
        target = jnp.where(live, lane + begin, target)
    rows = 256
    for r0 in range(0, total, rows):
        slot = lax.broadcasted_iota(jnp.int32, (rows, 1), 0) + r0
        pick = jnp.where(target == slot, 1.0, 0.0).astype(jnp.bfloat16)
        got = jnp.dot(pick, flat, preferred_element_type=jnp.float32).astype(jnp.bfloat16)
        keys_out[0, r0 : r0 + rows, :] = got[:, :HD]
        vals_out[0, r0 : r0 + rows, :] = got[:, HD:]


def join(first, begins, lengths, source):
    share = source.shape[1]
    total = BRANCHES * SPAN
    out = pl.BlockSpec((1, total, HD), lambda i, *_: (i, 0, 0))
    shape = jax.ShapeDtypeStruct((share, total, HD), jnp.bfloat16)
    return pl.pallas_call(
        join_kernel,
        grid_spec=pltpu.PrefetchScalarGridSpec(
            num_scalar_prefetch=3,
            grid=(share,),
            in_specs=[pl.BlockSpec((BRANCHES, 1, SPAN, 2 * HD), lambda i, *_: (0, i, 0, 0))],
            out_specs=[out, out],
        ),
        out_shape=[shape, shape],
        compiler_params=params(LITTLE),
        cost_estimate=LIGHT,
    )(first, begins, lengths, source)


def chip_of(branch, dz, dy):
    return ((branch // 8) ^ dz) * 8 + ((branch // 2 + dy) % 4) * 2


def move_chip(value, dz, dy):
    perm = [(b, chip_of(b, dz, dy) + b % 2) for b in range(BRANCHES)]
    return lax.ppermute(value, "branch", perm)


def swap_core(value):
    return lax.ppermute(value, "branch", [(b, b ^ 1) for b in range(BRANCHES)])


def move_x(value, flip):
    return lax.ppermute(value, "head", [(h, h ^ flip) for h in range(KVH)])


def move_roles(o, p, q):
    return move_x(p, 1), move_x(q, 3), move_x(o, 2)


def add(*values):
    total = values[0].astype(jnp.float32)
    for value in values[1:]:
        total = total + value.astype(jnp.float32)
    return total.astype(jnp.bfloat16)


def after(value, *others):
    return lax.optimization_barrier((value, others))[0]


def shards(
    queries, new_keys, new_values, prompt_keys, prompt_values, span_keys, span_values,
    span_lengths, join_offsets, pattern, out_weight,
):
    me = lax.axis_index("branch")
    one = me.reshape(1)
    head = lax.axis_index("head").reshape(1)
    prompt_len = P_DEV * BRANCHES
    share = PROBS // BRANCHES

    own = pack_block(prompt_keys, prompt_values)
    near_at = [(0, 0), (1, 0), (0, 1), (0, 3)]
    far_at = [(0, 2), (1, 1), (1, 3), (1, 2)]
    near = [own] + [move_chip(own, dz, dy) for dz, dy in near_at[1:]]
    far = [move_chip(own, 0, 2)] + [move_chip(near[1], 0, dy) for dy in (1, 3)]

    lengths = span_lengths.T
    offsets = join_offsets.T
    live = lax.dynamic_slice_in_dim(lengths, me, 1, 0)
    shift = lax.dynamic_slice_in_dim(offsets, me, 1, 0) - prompt_len
    steps = jnp.arange(STEPS, dtype=jnp.int32)[:, None]
    cosine, sine = tables(jnp.concatenate([prompt_len + live + steps, shift]))
    far.append(move_chip(after(far[0], cosine), 1, 0))
    query, top, accum, sent = span_part(
        lengths,
        one,
        jnp.transpose(queries[0], (1, 0, 2)),
        cosine,
        sine,
        jnp.transpose(new_keys[0], (1, 0, 2)),
        jnp.transpose(new_values[0], (1, 0, 2)),
        span_keys[0],
        span_values[0],
    )

    near, far = after((near, far), query)
    near_stack, far_stack = jnp.stack(near), jnp.stack(far)
    near_other, far_other = swap_core(near_stack), swap_core(far_stack)
    sent = after(sent, near_stack, far_stack).reshape(BRANCHES, share, SPAN, 2 * HD)
    gathered = lax.all_to_all(sent, "branch", 0, 0, tiled=True)
    places = [(dz, dy, c) for at in (near_at, far_at) for c in (0, 1) for dz, dy in at]
    stacks = [near_stack, near_other, far_stack, far_other]

    half = 8
    roles = range(4)
    both = [[(0, far, r) for far in (1, 0)] for r in roles]
    zhere = [(half, 0, r) for r in roles]
    zthere = [(half, 1, r) for r in roles]
    zsend, xo, xp, xq, attended = prompt_part(
        pattern[0], one, head, places, [zthere] + both[:3], query, top, accum, stacks, out_weight
    )
    got_z = move_x(zsend, 4)
    got_x = move_roles(xo, xp, xq)
    kept = project(attended, out_weight, head, zhere + both[3])
    got_z = after(got_z, got_x)
    rows = STEPS * PROBS // 2
    halves = [slice(k, k + rows) for k in (0, rows)]
    zpart = [[add(kept[r][h], got_z[r][h]) for r in roles] for h in halves]
    got_zx = [move_roles(*part[:3]) for part in zpart]
    got_x = after(got_x, zpart[1][3], gathered)
    xsum = add(kept[4:], *got_x)
    got_zx[1] = after(got_zx[1], xsum)
    zsum = [add(part[3], *got) for part, got in zip(zpart, got_zx)]

    pair = add(xsum, move_x(xsum, 4)[::-1])
    zback = [move_roles(part, part, part) for part in zsum]
    zback[1] = after(zback[1], pair)
    zfour = [jnp.stack([zo, zp, zq, part]) for (zp, zq, zo), part in zip(zback, zsum)]
    zother = [move_x(part, 4) for part in zfour]
    xp, xq, xo = move_roles(pair, pair, pair)
    joined_keys, joined_values = join(
        (me * share).reshape(1), offsets, lengths, after(gathered, zfour[1])
    )
    mixed = assemble(head, [both[3], zhere, zhere], after([pair] + zfour, joined_keys))
    mixed = complete(head, [zthere, zthere] + both[:3], mixed, zother + [xo, xp, xq])
    mixed = jnp.transpose(mixed.reshape(STEPS, PROBS, 16 * CHUNK), (1, 0, 2))[None]
    return mixed, joined_keys, joined_values


def solution(mesh):
    return jax.shard_map(
        shards,
        mesh=mesh,
        in_specs=(
            P("branch", None, None, "head"),
            P("branch", None, None, "head"),
            P("branch", None, None, "head"),
            P("branch", "head"),
            P("branch", "head"),
            P("branch", None, None, "head"),
            P("branch", None, None, "head"),
            P(),
            P(),
            P("branch", None, None),
            P("head", None),
        ),
        out_specs=(
            P("branch", None, None, None),
            P("branch", None, "head"),
            P("branch", None, "head"),
        ),
        check_vma=False,
    )
```

```python
import functools
import math

import jax
import jax.numpy as jnp
import numpy as np
from jax import lax
from jax.experimental import pallas as pl
from jax.experimental.pallas import tpu as pltpu
from jax.sharding import PartitionSpec as P

HEADS = 64
KVH = 8
HD = 128
GROUP = HEADS // KVH
STEPS = 3
SPAN = 64
BRANCHES = 16
QBLOCKS = 4
PROBS = 64
QP = PROBS // QBLOCKS
PIECES = STEPS * GROUP
TILE = PIECES * QP
P_DEV = 512
CHUNK = 512

rope_base = 500000.0
masked_score = -1e30
SCALE2 = math.log2(math.e) / math.sqrt(HD)
VMEM = 60 * 1024 * 1024
PART = 46 * 1024 * 1024
LITTLE = 24 * 1024 * 1024
LIGHT = pl.CostEstimate(flops=0, bytes_accessed=0, transcendentals=0)


def params(limit=VMEM):
    return pltpu.CompilerParams(dimension_semantics=("arbitrary",), vmem_limit_bytes=limit)


def tables(position):
    half = HD // 2
    exponent = np.arange(half) * (2.0 / HD)
    frequency = np.tile(np.exp(-math.log(rope_base) * exponent), 2).astype(np.float32)
    sign = np.repeat(np.float32([-1.0, 1.0]), half)
    angle = position.astype(jnp.float32)[..., None] * frequency
    return jnp.cos(angle), jnp.sin(angle) * sign


def turn(values, cosine, sine):
    return values * cosine + pltpu.roll(values, HD // 2, values.ndim - 1) * sine


def with_ones(values):
    return jnp.concatenate([values, jnp.ones_like(values)], 1)


def dot(a, b):
    return jnp.dot(a, b, preferred_element_type=jnp.float32)


def span_kernel(
    len_ref, me_ref, q_ref, cos_ref, sin_ref, nk_ref, nv_ref, sk_ref, sv_ref,
    q_out, m_out, acc_out, sent_out,
):
    first = pl.program_id(0) * QP
    lane = lax.broadcasted_iota(jnp.int32, (1, QP * SPAN), 1)
    code = jnp.full((1, QP * SPAN), -1, jnp.int32)
    for p in range(QP):
        live = len_ref[me_ref[0], first + p]
        code = jnp.where((lane >= p * SPAN) & (lane < p * SPAN + live), p, code)
    rotated = {}
    for g in range(GROUP):
        for s in range(STEPS):
            lanes = slice(g * HD, (g + 1) * HD)
            raw = q_ref[s, :, lanes].astype(jnp.float32)
            rotated[g, s] = turn(raw, cos_ref[s], sin_ref[s])
            q_out[s, :, lanes] = rotated[g, s].astype(jnp.bfloat16)
    fresh = [
        turn(nk_ref[s].astype(jnp.float32), cos_ref[s], sin_ref[s]).astype(jnp.bfloat16)
        for s in range(STEPS)
    ]
    pad = jnp.zeros((HD - STEPS * QP, HD), jnp.bfloat16)
    fresh_keys = jnp.concatenate(fresh + [pad], 0).T
    fresh_vals = with_ones(jnp.concatenate([nv_ref[s] for s in range(STEPS)] + [pad], 0))
    few = QP // 2
    rows = few * PIECES
    keys_of = few * SPAN
    row = lax.broadcasted_iota(jnp.int32, (rows, 1), 0)
    piece = row >> 3
    step = piece - 3 * ((piece * 22) >> 6)
    fresh_lane = lax.broadcasted_iota(jnp.int32, (1, HD), 1)
    for part in range(2):
        low = part * few
        prob = (row & (few - 1)) + low
        q = jnp.concatenate(
            [rotated[g, s][low : low + few] for g in range(GROUP) for s in range(STEPS)], 0
        ).astype(jnp.bfloat16)
        span_keys = sk_ref[low : low + few].reshape(keys_of, HD).T
        span_vals = with_ones(sv_ref[low : low + few].reshape(keys_of, HD))
        s1 = jnp.where(
            code[:, part * keys_of : (part + 1) * keys_of] == prob, dot(q, span_keys), masked_score
        )
        ok = ((fresh_lane & (QP - 1)) == prob) & ((fresh_lane >> 4) <= step)
        s2 = jnp.where(ok, dot(q, fresh_keys), masked_score)
        top = jnp.maximum(s1.max(1, keepdims=True), s2.max(1, keepdims=True)) * SCALE2
        p1 = jnp.exp2(s1 * SCALE2 - top).astype(jnp.bfloat16)
        p2 = jnp.exp2(s2 * SCALE2 - top).astype(jnp.bfloat16)
        total = dot(p1, span_vals) + dot(p2, fresh_vals)
        wide = jnp.broadcast_to(top, (rows, HD))
        for k in range(PIECES):
            m_out[0, k * QP + low : k * QP + low + few, :] = wide[k * few : (k + 1) * few]
            acc_out[0, k * QP + low : k * QP + low + few, :] = total[k * few : (k + 1) * few]
    keys = sk_ref[...].astype(jnp.float32)
    kcos = cos_ref[STEPS][:, None, :]
    ksin = sin_ref[STEPS][:, None, :]
    sent_out[:, :, :HD] = turn(keys, kcos, ksin).astype(jnp.bfloat16)
    sent_out[:, :, HD:] = sv_ref[...]


def span_part(
    lengths, me, queries, cosine, sine, new_keys, new_values, span_keys, span_values
):
    three = lambda width: pl.BlockSpec((STEPS, QP, width), lambda i, *_: (0, i, 0))
    span = lambda width: pl.BlockSpec((QP, SPAN, width), lambda i, *_: (i, 0, 0))
    table = pl.BlockSpec((STEPS + 1, QP, HD), lambda i, *_: (0, i, 0))
    state = lambda width: pl.BlockSpec((1, TILE, width), lambda i, *_: (i, 0, 0))
    wide = GROUP * HD
    return pl.pallas_call(
        span_kernel,
        grid_spec=pltpu.PrefetchScalarGridSpec(
            num_scalar_prefetch=2,
            grid=(QBLOCKS,),
            in_specs=[
                three(wide), table, table, three(HD), three(HD), span(HD), span(HD),
            ],
            out_specs=[three(wide), state(HD), state(2 * HD), span(2 * HD)],
        ),
        out_shape=[
            jax.ShapeDtypeStruct((STEPS, PROBS, wide), jnp.bfloat16),
            jax.ShapeDtypeStruct((QBLOCKS, TILE, HD), jnp.float32),
            jax.ShapeDtypeStruct((QBLOCKS, TILE, 2 * HD), jnp.float32),
            jax.ShapeDtypeStruct((PROBS, SPAN, 2 * HD), jnp.bfloat16),
        ],
        compiler_params=params(),
        cost_estimate=LIGHT,
    )(lengths, me, queries, cosine, sine, new_keys, new_values, span_keys, span_values)


def pack_kernel(keys_ref, vals_ref, out):
    for c in range(0, P_DEV, HD):
        out[c : c + HD, :] = keys_ref[c : c + HD, :].T
    out[P_DEV:, :] = vals_ref[...]


def pack_block(keys, vals):
    return pl.pallas_call(
        pack_kernel,
        out_shape=jax.ShapeDtypeStruct((2 * P_DEV, HD), jnp.bfloat16),
        compiler_params=pltpu.CompilerParams(vmem_limit_bytes=VMEM),
        cost_estimate=LIGHT,
    )(keys, vals)


def attend(picks, valid, kv, qs, m_ref, acc_ref):
    rows = 128
    keys = []
    vals = []
    for k in picks:
        flat = jnp.concatenate([kv[k, c : c + HD, :] for c in range(0, P_DEV, HD)], 1)
        keys.append(jnp.concatenate([flat, flat], 0))
        vals.append(with_ones(kv[k, P_DEV:, :]))
    for r0 in range(0, TILE, rows):
        at = slice(r0, r0 + rows)
        query = qs[at, :]
        old = m_ref[at, :]
        scores = [jnp.dot(query, key, preferred_element_type=jnp.float32) for key in keys]
        top = old
        for value, ok in zip(scores, valid):
            best = value.max(1, keepdims=True)
            top = jnp.maximum(top, best if ok is None else jnp.where(ok, best, masked_score))
        factor = jnp.exp2(old - top)
        total = acc_ref[at, :] * jnp.concatenate([factor, factor], 1)
        for value, val, ok in zip(scores, vals, valid):
            base = top if ok is None else jnp.where(ok, top, -masked_score)
            weights = jnp.concatenate(
                [
                    jnp.exp2(value[:, c : c + HD] - base).astype(jnp.bfloat16)
                    for c in range(0, P_DEV, HD)
                ],
                1,
            )
            total = total + jnp.dot(weights, val, preferred_element_type=jnp.float32)
        m_ref[at, :] = top
        acc_ref[at, :] = total


def attend_active(places, pat_ref, me_ref, picked, kv, qs, m_ref, acc_ref):
    i = pl.program_id(0)
    me = me_ref[0]
    for k in range(len(places) + 4):
        picked[k] = 0
    count = jnp.int32(0)
    for k, (dz, dy, other) in enumerate(places):
        picked[count] = k
        owner = chip_of(me, dz, -dy) + ((me & 1) ^ other)
        count = count + jnp.where(pat_ref[i, owner] > 0, 1, 0)
    fours = (count + 1) // 4

    def four(t, carry):
        base = 4 * t
        attend(
            [picked[base + k] for k in range(4)],
            [None, None, None, base + 3 < count],
            kv, qs, m_ref, acc_ref,
        )
        return carry

    lax.fori_loop(0, fours, four, 0)

    @pl.when(4 * fours < count)
    def _():
        base = 4 * fours
        attend(
            [picked[base], picked[base + 1]], [None, base + 1 < count], kv, qs, m_ref, acc_ref
        )


def load_state(q_ref, m_in, acc_in, qs, m_ref, acc_ref):
    for g in range(GROUP):
        for s in range(STEPS):
            at = (g * STEPS + s) * QP
            scaled = q_ref[s, :, g * HD : (g + 1) * HD].astype(jnp.float32) * SCALE2
            high = scaled.astype(jnp.bfloat16)
            qs[at : at + QP, :HD] = high
            qs[at : at + QP, HD:] = (scaled - high.astype(jnp.float32)).astype(jnp.bfloat16)
    m_ref[...] = m_in[0]
    acc_ref[...] = acc_in[0]


def prompt_kernel(
    places, groups, stacks, pat_ref, me_ref, head_ref, q_ref, m_in, acc_in, *refs
):
    blocks, weight, refs = refs[:stacks], refs[stacks], refs[stacks + 1 :]
    outs, att = refs[: len(groups)], refs[len(groups)]
    qs, m_ref, acc_ref, kv, picked, w_s, o_s, sems, w_sems, o_sems = refs[len(groups) + 1 :]
    i = pl.program_id(0)
    sizes = [ref.shape[0] for ref in blocks]
    copies = [
        pltpu.make_async_copy(ref, kv.at[pl.ds(sum(sizes[:k]), sizes[k])], sems.at[k])
        for k, ref in enumerate(blocks)
    ]
    chunks = [(k, j, place) for k, group in enumerate(groups) for j, place in enumerate(group)]
    each = -(-len(chunks) // QBLOCKS)

    def weight_copy(n):
        return pltpu.make_async_copy(
            weight.at[:, chunk_at(head_ref, chunks[n][2])], w_s.at[n], w_sems.at[n]
        )

    def out_copy(n):
        k, j, _ = chunks[n]
        return pltpu.make_async_copy(o_s.at[n], outs[k].at[j], o_sems.at[n])

    @pl.when(i == 0)
    def _():
        for copy in copies:
            copy.start()

    load_state(q_ref, m_in, acc_in, qs, m_ref, acc_ref)

    @pl.when(i == 0)
    def _():
        for copy in copies:
            copy.wait()

    for step in range(QBLOCKS):

        @pl.when(i == step)
        def _(step=step):
            for n in range(step * each, min((step + 1) * each, len(chunks))):
                weight_copy(n).start()

    attend_active(places, pat_ref, me_ref, picked, kv, qs, m_ref, acc_ref)
    done = (acc_ref[:, :HD] / acc_ref[:, HD:]).astype(jnp.bfloat16)
    for g in range(GROUP):
        for s in range(STEPS):
            at = (g * STEPS + s) * QP
            row = pl.multiple_of(s * PROBS + i * QP, QP)
            att[pl.ds(row, QP), g * HD : (g + 1) * HD] = done[at : at + QP]

    @pl.when(i == QBLOCKS - 1)
    def _():
        for n in range(len(chunks)):
            weight_copy(n).wait()
            o_s[n] = dot(att[...], w_s[n]).astype(jnp.bfloat16)
            out_copy(n).start()
        for n in range(len(chunks)):
            out_copy(n).wait()


def prompt_part(pattern, me, head, places, groups, query, top, accum, stacks, weight):
    wide = GROUP * HD
    three = pl.BlockSpec((STEPS, QP, wide), lambda i, *_: (0, i, 0))
    state = lambda width: pl.BlockSpec((1, TILE, width), lambda i, *_: (i, 0, 0))
    anywhere = pl.BlockSpec(memory_space=pl.ANY)
    rows = STEPS * PROBS
    depth = weight.shape[0]
    chunks = sum(len(group) for group in groups)
    return pl.pallas_call(
        functools.partial(prompt_kernel, places, groups, len(stacks)),
        grid_spec=pltpu.PrefetchScalarGridSpec(
            num_scalar_prefetch=3,
            grid=(QBLOCKS,),
            in_specs=[three, state(HD), state(2 * HD)] + [anywhere] * (len(stacks) + 1),
            out_specs=[anywhere] * len(groups) + [pl.BlockSpec((rows, wide), lambda i, *_: (0, 0))],
            scratch_shapes=[
                pltpu.VMEM((TILE, 2 * HD), jnp.bfloat16),
                pltpu.VMEM((TILE, HD), jnp.float32),
                pltpu.VMEM((TILE, 2 * HD), jnp.float32),
                pltpu.VMEM((len(places), 2 * P_DEV, HD), jnp.bfloat16),
                pltpu.SMEM((len(places) + 4,), jnp.int32),
                pltpu.VMEM((chunks, depth, CHUNK), jnp.bfloat16),
                pltpu.VMEM((chunks, rows, CHUNK), jnp.bfloat16),
                pltpu.SemaphoreType.DMA((len(stacks),)),
                pltpu.SemaphoreType.DMA((chunks,)),
                pltpu.SemaphoreType.DMA((chunks,)),
            ],
        ),
        out_shape=[
            jax.ShapeDtypeStruct((len(group), rows, CHUNK), jnp.bfloat16) for group in groups
        ]
        + [jax.ShapeDtypeStruct((rows, wide), jnp.bfloat16)],
        compiler_params=params(),
        cost_estimate=LIGHT,
    )(pattern, me, head, query, top, accum, *stacks, weight)


def flip(r):
    return (0x36 >> (2 * r)) & 3


def column(head, base, far, r):
    return base + (((head // 4) ^ far) * 4) + ((head & 3) ^ flip(r))


def project_kernel(places, head_ref, a_ref, w_ref, out):
    out[0] = dot(a_ref[...], w_ref[...]).astype(jnp.bfloat16)


def project(attended, weight, head, places):
    rows, depth = attended.shape

    def chunk(i, head):
        found = jnp.int32(0)
        for k, place in enumerate(places):
            found = jnp.where(i == k, column(head[0], *place), found)
        return (0, found)

    return pl.pallas_call(
        functools.partial(project_kernel, places),
        grid_spec=pltpu.PrefetchScalarGridSpec(
            num_scalar_prefetch=1,
            grid=(len(places),),
            in_specs=[
                pl.BlockSpec((rows, depth), lambda i, head: (0, 0)),
                pl.BlockSpec((depth, CHUNK), chunk),
            ],
            out_specs=pl.BlockSpec((1, rows, CHUNK), lambda i, head: (i, 0, 0)),
        ),
        out_shape=jax.ShapeDtypeStruct((len(places), rows, CHUNK), jnp.bfloat16),
        compiler_params=params(PART),
        cost_estimate=LIGHT,
    )(head, attended, weight)


def chunk_at(head_ref, place):
    return pl.ds(pl.multiple_of(column(head_ref[0], *place) * CHUNK, CHUNK), CHUNK)


def row_starts(places, refs):
    starts = []
    for k, group in enumerate(places):
        starts.append(refs[k].shape[1] if k and group == places[k - 1] else 0)
    return starts


def assemble_kernel(places, head_ref, *refs):
    for ref, group, row in zip(refs[:-1], places, row_starts(places, refs)):
        for j, place in enumerate(group):
            refs[-1][row : row + ref.shape[1], chunk_at(head_ref, place)] = ref[j]


def assemble(head, places, sources):
    rows = STEPS * PROBS
    whole = lambda value: pl.BlockSpec(value.shape, lambda i, head: (0, 0, 0))
    return pl.pallas_call(
        functools.partial(assemble_kernel, places),
        grid_spec=pltpu.PrefetchScalarGridSpec(
            num_scalar_prefetch=1,
            grid=(1,),
            in_specs=[whole(value) for value in sources],
            out_specs=pl.BlockSpec((rows, 16 * CHUNK), lambda i, head: (0, 0)),
        ),
        out_shape=jax.ShapeDtypeStruct((rows, 16 * CHUNK), jnp.bfloat16),
        compiler_params=params(LITTLE),
        cost_estimate=LIGHT,
    )(head, *sources)


def complete_kernel(places, head_ref, earlier, *refs):
    sources, out, sems = refs[:-2], refs[-2], refs[-1]
    copies = []
    for ref, group, row in zip(sources, places, row_starts(places, sources)):
        for j, place in enumerate(group):
            goal = out.at[row : row + ref.shape[1], chunk_at(head_ref, place)]
            copies.append(pltpu.make_async_copy(ref.at[j], goal, sems.at[len(copies)]))
    for copy in copies:
        copy.start()
    for copy in copies:
        copy.wait()


def complete(head, places, earlier, sources):
    anywhere = pl.BlockSpec(memory_space=pl.ANY)
    return pl.pallas_call(
        functools.partial(complete_kernel, places),
        grid_spec=pltpu.PrefetchScalarGridSpec(
            num_scalar_prefetch=1,
            grid=(1,),
            in_specs=[anywhere]
            + [pl.BlockSpec(value.shape, lambda i, head: (0, 0, 0)) for value in sources],
            out_specs=anywhere,
            scratch_shapes=[pltpu.SemaphoreType.DMA((sum(len(g) for g in places),))],
        ),
        out_shape=jax.ShapeDtypeStruct(earlier.shape, earlier.dtype),
        input_output_aliases={1: 0},
        compiler_params=params(LITTLE),
        cost_estimate=LIGHT,
    )(head, earlier, *sources)


def join_kernel(first_ref, begin_ref, len_ref, source, keys_out, vals_out):
    problem = first_ref[0] + pl.program_id(0)
    total = BRANCHES * SPAN
    flat = source[:, 0].reshape(total, 2 * HD)
    lane = lax.broadcasted_iota(jnp.int32, (1, total), 1)
    target = jnp.full((1, total), -1, jnp.int32)
    for b in range(BRANCHES):
        live = (lane >= b * SPAN) & (lane < b * SPAN + len_ref[b, problem])
        begin = begin_ref[b, problem] - P_DEV * BRANCHES - b * SPAN
        target = jnp.where(live, lane + begin, target)
    rows = 256
    for r0 in range(0, total, rows):
        slot = lax.broadcasted_iota(jnp.int32, (rows, 1), 0) + r0
        pick = jnp.where(target == slot, 1.0, 0.0).astype(jnp.bfloat16)
        got = jnp.dot(pick, flat, preferred_element_type=jnp.float32).astype(jnp.bfloat16)
        keys_out[0, r0 : r0 + rows, :] = got[:, :HD]
        vals_out[0, r0 : r0 + rows, :] = got[:, HD:]


def join(first, begins, lengths, source):
    share = source.shape[1]
    total = BRANCHES * SPAN
    out = pl.BlockSpec((1, total, HD), lambda i, *_: (i, 0, 0))
    shape = jax.ShapeDtypeStruct((share, total, HD), jnp.bfloat16)
    return pl.pallas_call(
        join_kernel,
        grid_spec=pltpu.PrefetchScalarGridSpec(
            num_scalar_prefetch=3,
            grid=(share,),
            in_specs=[pl.BlockSpec((BRANCHES, 1, SPAN, 2 * HD), lambda i, *_: (0, i, 0, 0))],
            out_specs=[out, out],
        ),
        out_shape=[shape, shape],
        compiler_params=params(LITTLE),
        cost_estimate=LIGHT,
    )(first, begins, lengths, source)


def chip_of(branch, dz, dy):
    return ((branch // 8) ^ dz) * 8 + ((branch // 2 + dy) % 4) * 2


def move_chip(value, dz, dy):
    perm = [(b, chip_of(b, dz, dy) + b % 2) for b in range(BRANCHES)]
    return lax.ppermute(value, "branch", perm)


def swap_core(value):
    return lax.ppermute(value, "branch", [(b, b ^ 1) for b in range(BRANCHES)])


def move_x(value, flip):
    return lax.ppermute(value, "head", [(h, h ^ flip) for h in range(KVH)])


def move_roles(o, p, q):
    return move_x(p, 1), move_x(q, 3), move_x(o, 2)


def add(*values):
    total = values[0].astype(jnp.float32)
    for value in values[1:]:
        total = total + value.astype(jnp.float32)
    return total.astype(jnp.bfloat16)


def after(value, *others):
    return lax.optimization_barrier((value, others))[0]


def shards(
    queries, new_keys, new_values, prompt_keys, prompt_values, span_keys, span_values,
    span_lengths, join_offsets, pattern, out_weight,
):
    me = lax.axis_index("branch")
    one = me.reshape(1)
    head = lax.axis_index("head").reshape(1)
    prompt_len = P_DEV * BRANCHES
    share = PROBS // BRANCHES

    own = pack_block(prompt_keys, prompt_values)
    near_at = [(0, 0), (1, 0), (0, 1), (0, 3)]
    far_at = [(0, 2), (1, 1), (1, 3), (1, 2)]
    near = [own] + [move_chip(own, dz, dy) for dz, dy in near_at[1:]]
    far = [move_chip(own, 0, 2)] + [move_chip(near[1], 0, dy) for dy in (1, 3)]

    lengths = span_lengths.T
    offsets = join_offsets.T
    live = lax.dynamic_slice_in_dim(lengths, me, 1, 0)
    shift = lax.dynamic_slice_in_dim(offsets, me, 1, 0) - prompt_len
    steps = jnp.arange(STEPS, dtype=jnp.int32)[:, None]
    cosine, sine = tables(jnp.concatenate([prompt_len + live + steps, shift]))
    far.append(move_chip(after(far[0], cosine), 1, 0))
    query, top, accum, sent = span_part(
        lengths,
        one,
        jnp.transpose(queries[0], (1, 0, 2)),
        cosine,
        sine,
        jnp.transpose(new_keys[0], (1, 0, 2)),
        jnp.transpose(new_values[0], (1, 0, 2)),
        span_keys[0],
        span_values[0],
    )

    near, far = after((near, far), query)
    near_stack, far_stack = jnp.stack(near), jnp.stack(far)
    near_other, far_other = swap_core(near_stack), swap_core(far_stack)
    sent = after(sent, near_stack, far_stack).reshape(BRANCHES, share, SPAN, 2 * HD)
    gathered = lax.all_to_all(sent, "branch", 0, 0, tiled=True)
    places = [(dz, dy, c) for at in (near_at, far_at) for c in (0, 1) for dz, dy in at]
    stacks = [near_stack, near_other, far_stack, far_other]

    half = 8
    roles = range(4)
    both = [[(0, far, r) for far in (1, 0)] for r in roles]
    zhere = [(half, 0, r) for r in roles]
    zthere = [(half, 1, r) for r in roles]
    zsend, xo, xp, xq, attended = prompt_part(
        pattern[0], one, head, places, [zthere] + both[:3], query, top, accum, stacks, out_weight
    )
    got_z = move_x(zsend, 4)
    got_x = move_roles(xo, xp, xq)
    kept = project(attended, out_weight, head, zhere + both[3])
    xsum = add(kept[4:], *after(got_x, gathered))
    got_z = after(got_z, xsum)
    rows = STEPS * PROBS // 2
    halves = [slice(k, k + rows) for k in (0, rows)]
    zpart = [[add(kept[r][h], got_z[r][h]) for r in roles] for h in halves]
    got_zx = [move_roles(*part[:3]) for part in zpart]

    pair = add(xsum, move_x(xsum, 4)[::-1])
    xo = move_x(pair, 2)
    zsum = [add(zpart[0][3], *got_zx[0])]
    zsum.append(add(zpart[1][3], *after(got_zx[1], pair, zsum[0])))
    zback = [move_roles(part, part, part) for part in zsum]
    zback[1] = after(zback[1], xo)
    zfour = [jnp.stack([zo, zp, zq, part]) for (zp, zq, zo), part in zip(zback, zsum)]
    pair = after(pair, zfour[0])
    xp, xq = move_x(pair, 1), move_x(pair, 3)
    zother = [move_x(part, 4) for part in zfour]
    joined_keys, joined_values = join(
        (me * share).reshape(1), offsets, lengths, after(gathered, zfour[1])
    )
    mixed = assemble(
        head, [both[3], both[0], zhere, zhere], after([pair, xo] + zfour, joined_keys)
    )
    mixed = complete(head, [zthere, zthere] + both[1:3], mixed, zother + [xp, xq])
    mixed = jnp.transpose(mixed.reshape(STEPS, PROBS, 16 * CHUNK), (1, 0, 2))[None]
    return mixed, joined_keys, joined_values


def solution(mesh):
    return jax.shard_map(
        shards,
        mesh=mesh,
        in_specs=(
            P("branch", None, None, "head"),
            P("branch", None, None, "head"),
            P("branch", None, None, "head"),
            P("branch", "head"),
            P("branch", "head"),
            P("branch", None, None, "head"),
            P("branch", None, None, "head"),
            P(),
            P(),
            P("branch", None, None),
            P("head", None),
        ),
        out_specs=(
            P("branch", None, None, None),
            P("branch", None, "head"),
            P("branch", None, "head"),
        ),
        check_vma=False,
    )
```

```python
import functools
import math

import jax
import jax.numpy as jnp
import numpy as np
from jax import lax
from jax.experimental import pallas as pl
from jax.experimental.pallas import tpu as pltpu
from jax.sharding import PartitionSpec as P

HEADS = 64
KVH = 8
HD = 128
GROUP = HEADS // KVH
STEPS = 3
SPAN = 64
BRANCHES = 16
QBLOCKS = 4
PROBS = 64
QP = PROBS // QBLOCKS
PIECES = STEPS * GROUP
TILE = PIECES * QP
P_DEV = 512
CHUNK = 512

rope_base = 500000.0
masked_score = -1e30
SCALE2 = math.log2(math.e) / math.sqrt(HD)
VMEM = 60 * 1024 * 1024
PART = 46 * 1024 * 1024
LITTLE = 24 * 1024 * 1024
LIGHT = pl.CostEstimate(flops=0, bytes_accessed=0, transcendentals=0)


def params(limit=VMEM):
    return pltpu.CompilerParams(dimension_semantics=("arbitrary",), vmem_limit_bytes=limit)


def tables(position):
    half = HD // 2
    exponent = np.arange(half) * (2.0 / HD)
    frequency = np.tile(np.exp(-math.log(rope_base) * exponent), 2).astype(np.float32)
    sign = np.repeat(np.float32([-1.0, 1.0]), half)
    angle = position.astype(jnp.float32)[..., None] * frequency
    return jnp.cos(angle), jnp.sin(angle) * sign


def turn(values, cosine, sine):
    return values * cosine + pltpu.roll(values, HD // 2, values.ndim - 1) * sine


def with_ones(values):
    return jnp.concatenate([values, jnp.ones_like(values)], 1)


def dot(a, b):
    return jnp.dot(a, b, preferred_element_type=jnp.float32)


def span_kernel(
    len_ref, me_ref, q_ref, cos_ref, sin_ref, nk_ref, nv_ref, sk_ref, sv_ref,
    q_out, m_out, acc_out, sent_out,
):
    first = pl.program_id(0) * QP
    lane = lax.broadcasted_iota(jnp.int32, (1, QP * SPAN), 1)
    code = jnp.full((1, QP * SPAN), -1, jnp.int32)
    for p in range(QP):
        live = len_ref[me_ref[0], first + p]
        code = jnp.where((lane >= p * SPAN) & (lane < p * SPAN + live), p, code)
    rotated = {}
    for g in range(GROUP):
        for s in range(STEPS):
            lanes = slice(g * HD, (g + 1) * HD)
            raw = q_ref[s, :, lanes].astype(jnp.float32)
            rotated[g, s] = turn(raw, cos_ref[s], sin_ref[s])
            q_out[s, :, lanes] = rotated[g, s].astype(jnp.bfloat16)
    fresh = [
        turn(nk_ref[s].astype(jnp.float32), cos_ref[s], sin_ref[s]).astype(jnp.bfloat16)
        for s in range(STEPS)
    ]
    pad = jnp.zeros((HD - STEPS * QP, HD), jnp.bfloat16)
    fresh_keys = jnp.concatenate(fresh + [pad], 0).T
    fresh_vals = with_ones(jnp.concatenate([nv_ref[s] for s in range(STEPS)] + [pad], 0))
    few = QP // 2
    rows = few * PIECES
    keys_of = few * SPAN
    row = lax.broadcasted_iota(jnp.int32, (rows, 1), 0)
    piece = row >> 3
    step = piece - 3 * ((piece * 22) >> 6)
    fresh_lane = lax.broadcasted_iota(jnp.int32, (1, HD), 1)
    for part in range(2):
        low = part * few
        prob = (row & (few - 1)) + low
        q = jnp.concatenate(
            [rotated[g, s][low : low + few] for g in range(GROUP) for s in range(STEPS)], 0
        ).astype(jnp.bfloat16)
        span_keys = sk_ref[low : low + few].reshape(keys_of, HD).T
        span_vals = with_ones(sv_ref[low : low + few].reshape(keys_of, HD))
        s1 = jnp.where(
            code[:, part * keys_of : (part + 1) * keys_of] == prob, dot(q, span_keys), masked_score
        )
        ok = ((fresh_lane & (QP - 1)) == prob) & ((fresh_lane >> 4) <= step)
        s2 = jnp.where(ok, dot(q, fresh_keys), masked_score)
        top = jnp.maximum(s1.max(1, keepdims=True), s2.max(1, keepdims=True)) * SCALE2
        p1 = jnp.exp2(s1 * SCALE2 - top).astype(jnp.bfloat16)
        p2 = jnp.exp2(s2 * SCALE2 - top).astype(jnp.bfloat16)
        total = dot(p1, span_vals) + dot(p2, fresh_vals)
        wide = jnp.broadcast_to(top, (rows, HD))
        for k in range(PIECES):
            m_out[0, k * QP + low : k * QP + low + few, :] = wide[k * few : (k + 1) * few]
            acc_out[0, k * QP + low : k * QP + low + few, :] = total[k * few : (k + 1) * few]
    keys = sk_ref[...].astype(jnp.float32)
    kcos = cos_ref[STEPS][:, None, :]
    ksin = sin_ref[STEPS][:, None, :]
    sent_out[:, :, :HD] = turn(keys, kcos, ksin).astype(jnp.bfloat16)
    sent_out[:, :, HD:] = sv_ref[...]


def span_part(
    lengths, me, queries, cosine, sine, new_keys, new_values, span_keys, span_values
):
    three = lambda width: pl.BlockSpec((STEPS, QP, width), lambda i, *_: (0, i, 0))
    span = lambda width: pl.BlockSpec((QP, SPAN, width), lambda i, *_: (i, 0, 0))
    table = pl.BlockSpec((STEPS + 1, QP, HD), lambda i, *_: (0, i, 0))
    state = lambda width: pl.BlockSpec((1, TILE, width), lambda i, *_: (i, 0, 0))
    wide = GROUP * HD
    return pl.pallas_call(
        span_kernel,
        grid_spec=pltpu.PrefetchScalarGridSpec(
            num_scalar_prefetch=2,
            grid=(QBLOCKS,),
            in_specs=[
                three(wide), table, table, three(HD), three(HD), span(HD), span(HD),
            ],
            out_specs=[three(wide), state(HD), state(2 * HD), span(2 * HD)],
        ),
        out_shape=[
            jax.ShapeDtypeStruct((STEPS, PROBS, wide), jnp.bfloat16),
            jax.ShapeDtypeStruct((QBLOCKS, TILE, HD), jnp.float32),
            jax.ShapeDtypeStruct((QBLOCKS, TILE, 2 * HD), jnp.float32),
            jax.ShapeDtypeStruct((PROBS, SPAN, 2 * HD), jnp.bfloat16),
        ],
        compiler_params=params(),
        cost_estimate=LIGHT,
    )(lengths, me, queries, cosine, sine, new_keys, new_values, span_keys, span_values)


def pack_kernel(keys_ref, vals_ref, out):
    for c in range(0, P_DEV, HD):
        out[c : c + HD, :] = keys_ref[c : c + HD, :].T
    out[P_DEV:, :] = vals_ref[...]


def pack_block(keys, vals):
    return pl.pallas_call(
        pack_kernel,
        out_shape=jax.ShapeDtypeStruct((2 * P_DEV, HD), jnp.bfloat16),
        compiler_params=pltpu.CompilerParams(vmem_limit_bytes=VMEM),
        cost_estimate=LIGHT,
    )(keys, vals)


def attend(picks, valid, kv, qs, m_ref, acc_ref):
    rows = 128
    keys = []
    vals = []
    for k in picks:
        flat = jnp.concatenate([kv[k, c : c + HD, :] for c in range(0, P_DEV, HD)], 1)
        keys.append(jnp.concatenate([flat, flat], 0))
        vals.append(with_ones(kv[k, P_DEV:, :]))
    for r0 in range(0, TILE, rows):
        at = slice(r0, r0 + rows)
        query = qs[at, :]
        old = m_ref[at, :]
        scores = [jnp.dot(query, key, preferred_element_type=jnp.float32) for key in keys]
        top = old
        for value, ok in zip(scores, valid):
            best = value.max(1, keepdims=True)
            top = jnp.maximum(top, best if ok is None else jnp.where(ok, best, masked_score))
        factor = jnp.exp2(old - top)
        total = acc_ref[at, :] * jnp.concatenate([factor, factor], 1)
        for value, val, ok in zip(scores, vals, valid):
            base = top if ok is None else jnp.where(ok, top, -masked_score)
            weights = jnp.concatenate(
                [
                    jnp.exp2(value[:, c : c + HD] - base).astype(jnp.bfloat16)
                    for c in range(0, P_DEV, HD)
                ],
                1,
            )
            total = total + jnp.dot(weights, val, preferred_element_type=jnp.float32)
        m_ref[at, :] = top
        acc_ref[at, :] = total


def attend_active(places, pat_ref, me_ref, picked, kv, qs, m_ref, acc_ref):
    i = pl.program_id(0)
    me = me_ref[0]
    for k in range(len(places) + 4):
        picked[k] = 0
    count = jnp.int32(0)
    for k, (dz, dy, other) in enumerate(places):
        picked[count] = k
        owner = chip_of(me, dz, -dy) + ((me & 1) ^ other)
        count = count + jnp.where(pat_ref[i, owner] > 0, 1, 0)
    fours = (count + 1) // 4

    def four(t, carry):
        base = 4 * t
        attend(
            [picked[base + k] for k in range(4)],
            [None, None, None, base + 3 < count],
            kv, qs, m_ref, acc_ref,
        )
        return carry

    lax.fori_loop(0, fours, four, 0)

    @pl.when(4 * fours < count)
    def _():
        base = 4 * fours
        attend(
            [picked[base], picked[base + 1]], [None, base + 1 < count], kv, qs, m_ref, acc_ref
        )


def load_state(q_ref, m_in, acc_in, qs, m_ref, acc_ref):
    for g in range(GROUP):
        for s in range(STEPS):
            at = (g * STEPS + s) * QP
            scaled = q_ref[s, :, g * HD : (g + 1) * HD].astype(jnp.float32) * SCALE2
            high = scaled.astype(jnp.bfloat16)
            qs[at : at + QP, :HD] = high
            qs[at : at + QP, HD:] = (scaled - high.astype(jnp.float32)).astype(jnp.bfloat16)
    m_ref[...] = m_in[0]
    acc_ref[...] = acc_in[0]


def prompt_kernel(
    places, groups, stacks, pat_ref, me_ref, head_ref, q_ref, m_in, acc_in, *refs
):
    blocks, weight, refs = refs[:stacks], refs[stacks], refs[stacks + 1 :]
    outs, att = refs[: len(groups)], refs[len(groups)]
    qs, m_ref, acc_ref, kv, picked, w_s, o_s, sems, w_sems, o_sems = refs[len(groups) + 1 :]
    i = pl.program_id(0)
    sizes = [ref.shape[0] for ref in blocks]
    copies = [
        pltpu.make_async_copy(ref, kv.at[pl.ds(sum(sizes[:k]), sizes[k])], sems.at[k])
        for k, ref in enumerate(blocks)
    ]
    chunks = [(k, j, place) for k, group in enumerate(groups) for j, place in enumerate(group)]
    each = -(-len(chunks) // QBLOCKS)

    def weight_copy(n):
        return pltpu.make_async_copy(
            weight.at[:, chunk_at(head_ref, chunks[n][2])], w_s.at[n], w_sems.at[n]
        )

    def out_copy(n):
        k, j, _ = chunks[n]
        return pltpu.make_async_copy(o_s.at[n], outs[k].at[j], o_sems.at[n])

    @pl.when(i == 0)
    def _():
        for copy in copies:
            copy.start()

    load_state(q_ref, m_in, acc_in, qs, m_ref, acc_ref)

    @pl.when(i == 0)
    def _():
        for copy in copies:
            copy.wait()

    for step in range(QBLOCKS):

        @pl.when(i == step)
        def _(step=step):
            for n in range(step * each, min((step + 1) * each, len(chunks))):
                weight_copy(n).start()

    attend_active(places, pat_ref, me_ref, picked, kv, qs, m_ref, acc_ref)
    done = (acc_ref[:, :HD] / acc_ref[:, HD:]).astype(jnp.bfloat16)
    for g in range(GROUP):
        for s in range(STEPS):
            at = (g * STEPS + s) * QP
            row = pl.multiple_of(s * PROBS + i * QP, QP)
            att[pl.ds(row, QP), g * HD : (g + 1) * HD] = done[at : at + QP]

    @pl.when(i == QBLOCKS - 1)
    def _():
        for n in range(len(chunks)):
            weight_copy(n).wait()
            o_s[n] = dot(att[...], w_s[n]).astype(jnp.bfloat16)
            out_copy(n).start()
        for n in range(len(chunks)):
            out_copy(n).wait()


def prompt_part(pattern, me, head, places, groups, query, top, accum, stacks, weight):
    wide = GROUP * HD
    three = pl.BlockSpec((STEPS, QP, wide), lambda i, *_: (0, i, 0))
    state = lambda width: pl.BlockSpec((1, TILE, width), lambda i, *_: (i, 0, 0))
    anywhere = pl.BlockSpec(memory_space=pl.ANY)
    rows = STEPS * PROBS
    depth = weight.shape[0]
    chunks = sum(len(group) for group in groups)
    return pl.pallas_call(
        functools.partial(prompt_kernel, places, groups, len(stacks)),
        grid_spec=pltpu.PrefetchScalarGridSpec(
            num_scalar_prefetch=3,
            grid=(QBLOCKS,),
            in_specs=[three, state(HD), state(2 * HD)] + [anywhere] * (len(stacks) + 1),
            out_specs=[anywhere] * len(groups) + [pl.BlockSpec((rows, wide), lambda i, *_: (0, 0))],
            scratch_shapes=[
                pltpu.VMEM((TILE, 2 * HD), jnp.bfloat16),
                pltpu.VMEM((TILE, HD), jnp.float32),
                pltpu.VMEM((TILE, 2 * HD), jnp.float32),
                pltpu.VMEM((len(places), 2 * P_DEV, HD), jnp.bfloat16),
                pltpu.SMEM((len(places) + 4,), jnp.int32),
                pltpu.VMEM((chunks, depth, CHUNK), jnp.bfloat16),
                pltpu.VMEM((chunks, rows, CHUNK), jnp.bfloat16),
                pltpu.SemaphoreType.DMA((len(stacks),)),
                pltpu.SemaphoreType.DMA((chunks,)),
                pltpu.SemaphoreType.DMA((chunks,)),
            ],
        ),
        out_shape=[
            jax.ShapeDtypeStruct((len(group), rows, CHUNK), jnp.bfloat16) for group in groups
        ]
        + [jax.ShapeDtypeStruct((rows, wide), jnp.bfloat16)],
        compiler_params=params(),
        cost_estimate=LIGHT,
    )(pattern, me, head, query, top, accum, *stacks, weight)


def flip(r):
    return (0x36 >> (2 * r)) & 3


def column(head, base, far, r):
    return base + (((head // 4) ^ far) * 4) + ((head & 3) ^ flip(r))


def project_kernel(places, head_ref, a_ref, w_ref, out):
    out[0] = dot(a_ref[...], w_ref[...]).astype(jnp.bfloat16)


def project(attended, weight, head, places):
    rows, depth = attended.shape

    def chunk(i, head):
        found = jnp.int32(0)
        for k, place in enumerate(places):
            found = jnp.where(i == k, column(head[0], *place), found)
        return (0, found)

    return pl.pallas_call(
        functools.partial(project_kernel, places),
        grid_spec=pltpu.PrefetchScalarGridSpec(
            num_scalar_prefetch=1,
            grid=(len(places),),
            in_specs=[
                pl.BlockSpec((rows, depth), lambda i, head: (0, 0)),
                pl.BlockSpec((depth, CHUNK), chunk),
            ],
            out_specs=pl.BlockSpec((1, rows, CHUNK), lambda i, head: (i, 0, 0)),
        ),
        out_shape=jax.ShapeDtypeStruct((len(places), rows, CHUNK), jnp.bfloat16),
        compiler_params=params(PART),
        cost_estimate=LIGHT,
    )(head, attended, weight)


def chunk_at(head_ref, place):
    return pl.ds(pl.multiple_of(column(head_ref[0], *place) * CHUNK, CHUNK), CHUNK)


def row_starts(places, refs):
    starts = []
    for k, group in enumerate(places):
        starts.append(refs[k].shape[1] if k and group == places[k - 1] else 0)
    return starts


def assemble_kernel(places, head_ref, *refs):
    for ref, group, row in zip(refs[:-1], places, row_starts(places, refs)):
        for j, place in enumerate(group):
            refs[-1][row : row + ref.shape[1], chunk_at(head_ref, place)] = ref[j]


def assemble(head, places, sources):
    rows = STEPS * PROBS
    whole = lambda value: pl.BlockSpec(value.shape, lambda i, head: (0, 0, 0))
    return pl.pallas_call(
        functools.partial(assemble_kernel, places),
        grid_spec=pltpu.PrefetchScalarGridSpec(
            num_scalar_prefetch=1,
            grid=(1,),
            in_specs=[whole(value) for value in sources],
            out_specs=pl.BlockSpec((rows, 16 * CHUNK), lambda i, head: (0, 0)),
        ),
        out_shape=jax.ShapeDtypeStruct((rows, 16 * CHUNK), jnp.bfloat16),
        compiler_params=params(LITTLE),
        cost_estimate=LIGHT,
    )(head, *sources)


def complete_kernel(places, head_ref, earlier, *refs):
    sources, out, sems = refs[:-2], refs[-2], refs[-1]
    copies = []
    for ref, group, row in zip(sources, places, row_starts(places, sources)):
        for j, place in enumerate(group):
            goal = out.at[row : row + ref.shape[1], chunk_at(head_ref, place)]
            copies.append(pltpu.make_async_copy(ref.at[j], goal, sems.at[len(copies)]))
    for copy in copies:
        copy.start()
    for copy in copies:
        copy.wait()


def complete(head, places, earlier, sources):
    anywhere = pl.BlockSpec(memory_space=pl.ANY)
    return pl.pallas_call(
        functools.partial(complete_kernel, places),
        grid_spec=pltpu.PrefetchScalarGridSpec(
            num_scalar_prefetch=1,
            grid=(1,),
            in_specs=[anywhere]
            + [pl.BlockSpec(value.shape, lambda i, head: (0, 0, 0)) for value in sources],
            out_specs=anywhere,
            scratch_shapes=[pltpu.SemaphoreType.DMA((sum(len(g) for g in places),))],
        ),
        out_shape=jax.ShapeDtypeStruct(earlier.shape, earlier.dtype),
        input_output_aliases={1: 0},
        compiler_params=params(LITTLE),
        cost_estimate=LIGHT,
    )(head, earlier, *sources)


def join_kernel(first_ref, begin_ref, len_ref, source, keys_out, vals_out):
    problem = first_ref[0] + pl.program_id(0)
    total = BRANCHES * SPAN
    flat = source[:, 0].reshape(total, 2 * HD)
    lane = lax.broadcasted_iota(jnp.int32, (1, total), 1)
    target = jnp.full((1, total), -1, jnp.int32)
    for b in range(BRANCHES):
        live = (lane >= b * SPAN) & (lane < b * SPAN + len_ref[b, problem])
        begin = begin_ref[b, problem] - P_DEV * BRANCHES - b * SPAN
        target = jnp.where(live, lane + begin, target)
    rows = 256
    for r0 in range(0, total, rows):
        slot = lax.broadcasted_iota(jnp.int32, (rows, 1), 0) + r0
        pick = jnp.where(target == slot, 1.0, 0.0).astype(jnp.bfloat16)
        got = jnp.dot(pick, flat, preferred_element_type=jnp.float32).astype(jnp.bfloat16)
        keys_out[0, r0 : r0 + rows, :] = got[:, :HD]
        vals_out[0, r0 : r0 + rows, :] = got[:, HD:]


def join(first, begins, lengths, source):
    share = source.shape[1]
    total = BRANCHES * SPAN
    out = pl.BlockSpec((1, total, HD), lambda i, *_: (i, 0, 0))
    shape = jax.ShapeDtypeStruct((share, total, HD), jnp.bfloat16)
    return pl.pallas_call(
        join_kernel,
        grid_spec=pltpu.PrefetchScalarGridSpec(
            num_scalar_prefetch=3,
            grid=(share,),
            in_specs=[pl.BlockSpec((BRANCHES, 1, SPAN, 2 * HD), lambda i, *_: (0, i, 0, 0))],
            out_specs=[out, out],
        ),
        out_shape=[shape, shape],
        compiler_params=params(LITTLE),
        cost_estimate=LIGHT,
    )(first, begins, lengths, source)


def chip_of(branch, dz, dy):
    return ((branch // 8) ^ dz) * 8 + ((branch // 2 + dy) % 4) * 2


def move_chip(value, dz, dy):
    perm = [(b, chip_of(b, dz, dy) + b % 2) for b in range(BRANCHES)]
    return lax.ppermute(value, "branch", perm)


def swap_core(value):
    return lax.ppermute(value, "branch", [(b, b ^ 1) for b in range(BRANCHES)])


def move_x(value, flip):
    return lax.ppermute(value, "head", [(h, h ^ flip) for h in range(KVH)])


def move_roles(o, p, q):
    return move_x(p, 1), move_x(q, 3), move_x(o, 2)


def add(*values):
    total = values[0].astype(jnp.float32)
    for value in values[1:]:
        total = total + value.astype(jnp.float32)
    return total.astype(jnp.bfloat16)


def after(value, *others):
    return lax.optimization_barrier((value, others))[0]


def shards(
    queries, new_keys, new_values, prompt_keys, prompt_values, span_keys, span_values,
    span_lengths, join_offsets, pattern, out_weight,
):
    me = lax.axis_index("branch")
    one = me.reshape(1)
    head = lax.axis_index("head").reshape(1)
    prompt_len = P_DEV * BRANCHES
    share = PROBS // BRANCHES

    own = pack_block(prompt_keys, prompt_values)
    near_at = [(0, 0), (1, 0), (0, 1), (0, 3)]
    far_at = [(0, 2), (1, 1), (1, 3), (1, 2)]
    near = [own] + [move_chip(own, dz, dy) for dz, dy in near_at[1:]]
    far = [move_chip(own, 0, 2)] + [move_chip(near[1], 0, dy) for dy in (1, 3)]

    lengths = span_lengths.T
    offsets = join_offsets.T
    live = lax.dynamic_slice_in_dim(lengths, me, 1, 0)
    shift = lax.dynamic_slice_in_dim(offsets, me, 1, 0) - prompt_len
    steps = jnp.arange(STEPS, dtype=jnp.int32)[:, None]
    cosine, sine = tables(jnp.concatenate([prompt_len + live + steps, shift]))
    near = after(near, cosine)
    near_stack = jnp.stack(near)
    near_other = swap_core(near_stack)
    far.append(move_chip(after(far[0], cosine), 1, 0))
    query, top, accum, sent = span_part(
        lengths,
        one,
        after(jnp.transpose(queries[0], (1, 0, 2)), near_stack),
        cosine,
        sine,
        jnp.transpose(new_keys[0], (1, 0, 2)),
        jnp.transpose(new_values[0], (1, 0, 2)),
        span_keys[0],
        span_values[0],
    )

    far_stack = jnp.stack(after(far, query))
    far_other = swap_core(far_stack)
    sent = after(sent, far_stack).reshape(BRANCHES, share, SPAN, 2 * HD)
    gathered = lax.all_to_all(sent, "branch", 0, 0, tiled=True)
    places = [(dz, dy, c) for at in (near_at, far_at) for c in (0, 1) for dz, dy in at]
    stacks = [near_stack, near_other, far_stack, far_other]

    half = 8
    roles = range(4)
    both = [[(0, far, r) for far in (1, 0)] for r in roles]
    zhere = [(half, 0, r) for r in roles]
    zthere = [(half, 1, r) for r in roles]
    zsend, xo, xp, xq, attended = prompt_part(
        pattern[0], one, head, places, [zthere] + both[:3], query, top, accum, stacks, out_weight
    )
    got_z = move_x(zsend, 4)
    got_x = move_roles(xo, xp, xq)
    kept = project(attended, out_weight, head, zhere + both[3])
    got_z = after(got_z, got_x)
    rows = STEPS * PROBS // 2
    halves = [slice(k, k + rows) for k in (0, rows)]
    zpart = [[add(kept[r][h], got_z[r][h]) for r in roles] for h in halves]
    got_zx = [move_roles(*part[:3]) for part in zpart]
    got_x = after(got_x, zpart[1][3], gathered)
    xsum = add(kept[4:], *got_x)
    got_zx[1] = after(got_zx[1], xsum)
    zsum = [add(part[3], *got) for part, got in zip(zpart, got_zx)]

    pair = add(xsum, move_x(xsum, 4)[::-1])
    zback = [move_roles(part, part, part) for part in zsum]
    zback[1] = after(zback[1], pair)
    zfour = [jnp.stack([zo, zp, zq, part]) for (zp, zq, zo), part in zip(zback, zsum)]
    zother = [move_x(part, 4) for part in zfour]
    xp, xq, xo = move_roles(pair, pair, pair)
    joined_keys, joined_values = join(
        (me * share).reshape(1), offsets, lengths, after(gathered, zfour[1])
    )
    mixed = assemble(head, [both[3], zhere, zhere], after([pair] + zfour, joined_keys))
    mixed = complete(head, [zthere, zthere] + both[:3], mixed, zother + [xo, xp, xq])
    mixed = jnp.transpose(mixed.reshape(STEPS, PROBS, 16 * CHUNK), (1, 0, 2))[None]
    return mixed, joined_keys, joined_values


def solution(mesh):
    return jax.shard_map(
        shards,
        mesh=mesh,
        in_specs=(
            P("branch", None, None, "head"),
            P("branch", None, None, "head"),
            P("branch", None, None, "head"),
            P("branch", "head"),
            P("branch", "head"),
            P("branch", None, None, "head"),
            P("branch", None, None, "head"),
            P(),
            P(),
            P("branch", None, None),
            P("head", None),
        ),
        out_specs=(
            P("branch", None, None, None),
            P("branch", None, "head"),
            P("branch", None, "head"),
        ),
        check_vma=False,
    )
```

```python
import functools
import math

import jax
import jax.numpy as jnp
import numpy as np
from jax import lax
from jax.experimental import pallas as pl
from jax.experimental.pallas import tpu as pltpu
from jax.sharding import PartitionSpec as P

HEADS = 64
KVH = 8
HD = 128
GROUP = HEADS // KVH
STEPS = 3
SPAN = 64
BRANCHES = 16
QBLOCKS = 4
PROBS = 64
QP = PROBS // QBLOCKS
PIECES = STEPS * GROUP
TILE = PIECES * QP
P_DEV = 512
CHUNK = 512

rope_base = 500000.0
masked_score = -1e30
SCALE2 = math.log2(math.e) / math.sqrt(HD)
VMEM = 60 * 1024 * 1024
PART = 46 * 1024 * 1024
LITTLE = 24 * 1024 * 1024
LIGHT = pl.CostEstimate(flops=0, bytes_accessed=0, transcendentals=0)


def params(limit=VMEM):
    return pltpu.CompilerParams(dimension_semantics=("arbitrary",), vmem_limit_bytes=limit)


def tables(position):
    half = HD // 2
    exponent = np.arange(half) * (2.0 / HD)
    frequency = np.tile(np.exp(-math.log(rope_base) * exponent), 2).astype(np.float32)
    sign = np.repeat(np.float32([-1.0, 1.0]), half)
    angle = position.astype(jnp.float32)[..., None] * frequency
    return jnp.cos(angle), jnp.sin(angle) * sign


def turn(values, cosine, sine):
    return values * cosine + pltpu.roll(values, HD // 2, values.ndim - 1) * sine


def with_ones(values):
    return jnp.concatenate([values, jnp.ones_like(values)], 1)


def dot(a, b):
    return jnp.dot(a, b, preferred_element_type=jnp.float32)


def span_kernel(
    len_ref, me_ref, q_ref, cos_ref, sin_ref, nk_ref, nv_ref, sk_ref, sv_ref,
    q_out, m_out, acc_out, sent_out,
):
    first = pl.program_id(0) * QP
    lane = lax.broadcasted_iota(jnp.int32, (1, QP * SPAN), 1)
    code = jnp.full((1, QP * SPAN), -1, jnp.int32)
    for p in range(QP):
        live = len_ref[me_ref[0], first + p]
        code = jnp.where((lane >= p * SPAN) & (lane < p * SPAN + live), p, code)
    rotated = {}
    for g in range(GROUP):
        for s in range(STEPS):
            lanes = slice(g * HD, (g + 1) * HD)
            raw = q_ref[s, :, lanes].astype(jnp.float32)
            rotated[g, s] = turn(raw, cos_ref[s], sin_ref[s])
            q_out[s, :, lanes] = rotated[g, s].astype(jnp.bfloat16)
    fresh = [
        turn(nk_ref[s].astype(jnp.float32), cos_ref[s], sin_ref[s]).astype(jnp.bfloat16)
        for s in range(STEPS)
    ]
    pad = jnp.zeros((HD - STEPS * QP, HD), jnp.bfloat16)
    fresh_keys = jnp.concatenate(fresh + [pad], 0).T
    fresh_vals = with_ones(jnp.concatenate([nv_ref[s] for s in range(STEPS)] + [pad], 0))
    few = QP // 2
    rows = few * PIECES
    keys_of = few * SPAN
    row = lax.broadcasted_iota(jnp.int32, (rows, 1), 0)
    piece = row >> 3
    step = piece - 3 * ((piece * 22) >> 6)
    fresh_lane = lax.broadcasted_iota(jnp.int32, (1, HD), 1)
    for part in range(2):
        low = part * few
        prob = (row & (few - 1)) + low
        q = jnp.concatenate(
            [rotated[g, s][low : low + few] for g in range(GROUP) for s in range(STEPS)], 0
        ).astype(jnp.bfloat16)
        span_keys = sk_ref[low : low + few].reshape(keys_of, HD).T
        span_vals = with_ones(sv_ref[low : low + few].reshape(keys_of, HD))
        s1 = jnp.where(
            code[:, part * keys_of : (part + 1) * keys_of] == prob, dot(q, span_keys), masked_score
        )
        ok = ((fresh_lane & (QP - 1)) == prob) & ((fresh_lane >> 4) <= step)
        s2 = jnp.where(ok, dot(q, fresh_keys), masked_score)
        top = jnp.maximum(s1.max(1, keepdims=True), s2.max(1, keepdims=True)) * SCALE2
        p1 = jnp.exp2(s1 * SCALE2 - top).astype(jnp.bfloat16)
        p2 = jnp.exp2(s2 * SCALE2 - top).astype(jnp.bfloat16)
        total = dot(p1, span_vals) + dot(p2, fresh_vals)
        wide = jnp.broadcast_to(top, (rows, HD))
        for k in range(PIECES):
            m_out[0, k * QP + low : k * QP + low + few, :] = wide[k * few : (k + 1) * few]
            acc_out[0, k * QP + low : k * QP + low + few, :] = total[k * few : (k + 1) * few]
    keys = sk_ref[...].astype(jnp.float32)
    kcos = cos_ref[STEPS][:, None, :]
    ksin = sin_ref[STEPS][:, None, :]
    sent_out[:, :, :HD] = turn(keys, kcos, ksin).astype(jnp.bfloat16)
    sent_out[:, :, HD:] = sv_ref[...]


def span_part(
    lengths, me, queries, cosine, sine, new_keys, new_values, span_keys, span_values
):
    three = lambda width: pl.BlockSpec((STEPS, QP, width), lambda i, *_: (0, i, 0))
    span = lambda width: pl.BlockSpec((QP, SPAN, width), lambda i, *_: (i, 0, 0))
    table = pl.BlockSpec((STEPS + 1, QP, HD), lambda i, *_: (0, i, 0))
    state = lambda width: pl.BlockSpec((1, TILE, width), lambda i, *_: (i, 0, 0))
    wide = GROUP * HD
    return pl.pallas_call(
        span_kernel,
        grid_spec=pltpu.PrefetchScalarGridSpec(
            num_scalar_prefetch=2,
            grid=(QBLOCKS,),
            in_specs=[
                three(wide), table, table, three(HD), three(HD), span(HD), span(HD),
            ],
            out_specs=[three(wide), state(HD), state(2 * HD), span(2 * HD)],
        ),
        out_shape=[
            jax.ShapeDtypeStruct((STEPS, PROBS, wide), jnp.bfloat16),
            jax.ShapeDtypeStruct((QBLOCKS, TILE, HD), jnp.float32),
            jax.ShapeDtypeStruct((QBLOCKS, TILE, 2 * HD), jnp.float32),
            jax.ShapeDtypeStruct((PROBS, SPAN, 2 * HD), jnp.bfloat16),
        ],
        compiler_params=params(),
        cost_estimate=LIGHT,
    )(lengths, me, queries, cosine, sine, new_keys, new_values, span_keys, span_values)


def pack_kernel(keys_ref, vals_ref, out):
    for c in range(0, P_DEV, HD):
        out[c : c + HD, :] = keys_ref[c : c + HD, :].T
    out[P_DEV:, :] = vals_ref[...]


def pack_block(keys, vals):
    return pl.pallas_call(
        pack_kernel,
        out_shape=jax.ShapeDtypeStruct((2 * P_DEV, HD), jnp.bfloat16),
        compiler_params=pltpu.CompilerParams(vmem_limit_bytes=VMEM),
        cost_estimate=LIGHT,
    )(keys, vals)


def attend(picks, valid, kv, qs, m_ref, acc_ref):
    rows = 128
    keys = []
    vals = []
    for k in picks:
        flat = jnp.concatenate([kv[k, c : c + HD, :] for c in range(0, P_DEV, HD)], 1)
        keys.append(jnp.concatenate([flat, flat], 0))
        vals.append(with_ones(kv[k, P_DEV:, :]))
    for r0 in range(0, TILE, rows):
        at = slice(r0, r0 + rows)
        query = qs[at, :]
        old = m_ref[at, :]
        scores = [jnp.dot(query, key, preferred_element_type=jnp.float32) for key in keys]
        top = old
        for value, ok in zip(scores, valid):
            best = value.max(1, keepdims=True)
            top = jnp.maximum(top, best if ok is None else jnp.where(ok, best, masked_score))
        factor = jnp.exp2(old - top)
        total = acc_ref[at, :] * jnp.concatenate([factor, factor], 1)
        for value, val, ok in zip(scores, vals, valid):
            base = top if ok is None else jnp.where(ok, top, -masked_score)
            weights = jnp.concatenate(
                [
                    jnp.exp2(value[:, c : c + HD] - base).astype(jnp.bfloat16)
                    for c in range(0, P_DEV, HD)
                ],
                1,
            )
            total = total + jnp.dot(weights, val, preferred_element_type=jnp.float32)
        m_ref[at, :] = top
        acc_ref[at, :] = total


def attend_active(places, pat_ref, me_ref, picked, kv, qs, m_ref, acc_ref):
    i = pl.program_id(0)
    me = me_ref[0]
    for k in range(len(places) + 4):
        picked[k] = 0
    count = jnp.int32(0)
    for k, (dz, dy, other) in enumerate(places):
        picked[count] = k
        owner = chip_of(me, dz, -dy) + ((me & 1) ^ other)
        count = count + jnp.where(pat_ref[i, owner] > 0, 1, 0)
    fours = (count + 1) // 4

    def four(t, carry):
        base = 4 * t
        attend(
            [picked[base + k] for k in range(4)],
            [None, None, None, base + 3 < count],
            kv, qs, m_ref, acc_ref,
        )
        return carry

    lax.fori_loop(0, fours, four, 0)

    @pl.when(4 * fours < count)
    def _():
        base = 4 * fours
        attend(
            [picked[base], picked[base + 1]], [None, base + 1 < count], kv, qs, m_ref, acc_ref
        )


def load_state(q_ref, m_in, acc_in, qs, m_ref, acc_ref):
    for g in range(GROUP):
        for s in range(STEPS):
            at = (g * STEPS + s) * QP
            scaled = q_ref[s, :, g * HD : (g + 1) * HD].astype(jnp.float32) * SCALE2
            high = scaled.astype(jnp.bfloat16)
            qs[at : at + QP, :HD] = high
            qs[at : at + QP, HD:] = (scaled - high.astype(jnp.float32)).astype(jnp.bfloat16)
    m_ref[...] = m_in[0]
    acc_ref[...] = acc_in[0]


def prompt_kernel(
    places, groups, stacks, pat_ref, me_ref, head_ref, q_ref, m_in, acc_in, *refs
):
    blocks, weight, refs = refs[:stacks], refs[stacks], refs[stacks + 1 :]
    outs, att = refs[: len(groups)], refs[len(groups)]
    qs, m_ref, acc_ref, kv, picked, w_s, o_s, sems, w_sems, o_sems = refs[len(groups) + 1 :]
    i = pl.program_id(0)
    sizes = [ref.shape[0] for ref in blocks]
    copies = [
        pltpu.make_async_copy(ref, kv.at[pl.ds(sum(sizes[:k]), sizes[k])], sems.at[k])
        for k, ref in enumerate(blocks)
    ]
    chunks = [(k, j, place) for k, group in enumerate(groups) for j, place in enumerate(group)]
    each = -(-len(chunks) // QBLOCKS)

    def weight_copy(n):
        return pltpu.make_async_copy(
            weight.at[:, chunk_at(head_ref, chunks[n][2])], w_s.at[n], w_sems.at[n]
        )

    def out_copy(n):
        k, j, _ = chunks[n]
        return pltpu.make_async_copy(o_s.at[n], outs[k].at[j], o_sems.at[n])

    @pl.when(i == 0)
    def _():
        for copy in copies:
            copy.start()

    load_state(q_ref, m_in, acc_in, qs, m_ref, acc_ref)

    @pl.when(i == 0)
    def _():
        for copy in copies:
            copy.wait()

    for step in range(QBLOCKS):

        @pl.when(i == step)
        def _(step=step):
            for n in range(step * each, min((step + 1) * each, len(chunks))):
                weight_copy(n).start()

    attend_active(places, pat_ref, me_ref, picked, kv, qs, m_ref, acc_ref)
    done = (acc_ref[:, :HD] / acc_ref[:, HD:]).astype(jnp.bfloat16)
    for g in range(GROUP):
        for s in range(STEPS):
            at = (g * STEPS + s) * QP
            row = pl.multiple_of(s * PROBS + i * QP, QP)
            att[pl.ds(row, QP), g * HD : (g + 1) * HD] = done[at : at + QP]

    @pl.when(i == QBLOCKS - 1)
    def _():
        for n in range(len(chunks)):
            weight_copy(n).wait()
            o_s[n] = dot(att[...], w_s[n]).astype(jnp.bfloat16)
            out_copy(n).start()
        for n in range(len(chunks)):
            out_copy(n).wait()


def prompt_part(pattern, me, head, places, groups, query, top, accum, stacks, weight):
    wide = GROUP * HD
    three = pl.BlockSpec((STEPS, QP, wide), lambda i, *_: (0, i, 0))
    state = lambda width: pl.BlockSpec((1, TILE, width), lambda i, *_: (i, 0, 0))
    anywhere = pl.BlockSpec(memory_space=pl.ANY)
    rows = STEPS * PROBS
    depth = weight.shape[0]
    chunks = sum(len(group) for group in groups)
    return pl.pallas_call(
        functools.partial(prompt_kernel, places, groups, len(stacks)),
        grid_spec=pltpu.PrefetchScalarGridSpec(
            num_scalar_prefetch=3,
            grid=(QBLOCKS,),
            in_specs=[three, state(HD), state(2 * HD)] + [anywhere] * (len(stacks) + 1),
            out_specs=[anywhere] * len(groups) + [pl.BlockSpec((rows, wide), lambda i, *_: (0, 0))],
            scratch_shapes=[
                pltpu.VMEM((TILE, 2 * HD), jnp.bfloat16),
                pltpu.VMEM((TILE, HD), jnp.float32),
                pltpu.VMEM((TILE, 2 * HD), jnp.float32),
                pltpu.VMEM((len(places), 2 * P_DEV, HD), jnp.bfloat16),
                pltpu.SMEM((len(places) + 4,), jnp.int32),
                pltpu.VMEM((chunks, depth, CHUNK), jnp.bfloat16),
                pltpu.VMEM((chunks, rows, CHUNK), jnp.bfloat16),
                pltpu.SemaphoreType.DMA((len(stacks),)),
                pltpu.SemaphoreType.DMA((chunks,)),
                pltpu.SemaphoreType.DMA((chunks,)),
            ],
        ),
        out_shape=[
            jax.ShapeDtypeStruct((len(group), rows, CHUNK), jnp.bfloat16) for group in groups
        ]
        + [jax.ShapeDtypeStruct((rows, wide), jnp.bfloat16)],
        compiler_params=params(),
        cost_estimate=LIGHT,
    )(pattern, me, head, query, top, accum, *stacks, weight)


def flip(r):
    return (0x36 >> (2 * r)) & 3


def column(head, base, far, r):
    return base + (((head // 4) ^ far) * 4) + ((head & 3) ^ flip(r))


def project_kernel(places, head_ref, a_ref, w_ref, out):
    out[0] = dot(a_ref[...], w_ref[...]).astype(jnp.bfloat16)


def project(attended, weight, head, places):
    rows, depth = attended.shape

    def chunk(i, head):
        found = jnp.int32(0)
        for k, place in enumerate(places):
            found = jnp.where(i == k, column(head[0], *place), found)
        return (0, found)

    return pl.pallas_call(
        functools.partial(project_kernel, places),
        grid_spec=pltpu.PrefetchScalarGridSpec(
            num_scalar_prefetch=1,
            grid=(len(places),),
            in_specs=[
                pl.BlockSpec((rows, depth), lambda i, head: (0, 0)),
                pl.BlockSpec((depth, CHUNK), chunk),
            ],
            out_specs=pl.BlockSpec((1, rows, CHUNK), lambda i, head: (i, 0, 0)),
        ),
        out_shape=jax.ShapeDtypeStruct((len(places), rows, CHUNK), jnp.bfloat16),
        compiler_params=params(PART),
        cost_estimate=LIGHT,
    )(head, attended, weight)


def chunk_at(head_ref, place):
    return pl.ds(pl.multiple_of(column(head_ref[0], *place) * CHUNK, CHUNK), CHUNK)


def row_starts(places, refs):
    starts = []
    for k, group in enumerate(places):
        starts.append(refs[k].shape[1] if k and group == places[k - 1] else 0)
    return starts


def assemble_kernel(places, head_ref, *refs):
    for ref, group, row in zip(refs[:-1], places, row_starts(places, refs)):
        for j, place in enumerate(group):
            refs[-1][row : row + ref.shape[1], chunk_at(head_ref, place)] = ref[j]


def assemble(head, places, sources):
    rows = STEPS * PROBS
    whole = lambda value: pl.BlockSpec(value.shape, lambda i, head: (0, 0, 0))
    return pl.pallas_call(
        functools.partial(assemble_kernel, places),
        grid_spec=pltpu.PrefetchScalarGridSpec(
            num_scalar_prefetch=1,
            grid=(1,),
            in_specs=[whole(value) for value in sources],
            out_specs=pl.BlockSpec((rows, 16 * CHUNK), lambda i, head: (0, 0)),
        ),
        out_shape=jax.ShapeDtypeStruct((rows, 16 * CHUNK), jnp.bfloat16),
        compiler_params=params(LITTLE),
        cost_estimate=LIGHT,
    )(head, *sources)


def complete_kernel(places, head_ref, earlier, *refs):
    sources, out, sems = refs[:-2], refs[-2], refs[-1]
    copies = []
    for ref, group, row in zip(sources, places, row_starts(places, sources)):
        for j, place in enumerate(group):
            goal = out.at[row : row + ref.shape[1], chunk_at(head_ref, place)]
            copies.append(pltpu.make_async_copy(ref.at[j], goal, sems.at[len(copies)]))
    for copy in copies:
        copy.start()
    for copy in copies:
        copy.wait()


def complete(head, places, earlier, sources):
    anywhere = pl.BlockSpec(memory_space=pl.ANY)
    return pl.pallas_call(
        functools.partial(complete_kernel, places),
        grid_spec=pltpu.PrefetchScalarGridSpec(
            num_scalar_prefetch=1,
            grid=(1,),
            in_specs=[anywhere]
            + [pl.BlockSpec(value.shape, lambda i, head: (0, 0, 0)) for value in sources],
            out_specs=anywhere,
            scratch_shapes=[pltpu.SemaphoreType.DMA((sum(len(g) for g in places),))],
        ),
        out_shape=jax.ShapeDtypeStruct(earlier.shape, earlier.dtype),
        input_output_aliases={1: 0},
        compiler_params=params(LITTLE),
        cost_estimate=LIGHT,
    )(head, earlier, *sources)


def join_kernel(first_ref, begin_ref, len_ref, source, keys_out, vals_out):
    problem = first_ref[0] + pl.program_id(0)
    total = BRANCHES * SPAN
    flat = source[:, 0].reshape(total, 2 * HD)
    lane = lax.broadcasted_iota(jnp.int32, (1, total), 1)
    target = jnp.full((1, total), -1, jnp.int32)
    for b in range(BRANCHES):
        live = (lane >= b * SPAN) & (lane < b * SPAN + len_ref[b, problem])
        begin = begin_ref[b, problem] - P_DEV * BRANCHES - b * SPAN
        target = jnp.where(live, lane + begin, target)
    rows = 256
    for r0 in range(0, total, rows):
        slot = lax.broadcasted_iota(jnp.int32, (rows, 1), 0) + r0
        pick = jnp.where(target == slot, 1.0, 0.0).astype(jnp.bfloat16)
        got = jnp.dot(pick, flat, preferred_element_type=jnp.float32).astype(jnp.bfloat16)
        keys_out[0, r0 : r0 + rows, :] = got[:, :HD]
        vals_out[0, r0 : r0 + rows, :] = got[:, HD:]


def join(first, begins, lengths, source):
    share = source.shape[1]
    total = BRANCHES * SPAN
    out = pl.BlockSpec((1, total, HD), lambda i, *_: (i, 0, 0))
    shape = jax.ShapeDtypeStruct((share, total, HD), jnp.bfloat16)
    return pl.pallas_call(
        join_kernel,
        grid_spec=pltpu.PrefetchScalarGridSpec(
            num_scalar_prefetch=3,
            grid=(share,),
            in_specs=[pl.BlockSpec((BRANCHES, 1, SPAN, 2 * HD), lambda i, *_: (0, i, 0, 0))],
            out_specs=[out, out],
        ),
        out_shape=[shape, shape],
        compiler_params=params(LITTLE),
        cost_estimate=LIGHT,
    )(first, begins, lengths, source)


def chip_of(branch, dz, dy):
    return ((branch // 8) ^ dz) * 8 + ((branch // 2 + dy) % 4) * 2


def move_chip(value, dz, dy):
    perm = [(b, chip_of(b, dz, dy) + b % 2) for b in range(BRANCHES)]
    return lax.ppermute(value, "branch", perm)


def swap_core(value):
    return lax.ppermute(value, "branch", [(b, b ^ 1) for b in range(BRANCHES)])


def move_x(value, flip):
    return lax.ppermute(value, "head", [(h, h ^ flip) for h in range(KVH)])


def move_roles(o, p, q):
    return move_x(p, 1), move_x(q, 3), move_x(o, 2)


def add(*values):
    total = values[0].astype(jnp.float32)
    for value in values[1:]:
        total = total + value.astype(jnp.float32)
    return total.astype(jnp.bfloat16)


def after(value, *others):
    return lax.optimization_barrier((value, others))[0]


def shards(
    queries, new_keys, new_values, prompt_keys, prompt_values, span_keys, span_values,
    span_lengths, join_offsets, pattern, out_weight,
):
    me = lax.axis_index("branch")
    one = me.reshape(1)
    head = lax.axis_index("head").reshape(1)
    prompt_len = P_DEV * BRANCHES
    share = PROBS // BRANCHES

    own = pack_block(prompt_keys, prompt_values)
    near_at = [(0, 0), (1, 0), (0, 1), (0, 3)]
    far_at = [(0, 2), (1, 1), (1, 3), (1, 2)]
    near = [own] + [move_chip(own, dz, dy) for dz, dy in near_at[1:]]
    far = [move_chip(own, 0, 2)] + [move_chip(near[1], 0, dy) for dy in (1, 3)]

    lengths = span_lengths.T
    offsets = join_offsets.T
    live = lax.dynamic_slice_in_dim(lengths, me, 1, 0)
    shift = lax.dynamic_slice_in_dim(offsets, me, 1, 0) - prompt_len
    steps = jnp.arange(STEPS, dtype=jnp.int32)[:, None]
    cosine, sine = tables(jnp.concatenate([prompt_len + live + steps, shift]))
    far.append(move_chip(after(far[0], cosine), 1, 0))
    query, top, accum, sent = span_part(
        lengths,
        one,
        jnp.transpose(queries[0], (1, 0, 2)),
        cosine,
        sine,
        jnp.transpose(new_keys[0], (1, 0, 2)),
        jnp.transpose(new_values[0], (1, 0, 2)),
        span_keys[0],
        span_values[0],
    )

    near, far = after((near, far), query)
    near_stack, far_stack = jnp.stack(near), jnp.stack(far)
    near_other, far_other = swap_core(near_stack), swap_core(far_stack)
    sent = after(sent, near_stack, far_stack).reshape(BRANCHES, share, SPAN, 2 * HD)
    gathered = lax.all_to_all(sent, "branch", 0, 0, tiled=True)
    places = [(dz, dy, c) for at in (near_at, far_at) for c in (0, 1) for dz, dy in at]
    stacks = [near_stack, near_other, far_stack, far_other]

    half = 8
    roles = range(4)
    both = [[(0, far, r) for far in (1, 0)] for r in roles]
    zhere = [(half, 0, r) for r in roles]
    zthere = [(half, 1, r) for r in roles]
    zsend, xo, xp, xq, attended = prompt_part(
        pattern[0], one, head, places, [zthere] + both[:3], query, top, accum, stacks, out_weight
    )
    got_z = move_x(zsend, 4)
    got_x = move_roles(xo, xp, xq)
    kept = project(attended, out_weight, head, zhere + both[3])
    got_z = after(got_z, got_x)
    rows = STEPS * PROBS // 2
    halves = [slice(k, k + rows) for k in (0, rows)]
    zpart = [[add(kept[r][h], got_z[r][h]) for r in roles] for h in halves]
    got_zx = [move_roles(*part[:3]) for part in zpart]
    got_x = after(got_x, zpart[1][3], gathered)
    xsum = add(kept[4:], *got_x)
    zsum = [add(zpart[0][3], *got_zx[0])]
    zsum.append(add(zpart[1][3], *after(got_zx[1], xsum, zsum[0])))

    pair = add(xsum, move_x(xsum, 4)[::-1])
    zback = [move_roles(part, part, part) for part in zsum]
    zback[1] = after(zback[1], pair)
    zfour = [jnp.stack([zo, zp, zq, part]) for (zp, zq, zo), part in zip(zback, zsum)]
    zother = [move_x(part, 4) for part in zfour]
    xp, xq, xo = move_roles(pair, pair, pair)
    joined_keys, joined_values = join(
        (me * share).reshape(1), offsets, lengths, after(gathered, zfour[1])
    )
    mixed = assemble(head, [both[3], zhere, zhere], after([pair] + zfour, joined_keys))
    mixed = complete(head, [zthere, zthere] + both[:3], mixed, zother + [xo, xp, xq])
    mixed = jnp.transpose(mixed.reshape(STEPS, PROBS, 16 * CHUNK), (1, 0, 2))[None]
    return mixed, joined_keys, joined_values


def solution(mesh):
    return jax.shard_map(
        shards,
        mesh=mesh,
        in_specs=(
            P("branch", None, None, "head"),
            P("branch", None, None, "head"),
            P("branch", None, None, "head"),
            P("branch", "head"),
            P("branch", "head"),
            P("branch", None, None, "head"),
            P("branch", None, None, "head"),
            P(),
            P(),
            P("branch", None, None),
            P("head", None),
        ),
        out_specs=(
            P("branch", None, None, None),
            P("branch", None, "head"),
            P("branch", None, "head"),
        ),
        check_vma=False,
    )
```

```python
import functools
import math

import jax
import jax.numpy as jnp
import numpy as np
from jax import lax
from jax.experimental import pallas as pl
from jax.experimental.pallas import tpu as pltpu
from jax.sharding import PartitionSpec as P

HEADS = 64
KVH = 8
HD = 128
GROUP = HEADS // KVH
STEPS = 3
SPAN = 64
BRANCHES = 16
QBLOCKS = 4
PROBS = 64
QP = PROBS // QBLOCKS
PIECES = STEPS * GROUP
TILE = PIECES * QP
P_DEV = 512
CHUNK = 512

rope_base = 500000.0
masked_score = -1e30
SCALE2 = math.log2(math.e) / math.sqrt(HD)
VMEM = 60 * 1024 * 1024
PART = 46 * 1024 * 1024
LITTLE = 24 * 1024 * 1024
LIGHT = pl.CostEstimate(flops=0, bytes_accessed=0, transcendentals=0)


def params(limit=VMEM):
    return pltpu.CompilerParams(dimension_semantics=("arbitrary",), vmem_limit_bytes=limit)


def tables(position):
    half = HD // 2
    exponent = np.arange(half) * (2.0 / HD)
    frequency = np.tile(np.exp(-math.log(rope_base) * exponent), 2).astype(np.float32)
    sign = np.repeat(np.float32([-1.0, 1.0]), half)
    angle = position.astype(jnp.float32)[..., None] * frequency
    return jnp.cos(angle), jnp.sin(angle) * sign


def turn(values, cosine, sine):
    return values * cosine + pltpu.roll(values, HD // 2, values.ndim - 1) * sine


def with_ones(values):
    return jnp.concatenate([values, jnp.ones_like(values)], 1)


def dot(a, b):
    return jnp.dot(a, b, preferred_element_type=jnp.float32)


def span_kernel(
    len_ref, me_ref, q_ref, cos_ref, sin_ref, nk_ref, nv_ref, sk_ref, sv_ref,
    q_out, m_out, acc_out, sent_out,
):
    first = pl.program_id(0) * QP
    lane = lax.broadcasted_iota(jnp.int32, (1, QP * SPAN), 1)
    code = jnp.full((1, QP * SPAN), -1, jnp.int32)
    for p in range(QP):
        live = len_ref[me_ref[0], first + p]
        code = jnp.where((lane >= p * SPAN) & (lane < p * SPAN + live), p, code)
    rotated = {}
    for g in range(GROUP):
        for s in range(STEPS):
            lanes = slice(g * HD, (g + 1) * HD)
            raw = q_ref[s, :, lanes].astype(jnp.float32)
            rotated[g, s] = turn(raw, cos_ref[s], sin_ref[s])
            q_out[s, :, lanes] = rotated[g, s].astype(jnp.bfloat16)
    fresh = [
        turn(nk_ref[s].astype(jnp.float32), cos_ref[s], sin_ref[s]).astype(jnp.bfloat16)
        for s in range(STEPS)
    ]
    pad = jnp.zeros((HD - STEPS * QP, HD), jnp.bfloat16)
    fresh_keys = jnp.concatenate(fresh + [pad], 0).T
    fresh_vals = with_ones(jnp.concatenate([nv_ref[s] for s in range(STEPS)] + [pad], 0))
    few = QP // 2
    rows = few * PIECES
    keys_of = few * SPAN
    row = lax.broadcasted_iota(jnp.int32, (rows, 1), 0)
    piece = row >> 3
    step = piece - 3 * ((piece * 22) >> 6)
    fresh_lane = lax.broadcasted_iota(jnp.int32, (1, HD), 1)
    for part in range(2):
        low = part * few
        prob = (row & (few - 1)) + low
        q = jnp.concatenate(
            [rotated[g, s][low : low + few] for g in range(GROUP) for s in range(STEPS)], 0
        ).astype(jnp.bfloat16)
        span_keys = sk_ref[low : low + few].reshape(keys_of, HD).T
        span_vals = with_ones(sv_ref[low : low + few].reshape(keys_of, HD))
        s1 = jnp.where(
            code[:, part * keys_of : (part + 1) * keys_of] == prob, dot(q, span_keys), masked_score
        )
        ok = ((fresh_lane & (QP - 1)) == prob) & ((fresh_lane >> 4) <= step)
        s2 = jnp.where(ok, dot(q, fresh_keys), masked_score)
        top = jnp.maximum(s1.max(1, keepdims=True), s2.max(1, keepdims=True)) * SCALE2
        p1 = jnp.exp2(s1 * SCALE2 - top).astype(jnp.bfloat16)
        p2 = jnp.exp2(s2 * SCALE2 - top).astype(jnp.bfloat16)
        total = dot(p1, span_vals) + dot(p2, fresh_vals)
        wide = jnp.broadcast_to(top, (rows, HD))
        for k in range(PIECES):
            m_out[0, k * QP + low : k * QP + low + few, :] = wide[k * few : (k + 1) * few]
            acc_out[0, k * QP + low : k * QP + low + few, :] = total[k * few : (k + 1) * few]
    keys = sk_ref[...].astype(jnp.float32)
    kcos = cos_ref[STEPS][:, None, :]
    ksin = sin_ref[STEPS][:, None, :]
    sent_out[:, :, :HD] = turn(keys, kcos, ksin).astype(jnp.bfloat16)
    sent_out[:, :, HD:] = sv_ref[...]


def span_part(
    lengths, me, queries, cosine, sine, new_keys, new_values, span_keys, span_values
):
    three = lambda width: pl.BlockSpec((STEPS, QP, width), lambda i, *_: (0, i, 0))
    span = lambda width: pl.BlockSpec((QP, SPAN, width), lambda i, *_: (i, 0, 0))
    table = pl.BlockSpec((STEPS + 1, QP, HD), lambda i, *_: (0, i, 0))
    state = lambda width: pl.BlockSpec((1, TILE, width), lambda i, *_: (i, 0, 0))
    wide = GROUP * HD
    return pl.pallas_call(
        span_kernel,
        grid_spec=pltpu.PrefetchScalarGridSpec(
            num_scalar_prefetch=2,
            grid=(QBLOCKS,),
            in_specs=[
                three(wide), table, table, three(HD), three(HD), span(HD), span(HD),
            ],
            out_specs=[three(wide), state(HD), state(2 * HD), span(2 * HD)],
        ),
        out_shape=[
            jax.ShapeDtypeStruct((STEPS, PROBS, wide), jnp.bfloat16),
            jax.ShapeDtypeStruct((QBLOCKS, TILE, HD), jnp.float32),
            jax.ShapeDtypeStruct((QBLOCKS, TILE, 2 * HD), jnp.float32),
            jax.ShapeDtypeStruct((PROBS, SPAN, 2 * HD), jnp.bfloat16),
        ],
        compiler_params=params(),
        cost_estimate=LIGHT,
    )(lengths, me, queries, cosine, sine, new_keys, new_values, span_keys, span_values)


def pack_kernel(keys_ref, vals_ref, out):
    for c in range(0, P_DEV, HD):
        out[c : c + HD, :] = keys_ref[c : c + HD, :].T
    out[P_DEV:, :] = vals_ref[...]


def pack_block(keys, vals):
    return pl.pallas_call(
        pack_kernel,
        out_shape=jax.ShapeDtypeStruct((2 * P_DEV, HD), jnp.bfloat16),
        compiler_params=pltpu.CompilerParams(vmem_limit_bytes=VMEM),
        cost_estimate=LIGHT,
    )(keys, vals)


def attend(picks, valid, kv, qs, m_ref, acc_ref):
    rows = 128
    keys = []
    vals = []
    for k in picks:
        flat = jnp.concatenate([kv[k, c : c + HD, :] for c in range(0, P_DEV, HD)], 1)
        keys.append(jnp.concatenate([flat, flat], 0))
        vals.append(with_ones(kv[k, P_DEV:, :]))
    for r0 in range(0, TILE, rows):
        at = slice(r0, r0 + rows)
        query = qs[at, :]
        old = m_ref[at, :]
        scores = [jnp.dot(query, key, preferred_element_type=jnp.float32) for key in keys]
        top = old
        for value, ok in zip(scores, valid):
            best = value.max(1, keepdims=True)
            top = jnp.maximum(top, best if ok is None else jnp.where(ok, best, masked_score))
        factor = jnp.exp2(old - top)
        total = acc_ref[at, :] * jnp.concatenate([factor, factor], 1)
        for value, val, ok in zip(scores, vals, valid):
            base = top if ok is None else jnp.where(ok, top, -masked_score)
            weights = jnp.concatenate(
                [
                    jnp.exp2(value[:, c : c + HD] - base).astype(jnp.bfloat16)
                    for c in range(0, P_DEV, HD)
                ],
                1,
            )
            total = total + jnp.dot(weights, val, preferred_element_type=jnp.float32)
        m_ref[at, :] = top
        acc_ref[at, :] = total


def attend_active(places, pat_ref, me_ref, picked, kv, qs, m_ref, acc_ref):
    i = pl.program_id(0)
    me = me_ref[0]
    for k in range(len(places) + 4):
        picked[k] = 0
    count = jnp.int32(0)
    for k, (dz, dy, other) in enumerate(places):
        picked[count] = k
        owner = chip_of(me, dz, -dy) + ((me & 1) ^ other)
        count = count + jnp.where(pat_ref[i, owner] > 0, 1, 0)
    fours = (count + 1) // 4

    def four(t, carry):
        base = 4 * t
        attend(
            [picked[base + k] for k in range(4)],
            [None, None, None, base + 3 < count],
            kv, qs, m_ref, acc_ref,
        )
        return carry

    lax.fori_loop(0, fours, four, 0)

    @pl.when(4 * fours < count)
    def _():
        base = 4 * fours
        attend(
            [picked[base], picked[base + 1]], [None, base + 1 < count], kv, qs, m_ref, acc_ref
        )


def load_state(q_ref, m_in, acc_in, qs, m_ref, acc_ref):
    for g in range(GROUP):
        for s in range(STEPS):
            at = (g * STEPS + s) * QP
            scaled = q_ref[s, :, g * HD : (g + 1) * HD].astype(jnp.float32) * SCALE2
            high = scaled.astype(jnp.bfloat16)
            qs[at : at + QP, :HD] = high
            qs[at : at + QP, HD:] = (scaled - high.astype(jnp.float32)).astype(jnp.bfloat16)
    m_ref[...] = m_in[0]
    acc_ref[...] = acc_in[0]


def prompt_kernel(
    places, groups, stacks, pat_ref, me_ref, head_ref, q_ref, m_in, acc_in, *refs
):
    blocks, weight, refs = refs[:stacks], refs[stacks], refs[stacks + 1 :]
    outs, att = refs[: len(groups)], refs[len(groups)]
    qs, m_ref, acc_ref, kv, picked, w_s, o_s, sems, w_sems, o_sems = refs[len(groups) + 1 :]
    i = pl.program_id(0)
    sizes = [ref.shape[0] for ref in blocks]
    copies = [
        pltpu.make_async_copy(ref, kv.at[pl.ds(sum(sizes[:k]), sizes[k])], sems.at[k])
        for k, ref in enumerate(blocks)
    ]
    chunks = [(k, j, place) for k, group in enumerate(groups) for j, place in enumerate(group)]
    each = -(-len(chunks) // QBLOCKS)

    def weight_copy(n):
        return pltpu.make_async_copy(
            weight.at[:, chunk_at(head_ref, chunks[n][2])], w_s.at[n], w_sems.at[n]
        )

    def out_copy(n):
        k, j, _ = chunks[n]
        return pltpu.make_async_copy(o_s.at[n], outs[k].at[j], o_sems.at[n])

    @pl.when(i == 0)
    def _():
        for copy in copies:
            copy.start()

    load_state(q_ref, m_in, acc_in, qs, m_ref, acc_ref)

    @pl.when(i == 0)
    def _():
        for copy in copies:
            copy.wait()

    for step in range(QBLOCKS):

        @pl.when(i == step)
        def _(step=step):
            for n in range(step * each, min((step + 1) * each, len(chunks))):
                weight_copy(n).start()

    attend_active(places, pat_ref, me_ref, picked, kv, qs, m_ref, acc_ref)
    done = (acc_ref[:, :HD] / acc_ref[:, HD:]).astype(jnp.bfloat16)
    for g in range(GROUP):
        for s in range(STEPS):
            at = (g * STEPS + s) * QP
            row = pl.multiple_of(s * PROBS + i * QP, QP)
            att[pl.ds(row, QP), g * HD : (g + 1) * HD] = done[at : at + QP]

    @pl.when(i == QBLOCKS - 1)
    def _():
        for n in range(len(chunks)):
            weight_copy(n).wait()
            o_s[n] = dot(att[...], w_s[n]).astype(jnp.bfloat16)
            out_copy(n).start()
        for n in range(len(chunks)):
            out_copy(n).wait()


def prompt_part(pattern, me, head, places, groups, query, top, accum, stacks, weight):
    wide = GROUP * HD
    three = pl.BlockSpec((STEPS, QP, wide), lambda i, *_: (0, i, 0))
    state = lambda width: pl.BlockSpec((1, TILE, width), lambda i, *_: (i, 0, 0))
    anywhere = pl.BlockSpec(memory_space=pl.ANY)
    rows = STEPS * PROBS
    depth = weight.shape[0]
    chunks = sum(len(group) for group in groups)
    return pl.pallas_call(
        functools.partial(prompt_kernel, places, groups, len(stacks)),
        grid_spec=pltpu.PrefetchScalarGridSpec(
            num_scalar_prefetch=3,
            grid=(QBLOCKS,),
            in_specs=[three, state(HD), state(2 * HD)] + [anywhere] * (len(stacks) + 1),
            out_specs=[anywhere] * len(groups) + [pl.BlockSpec((rows, wide), lambda i, *_: (0, 0))],
            scratch_shapes=[
                pltpu.VMEM((TILE, 2 * HD), jnp.bfloat16),
                pltpu.VMEM((TILE, HD), jnp.float32),
                pltpu.VMEM((TILE, 2 * HD), jnp.float32),
                pltpu.VMEM((len(places), 2 * P_DEV, HD), jnp.bfloat16),
                pltpu.SMEM((len(places) + 4,), jnp.int32),
                pltpu.VMEM((chunks, depth, CHUNK), jnp.bfloat16),
                pltpu.VMEM((chunks, rows, CHUNK), jnp.bfloat16),
                pltpu.SemaphoreType.DMA((len(stacks),)),
                pltpu.SemaphoreType.DMA((chunks,)),
                pltpu.SemaphoreType.DMA((chunks,)),
            ],
        ),
        out_shape=[
            jax.ShapeDtypeStruct((len(group), rows, CHUNK), jnp.bfloat16) for group in groups
        ]
        + [jax.ShapeDtypeStruct((rows, wide), jnp.bfloat16)],
        compiler_params=params(),
        cost_estimate=LIGHT,
    )(pattern, me, head, query, top, accum, *stacks, weight)


def flip(r):
    return (0x36 >> (2 * r)) & 3


def column(head, base, far, r):
    return base + (((head // 4) ^ far) * 4) + ((head & 3) ^ flip(r))


def project_kernel(places, head_ref, a_ref, w_ref, out):
    out[0] = dot(a_ref[...], w_ref[...]).astype(jnp.bfloat16)


def project(attended, weight, head, places):
    rows, depth = attended.shape

    def chunk(i, head):
        found = jnp.int32(0)
        for k, place in enumerate(places):
            found = jnp.where(i == k, column(head[0], *place), found)
        return (0, found)

    return pl.pallas_call(
        functools.partial(project_kernel, places),
        grid_spec=pltpu.PrefetchScalarGridSpec(
            num_scalar_prefetch=1,
            grid=(len(places),),
            in_specs=[
                pl.BlockSpec((rows, depth), lambda i, head: (0, 0)),
                pl.BlockSpec((depth, CHUNK), chunk),
            ],
            out_specs=pl.BlockSpec((1, rows, CHUNK), lambda i, head: (i, 0, 0)),
        ),
        out_shape=jax.ShapeDtypeStruct((len(places), rows, CHUNK), jnp.bfloat16),
        compiler_params=params(PART),
        cost_estimate=LIGHT,
    )(head, attended, weight)


def chunk_at(head_ref, place):
    return pl.ds(pl.multiple_of(column(head_ref[0], *place) * CHUNK, CHUNK), CHUNK)


def row_starts(places, refs):
    starts = []
    for k, group in enumerate(places):
        starts.append(refs[k].shape[1] if k and group == places[k - 1] else 0)
    return starts


def assemble_kernel(places, head_ref, *refs):
    for ref, group, row in zip(refs[:-1], places, row_starts(places, refs)):
        for j, place in enumerate(group):
            refs[-1][row : row + ref.shape[1], chunk_at(head_ref, place)] = ref[j]


def assemble(head, places, sources):
    rows = STEPS * PROBS
    whole = lambda value: pl.BlockSpec(value.shape, lambda i, head: (0, 0, 0))
    return pl.pallas_call(
        functools.partial(assemble_kernel, places),
        grid_spec=pltpu.PrefetchScalarGridSpec(
            num_scalar_prefetch=1,
            grid=(1,),
            in_specs=[whole(value) for value in sources],
            out_specs=pl.BlockSpec((rows, 16 * CHUNK), lambda i, head: (0, 0)),
        ),
        out_shape=jax.ShapeDtypeStruct((rows, 16 * CHUNK), jnp.bfloat16),
        compiler_params=params(LITTLE),
        cost_estimate=LIGHT,
    )(head, *sources)


def complete_kernel(places, head_ref, earlier, *refs):
    count = len(places)
    sources, out, held = refs[:count], refs[count], refs[count + 1 : -2]
    in_sems, out_sems = refs[-2:]
    fetches = [
        pltpu.make_async_copy(ref, buffer, in_sems.at[k])
        for k, (ref, buffer) in enumerate(zip(sources, held))
    ]
    for fetch in fetches:
        fetch.start()
    copies = []
    for fetch, ref, group, row in zip(fetches, held, places, row_starts(places, held)):
        fetch.wait()
        for j, place in enumerate(group):
            goal = out.at[row : row + ref.shape[1], chunk_at(head_ref, place)]
            copies.append(pltpu.make_async_copy(ref.at[j], goal, out_sems.at[len(copies)]))
            copies[-1].start()
    for copy in copies:
        copy.wait()


def complete(head, places, earlier, sources):
    anywhere = pl.BlockSpec(memory_space=pl.ANY)
    return pl.pallas_call(
        functools.partial(complete_kernel, places),
        grid_spec=pltpu.PrefetchScalarGridSpec(
            num_scalar_prefetch=1,
            grid=(1,),
            in_specs=[anywhere] * (1 + len(sources)),
            out_specs=anywhere,
            scratch_shapes=[pltpu.VMEM(value.shape, value.dtype) for value in sources]
            + [
                pltpu.SemaphoreType.DMA((len(sources),)),
                pltpu.SemaphoreType.DMA((sum(len(g) for g in places),)),
            ],
        ),
        out_shape=jax.ShapeDtypeStruct(earlier.shape, earlier.dtype),
        input_output_aliases={1: 0},
        compiler_params=params(LITTLE),
        cost_estimate=LIGHT,
    )(head, earlier, *sources)


def join_kernel(first_ref, begin_ref, len_ref, source, keys_out, vals_out):
    problem = first_ref[0] + pl.program_id(0)
    total = BRANCHES * SPAN
    flat = source[:, 0].reshape(total, 2 * HD)
    lane = lax.broadcasted_iota(jnp.int32, (1, total), 1)
    target = jnp.full((1, total), -1, jnp.int32)
    for b in range(BRANCHES):
        live = (lane >= b * SPAN) & (lane < b * SPAN + len_ref[b, problem])
        begin = begin_ref[b, problem] - P_DEV * BRANCHES - b * SPAN
        target = jnp.where(live, lane + begin, target)
    rows = 256
    for r0 in range(0, total, rows):
        slot = lax.broadcasted_iota(jnp.int32, (rows, 1), 0) + r0
        pick = jnp.where(target == slot, 1.0, 0.0).astype(jnp.bfloat16)
        got = jnp.dot(pick, flat, preferred_element_type=jnp.float32).astype(jnp.bfloat16)
        keys_out[0, r0 : r0 + rows, :] = got[:, :HD]
        vals_out[0, r0 : r0 + rows, :] = got[:, HD:]


def join(first, begins, lengths, source):
    share = source.shape[1]
    total = BRANCHES * SPAN
    out = pl.BlockSpec((1, total, HD), lambda i, *_: (i, 0, 0))
    shape = jax.ShapeDtypeStruct((share, total, HD), jnp.bfloat16)
    return pl.pallas_call(
        join_kernel,
        grid_spec=pltpu.PrefetchScalarGridSpec(
            num_scalar_prefetch=3,
            grid=(share,),
            in_specs=[pl.BlockSpec((BRANCHES, 1, SPAN, 2 * HD), lambda i, *_: (0, i, 0, 0))],
            out_specs=[out, out],
        ),
        out_shape=[shape, shape],
        compiler_params=params(LITTLE),
        cost_estimate=LIGHT,
    )(first, begins, lengths, source)


def chip_of(branch, dz, dy):
    return ((branch // 8) ^ dz) * 8 + ((branch // 2 + dy) % 4) * 2


def move_chip(value, dz, dy):
    perm = [(b, chip_of(b, dz, dy) + b % 2) for b in range(BRANCHES)]
    return lax.ppermute(value, "branch", perm)


def swap_core(value):
    return lax.ppermute(value, "branch", [(b, b ^ 1) for b in range(BRANCHES)])


def move_x(value, flip):
    return lax.ppermute(value, "head", [(h, h ^ flip) for h in range(KVH)])


def move_roles(o, p, q):
    return move_x(p, 1), move_x(q, 3), move_x(o, 2)


def add(*values):
    total = values[0].astype(jnp.float32)
    for value in values[1:]:
        total = total + value.astype(jnp.float32)
    return total.astype(jnp.bfloat16)


def after(value, *others):
    return lax.optimization_barrier((value, others))[0]


def shards(
    queries, new_keys, new_values, prompt_keys, prompt_values, span_keys, span_values,
    span_lengths, join_offsets, pattern, out_weight,
):
    me = lax.axis_index("branch")
    one = me.reshape(1)
    head = lax.axis_index("head").reshape(1)
    prompt_len = P_DEV * BRANCHES
    share = PROBS // BRANCHES

    own = pack_block(prompt_keys, prompt_values)
    near_at = [(0, 0), (1, 0), (0, 1), (0, 3)]
    far_at = [(0, 2), (1, 1), (1, 3), (1, 2)]
    near = [own] + [move_chip(own, dz, dy) for dz, dy in near_at[1:]]
    far = [move_chip(own, 0, 2)] + [move_chip(near[1], 0, dy) for dy in (1, 3)]

    lengths = span_lengths.T
    offsets = join_offsets.T
    live = lax.dynamic_slice_in_dim(lengths, me, 1, 0)
    shift = lax.dynamic_slice_in_dim(offsets, me, 1, 0) - prompt_len
    steps = jnp.arange(STEPS, dtype=jnp.int32)[:, None]
    cosine, sine = tables(jnp.concatenate([prompt_len + live + steps, shift]))
    far.append(move_chip(after(far[0], cosine), 1, 0))
    query, top, accum, sent = span_part(
        lengths,
        one,
        jnp.transpose(queries[0], (1, 0, 2)),
        cosine,
        sine,
        jnp.transpose(new_keys[0], (1, 0, 2)),
        jnp.transpose(new_values[0], (1, 0, 2)),
        span_keys[0],
        span_values[0],
    )

    near, far = after((near, far), query)
    near_stack, far_stack = jnp.stack(near), jnp.stack(far)
    near_other, far_other = swap_core(near_stack), swap_core(far_stack)
    sent = after(sent, near_stack, far_stack).reshape(BRANCHES, share, SPAN, 2 * HD)
    gathered = lax.all_to_all(sent, "branch", 0, 0, tiled=True)
    places = [(dz, dy, c) for at in (near_at, far_at) for c in (0, 1) for dz, dy in at]
    stacks = [near_stack, near_other, far_stack, far_other]

    half = 8
    roles = range(4)
    both = [[(0, far, r) for far in (1, 0)] for r in roles]
    zhere = [(half, 0, r) for r in roles]
    zthere = [(half, 1, r) for r in roles]
    zsend, xo, xp, xq, attended = prompt_part(
        pattern[0], one, head, places, [zthere] + both[:3], query, top, accum, stacks, out_weight
    )
    got_z = move_x(zsend, 4)
    got_x = move_roles(xo, xp, xq)
    kept = project(attended, out_weight, head, zhere + both[3])
    got_z = after(got_z, got_x)
    rows = STEPS * PROBS // 2
    halves = [slice(k, k + rows) for k in (0, rows)]
    zpart = [[add(kept[r][h], got_z[r][h]) for r in roles] for h in halves]
    got_zx = [move_roles(*part[:3]) for part in zpart]
    got_x = after(got_x, zpart[1][3], gathered)
    xsum = add(kept[4:], *got_x)
    zsum = [add(zpart[0][3], *got_zx[0])]
    zsum.append(add(zpart[1][3], *after(got_zx[1], xsum, zsum[0])))

    pair = add(xsum, move_x(xsum, 4)[::-1])
    zback = [move_roles(part, part, part) for part in zsum]
    zback[1] = after(zback[1], pair)
    zfour = [jnp.stack([zo, zp, zq, part]) for (zp, zq, zo), part in zip(zback, zsum)]
    zother = [move_x(part, 4) for part in zfour]
    xp, xq, xo = move_roles(pair, pair, pair)
    joined_keys, joined_values = join(
        (me * share).reshape(1), offsets, lengths, after(gathered, zfour[1])
    )
    mixed = assemble(head, [both[3], zhere, zhere], after([pair] + zfour, joined_keys))
    mixed = complete(head, [zthere, zthere] + both[:3], mixed, zother + [xo, xp, xq])
    mixed = jnp.transpose(mixed.reshape(STEPS, PROBS, 16 * CHUNK), (1, 0, 2))[None]
    return mixed, joined_keys, joined_values


def solution(mesh):
    return jax.shard_map(
        shards,
        mesh=mesh,
        in_specs=(
            P("branch", None, None, "head"),
            P("branch", None, None, "head"),
            P("branch", None, None, "head"),
            P("branch", "head"),
            P("branch", "head"),
            P("branch", None, None, "head"),
            P("branch", None, None, "head"),
            P(),
            P(),
            P("branch", None, None),
            P("head", None),
        ),
        out_specs=(
            P("branch", None, None, None),
            P("branch", None, "head"),
            P("branch", None, "head"),
        ),
        check_vma=False,
    )
```
